32 devices in a mesh: dp: 8 (over y, x, core), blk: 4 (over z).
Axes of the slice: x: 2, y: 2, z: 4, core: 2. Of those that a mesh axis runs over, the one named last changes fastest.
Arguments:
- patches: bfloat16 [8, 576, 768], P('dp', 'blk'), may hold values from -6 to 6
- keep: int32 [8, 576], P('dp', 'blk'), may hold values from 0 to 1, as said below
- coords: int32 [2, 8, 576], P(None, 'dp', 'blk'), may hold values from 0 to 23, as said below
- query_w: bfloat16 [2, 768, 768], replicated, may hold values from -0.21875 to 0.21875
- key_w: bfloat16 [2, 768, 768], replicated, may hold values from -0.21875 to 0.21875
- value_w: bfloat16 [2, 768, 768], replicated, may hold values from -0.21875 to 0.21875
- proj_w: bfloat16 [2, 768, 768], replicated, may hold values from -0.875 to 0.875
- up_w: bfloat16 [2, 768, 3072], replicated, may hold values from -0.21875 to 0.21875
- down_w: bfloat16 [2, 3072, 768], replicated, may hold values from -0.109375 to 0.109375
- norm1_gain: float32 [2, 768], replicated, may hold values from 0.25 to 1.75
- norm1_bias: float32 [2, 768], replicated, may hold values from -3 to 3
- norm2_gain: float32 [2, 768], replicated, may hold values from 0.25 to 1.75
- norm2_bias: float32 [2, 768], replicated, may hold values from -3 to 3
- freqs: float32 [2, 2, 12, 32], replicated, may hold values from -2.5 to 2.5
- cotangent: bfloat16 [8, 576, 768], P('dp', 'blk'), may hold values from -6 to 6
Outputs:
- output: bfloat16 [8, 576, 768], P('dp', 'blk')
- grad_patches: float32 [8, 576, 768], P('dp', 'blk')
- grad_query: float32 [2, 768, 768], P(None, 'dp', 'blk')
- grad_key: float32 [2, 768, 768], P(None, 'dp', 'blk')
- grad_value: float32 [2, 768, 768], P(None, 'dp', 'blk')
- grad_proj: float32 [2, 768, 768], P(None, 'dp', 'blk')
- grad_up: float32 [2, 768, 3072], P(None, 'dp', 'blk')
- grad_down: float32 [2, 3072, 768], P(None, 'dp', 'blk')
- grad_norm1_gain: float32 [2, 768], P(None, 'blk')
- grad_norm1_bias: float32 [2, 768], P(None, 'blk')
- grad_norm2_gain: float32 [2, 768], P(None, 'blk')
- grad_norm2_bias: float32 [2, 768], P(None, 'blk')
- grad_freqs: float32 [2, 2, 12, 32], P(None, None, 'blk')
The draws below stay inside these ranges and needn't reach their ends.
Inputs may be any that keep to these rules, and one draw needn't show every extreme that they name: `keep`: each image keeps at least one patch in every aligned run of 144 of its patches. For each image, the pairs (coords[0], coords[1]) run over the 576 cells of a 24 x 24 grid, each once.
All inputs are finite; a program needn't handle non-finite values.
Results may differ from the reference program's by a relative error of at most 0.028.
Values may be sent and summed in bfloat16 or wider, within the bound.
A program may use at most 576 MiB of HBM per device.

```python
import jax
import jax.numpy as jnp
from jax import lax

D = 768
HEADS = 12
HEAD = 64
FF = 3072
GRID = 24
LAYERS = 2
IMG_DEV = 1
P_SIZE = 576
PATCH_DEV = 144
IMAGES = 8


def draw_keep(key, part):
    key = jax.random.fold_in(key, 17)
    level_key, patch_key, anchor_key = jax.random.split(key, 3)
    runs = P_SIZE // PATCH_DEV
    keep_level = jax.random.randint(level_key, (IMAGES, 1), 0, 1000)
    keep_rate = 40 + keep_level * keep_level // 1000 * keep_level // 1000 * 96 // 100
    chances = jax.random.randint(patch_key, (IMAGES, P_SIZE), 0, 1000)
    kept_flags = (chances < keep_rate).reshape(IMAGES, runs, PATCH_DEV)
    offsets = jax.random.randint(anchor_key, (IMAGES, runs, 1), 0, PATCH_DEV)
    within = jnp.arange(PATCH_DEV)[None, None, :]
    kept_flags = jnp.logical_or(kept_flags, within == offsets)
    return kept_flags.reshape(IMAGES, P_SIZE).astype(jnp.int32)


def draw_coords(key, part):
    key = jax.random.fold_in(key, 29)
    ranking = jax.random.randint(key, (IMAGES, P_SIZE), 0, 1 << 20) * P_SIZE + jnp.arange(P_SIZE)[None, :]
    ordering = jnp.argsort(ranking, axis=-1, stable=True).astype(jnp.int32)
    return jnp.stack([ordering // GRID, ordering % GRID]).astype(jnp.int32)


def spiked(entries, key, source, target, parts, factor):
    owner, partner = [(jnp.arange(entries.shape[axis_at]) // (entries.shape[axis_at] // parts)).reshape([-1 if axis == axis_at else 1 for axis in range(entries.ndim)]) for axis_at in (source, target)]
    chosen = jax.random.permutation(key, parts)[partner]
    strong = (owner == chosen) | (owner == (partner + parts // 2) % parts)
    return jnp.where(strong, factor * entries, entries)


def shard_levels(key, shape, pieces, smallest, largest):
    level, own = 1.0, jax.random.fold_in(key, 6)
    for position, blocks in pieces:
        draws = jnp.exp(jax.random.uniform(jax.random.fold_in(own, position), (blocks,), jnp.float32, smallest / len(pieces), largest / len(pieces)))
        level = level * jnp.repeat(draws, shape[position] // blocks).reshape([-1 if axis == position else 1 for axis in range(len(shape))])
    return level


def bell_draw(stream_key, shape, scale, limit, cuts=(), held_as=jnp.bfloat16):
    entries = jax.random.normal(stream_key, shape, jnp.float32) * scale
    if len(cuts) > 0:
        entries = shard_levels(stream_key, shape, cuts, -0.22, 0.18) * entries
    return jnp.clip(entries, min=-limit, max=limit).astype(held_as)


def gaussian_with(rng, extent, scale, limit, cuts, heavy, kind=jnp.bfloat16):
    values = scale * jax.random.normal(rng, extent, jnp.float32)
    if cuts:
        values = values * shard_levels(rng, extent, cuts, -0.22, 0.18)
    return jnp.clip(spiked(values, jax.random.fold_in(rng, 3), *heavy), -limit, limit).astype(kind)


def setup_inputs(seed: int = 0) -> dict:
    streams_of = jax.random.split(jax.random.key(seed), 16)
    patches = bell_draw(streams_of[0], (IMAGES, P_SIZE, D), 1.0, 6.0, ((0, 8), (1, 4)))
    keep = draw_keep(jax.random.fold_in(streams_of[15], 71), 0)
    coords = draw_coords(jax.random.fold_in(streams_of[15], 71), 0)
    query_w = bell_draw(streams_of[3], (LAYERS, D, D), D ** -0.5, 0.21875)
    key_w = bell_draw(streams_of[4], (LAYERS, D, D), D ** -0.5, 0.21875)
    value_w = bell_draw(streams_of[5], (LAYERS, D, D), D ** -0.5, 0.21875)
    proj_w = bell_draw(streams_of[6], (LAYERS, D, D), (D // 16) ** -0.5, 0.875)
    up_w = bell_draw(streams_of[7], (LAYERS, D, FF), D ** -0.5, 0.21875)
    down_w = bell_draw(streams_of[8], (LAYERS, FF, D), FF ** -0.5, 0.109375)
    norm1_gain = jnp.clip(1.0 + 0.15 * jax.random.normal(streams_of[9], (LAYERS, D), jnp.float32), 0.25, 1.75)
    norm1_bias = bell_draw(streams_of[10], (LAYERS, D), 0.3, 3.0, (), jnp.float32)
    norm2_gain = jnp.clip(1.0 + 0.15 * jax.random.normal(streams_of[11], (LAYERS, D), jnp.float32), 0.25, 1.75)
    norm2_bias = bell_draw(streams_of[12], (LAYERS, D), 0.3, 3.0, (), jnp.float32)
    freqs = bell_draw(streams_of[13], (LAYERS, 2, HEADS, HEAD // 2), 0.4, 2.5, (), jnp.float32)
    cotangent = gaussian_with(streams_of[14], (IMAGES, P_SIZE, D), 1.0, 6.0, ((0, 8), (1, 4)), (0, 2, 8, 2.0))
    return {"patches": patches, "keep": keep, "coords": coords, "query_w": query_w, "key_w": key_w, "value_w": value_w, "proj_w": proj_w, "up_w": up_w, "down_w": down_w, "norm1_gain": norm1_gain, "norm1_bias": norm1_bias, "norm2_gain": norm2_gain, "norm2_bias": norm2_bias, "freqs": freqs, "cotangent": cotangent}


@jax.custom_vjp
def low(v):
    return lax.optimization_barrier(v.astype(jnp.bfloat16)).astype(jnp.float32)

@jax.custom_vjp
def low_back(v):
    return v

def low_keep(v):
    return (low(v), None)

def low_pass(kept, grad):
    return (grad,)

def back_keep(v):
    return (v, None)

def back_low(kept, grad):
    return (low(grad),)
low.defvjp(low_keep, low_pass)
low_back.defvjp(back_keep, back_low)
MASKED_SCORE = -1e+30
NORM_EPSILON = 1e-06
PRECISE = lax.Precision.HIGHEST

def layer_norm(values, weight_gain, weight_bias):
    centre = values - lax.optimization_barrier(jnp.mean(values, axis=-1, keepdims=True))
    spread = lax.optimization_barrier(jnp.mean(centre * centre, axis=-1, keepdims=True))
    return centre * lax.rsqrt(spread + NORM_EPSILON) * weight_gain + weight_bias

def rotate(tensor, cosine, sine_part):
    halfway = tensor.shape[-1] // 2
    former = tensor[..., :halfway]
    latter = tensor[..., halfway:]
    return jnp.concatenate([former * cosine - latter * sine_part, former * sine_part + latter * cosine], axis=-1)

def attend(queries, key_rows, value_rows, kept_mask):
    scaled = low_back(0.125 * jnp.einsum('gqhd,gkhd->ghqk', queries, key_rows, precision=PRECISE))
    allowed = kept_mask[:, None, None, :] > 0
    masked = jnp.where(allowed, scaled, MASKED_SCORE)
    highest = lax.optimization_barrier(jnp.max(masked, axis=-1, keepdims=True))
    weights = jnp.where(allowed, jnp.exp(masked - highest), 0.0)
    weights = weights / lax.optimization_barrier(jnp.sum(weights, axis=-1, keepdims=True))
    return jnp.einsum('ghqk,gkhd->gqhd', weights, value_rows, precision=PRECISE)

def project(values, weight):
    return jnp.einsum('ipd,de->ipe', values, weight, precision=PRECISE)

def exact_gelu(values):
    return jax.nn.gelu(values, approximate=False)

def forward(residual, query_w, key_w, value_w, proj_w, up_w, down_w, norm1_gain, norm1_bias, norm2_gain, norm2_bias, freqs, row_coord, column_coord, kept_mask):
    groups = IMAGES // IMG_DEV
    for layer_no in range(LAYERS):
        normed = low(layer_norm(residual, norm1_gain[layer_no], norm1_bias[layer_no]))
        phase_angle = row_coord[:, :, None, None] * freqs[layer_no, 0] + column_coord[:, :, None, None] * freqs[layer_no, 1]
        cosine = jnp.cos(phase_angle)
        sine_part = jnp.sin(phase_angle)
        queries = low_back(project(normed, query_w[layer_no])).reshape(IMAGES, P_SIZE, HEADS, HEAD)
        key_rows = low_back(project(normed, key_w[layer_no])).reshape(IMAGES, P_SIZE, HEADS, HEAD)
        value_rows = low(low_back(project(normed, value_w[layer_no]))).reshape(IMAGES, P_SIZE, HEADS, HEAD)
        queries = low(rotate(queries, cosine, sine_part))
        key_rows = low(rotate(key_rows, cosine, sine_part))

        def one_group(running, group_data):
            return (running, jax.checkpoint(attend)(group_data[0], group_data[1], group_data[2], group_data[3]))
        shaped = (queries.reshape(groups, IMG_DEV, P_SIZE, HEADS, HEAD), key_rows.reshape(groups, IMG_DEV, P_SIZE, HEADS, HEAD), value_rows.reshape(groups, IMG_DEV, P_SIZE, HEADS, HEAD), kept_mask.reshape(groups, IMG_DEV, P_SIZE))
        unused, mixed = lax.scan(one_group, None, shaped)
        attended = low(low_back(mixed.reshape(IMAGES, P_SIZE, HEADS * HEAD)))
        residual = residual + low_back(project(attended, proj_w[layer_no]))
        normed_two = low(layer_norm(residual, norm2_gain[layer_no], norm2_bias[layer_no]))
        hidden = low_back(project(normed_two, up_w[layer_no]))
        activated = low(exact_gelu(hidden))
        residual = residual + low_back(project(activated, down_w[layer_no]))
    return residual

def reference(patches, keep, coords, query_w, key_w, value_w, proj_w, up_w, down_w, norm1_gain, norm1_bias, norm2_gain, norm2_bias, freqs, cotangent):
    row_coord = coords[0].astype(jnp.float32)
    column_coord = coords[1].astype(jnp.float32)
    kept_mask = keep.astype(jnp.float32)

    def wrapped(residual, wq, wk, wv, wo, wu, wd, gain_one, bias_one, gain_two, bias_two, freq_table):
        return forward(residual, wq, wk, wv, wo, wu, wd, gain_one, bias_one, gain_two, bias_two, freq_table, row_coord, column_coord, kept_mask)
    primal = (patches.astype(jnp.float32), query_w.astype(jnp.float32), key_w.astype(jnp.float32), value_w.astype(jnp.float32), proj_w.astype(jnp.float32), up_w.astype(jnp.float32), down_w.astype(jnp.float32), norm1_gain.astype(jnp.float32), norm1_bias.astype(jnp.float32), norm2_gain.astype(jnp.float32), norm2_bias.astype(jnp.float32), freqs.astype(jnp.float32))
    result, pullback = jax.vjp(wrapped, *primal)
    grads = pullback(cotangent.astype(jnp.float32))
    return (result.astype(jnp.bfloat16), grads[0], grads[1], grads[2], grads[3], grads[4], grads[5], grads[6], grads[7], grads[8], grads[9], grads[10], grads[11])
```

```python
import jax
import jax.numpy as jnp
from jax import lax
from jax.experimental import pallas as pl
from jax.experimental.pallas import tpu as pltpu
from jax.sharding import PartitionSpec as P

MASKED_SCORE = -1e30
NORM_EPSILON = 1e-06
PRECISE = lax.Precision.HIGHEST


def passed_along(block, axis, distance):
    devices = range(lax.axis_size(axis))
    route = [((i - distance) % len(devices), i) for i in devices]
    return lax.ppermute(block, axis, route)


def layer_norm(values, weight_gain, weight_bias):
    centre = values - jnp.mean(values, axis=-1, keepdims=True)
    spread = jnp.mean(centre * centre, axis=-1, keepdims=True)
    return centre * lax.rsqrt(spread + NORM_EPSILON) * weight_gain + weight_bias


def exact_gelu(values):
    return jax.nn.gelu(values, approximate=False)


def rotate(tensor, cosine, sine_part):
    halfway = tensor.shape[-1] // 2
    former = tensor[..., :halfway]
    latter = tensor[..., halfway:]
    return jnp.concatenate(
        [former * cosine - latter * sine_part, former * sine_part + latter * cosine], axis=-1
    )


def unrotate(tensor, cosine, sine_part):
    halfway = tensor.shape[-1] // 2
    former = tensor[..., :halfway]
    latter = tensor[..., halfway:]
    return jnp.concatenate(
        [former * cosine + latter * sine_part, latter * cosine - former * sine_part], axis=-1
    )


def angle_grad(grad_rotated, rotated):
    halfway = rotated.shape[-1] // 2
    return (
        grad_rotated[..., halfway:] * rotated[..., :halfway]
        - grad_rotated[..., :halfway] * rotated[..., halfway:]
    )


def times_transposed(left_side, weight):
    return lax.dot_general(
        left_side, weight, (((1,), (1,)), ((), ())), preferred_element_type=jnp.float32
    )


def outer_sum(left_side, right_side):
    return lax.dot_general(
        left_side, right_side, (((0,), (0,)), ((), ())), preferred_element_type=jnp.float32
    )


def scores_of(queries, key_rows, kept_rows):
    scaled = 0.125 * jnp.einsum(
        "iqhd,ikhd->ihqk", queries, key_rows, preferred_element_type=jnp.float32
    )
    return jnp.where(kept_rows[:, None, None, :] > 0, scaled, MASKED_SCORE)


def merge_block(running, queries, key_rows, value_rows, kept_rows):
    highest, denominator, weighted = running
    masked = scores_of(queries, key_rows, kept_rows)
    new_highest = jnp.maximum(highest, jnp.max(masked, axis=-1))
    exponent = jnp.where(
        kept_rows[:, None, None, :] > 0, jnp.exp(masked - new_highest[..., None]), 0.0
    )
    factor = jnp.exp(highest - new_highest)
    denominator = factor * denominator + jnp.sum(exponent, axis=-1)
    weighted = factor[..., None] * weighted + jnp.einsum(
        "ihqk,ikhd->ihqd", exponent, value_rows.astype(jnp.float32), precision=PRECISE
    )
    return (new_highest, denominator, weighted)


def block_grads(queries, grad_attended, log_total, delta_rows, key_rows, value_rows, kept_rows):
    masked = scores_of(queries, key_rows, kept_rows)
    weights = jnp.where(
        kept_rows[:, None, None, :] > 0, jnp.exp(masked - log_total[..., None]), 0.0
    )
    grad_weights = jnp.einsum(
        "iqhd,ikhd->ihqk", grad_attended, value_rows, preferred_element_type=jnp.float32
    )
    grad_scores = (weights * (grad_weights - delta_rows[..., None])).astype(jnp.bfloat16)
    query_part = 0.125 * jnp.einsum(
        "ihqk,ikhd->iqhd", grad_scores, key_rows, preferred_element_type=jnp.float32
    )
    key_part = 0.125 * jnp.einsum(
        "ihqk,iqhd->ikhd", grad_scores, queries, preferred_element_type=jnp.float32
    )
    value_part = jnp.einsum(
        "ihqk,iqhd->ikhd", weights, grad_attended.astype(jnp.float32), precision=PRECISE
    )
    return (query_part, key_part, value_part)


MESH = pl.DeviceIdType.MESH
PLANS = {"down": (3, 384, True), "up": (2, 576, False), "proj": (3, 96, True), "qkv": (3, 288, False)}


class Place:
    def __init__(self):
        self.dp = lax.axis_index("dp")
        self.blk = lax.axis_index("blk")
        self.c = lax.rem(self.dp, 2)
        self.x = lax.rem(self.dp // 2, 2)
        self.y = lax.rem(self.dp // 4, 2)
        self.z0 = lax.rem(self.blk, 2)
        self.z1 = lax.rem(self.blk // 2, 2)

    def other(self, axis):
        step = {"c": 1, "x": 2, "y": 4}
        if axis in step:
            return (self.dp + step[axis] * (1 - 2 * getattr(self, axis)), self.blk)
        step = {"z0": 1, "z1": 2}
        return (self.dp, self.blk + step[axis] * (1 - 2 * getattr(self, axis)))


def greet(place, axes):
    barrier = pltpu.get_barrier_semaphore()
    for axis in axes:
        pl.semaphore_signal(barrier, inc=1, device_id=place.other(axis), device_id_type=MESH)
    pl.semaphore_wait(barrier, len(axes))


class Reduction:
    def __init__(self, place, plan, share, landing, sends, receives):
        self.place = place
        self.n, self.rows, x_first = plan
        self.share, self.landing = share, landing
        self.sends, self.receives = sends, receives
        self.first, self.second = ("x", "y") if x_first else ("y", "x")
        n = self.n
        self.half = 2 if n == 3 else 1
        a, b = getattr(place, self.first), getattr(place, self.second)
        self.offset = {}
        self.offset[1] = ((1 - a) * 4 * n, a * 4 * n, 4 * n, 8 * n)
        base = a * 4 * n
        self.offset[2] = (base + (1 - b) * 2 * n, base + b * 2 * n, 2 * n, 12 * n)
        base = base + b * 2 * n
        self.offset[3] = (base + (1 - place.z0) * n, base + place.z0 * n, n, 14 * n)
        base = base + place.z0 * n
        self.offset[4] = (base + 1 - place.z1, base + place.z1, self.half, 15 * n)

    def copy(self, stage):
        send, keep, count, land = self.offset[stage]
        axis = (None, self.first, self.second, "z0", "z1")[stage]
        return pltpu.make_async_remote_copy(
            src_ref=self.share.at[pl.ds(send, count)],
            dst_ref=self.landing.at[pl.ds(land, count)],
            send_sem=self.sends.at[stage],
            recv_sem=self.receives.at[stage],
            device_id=self.place.other(axis),
            device_id_type=MESH,
        )

    def start(self, stage):
        self.copy(stage).start()

    def add(self, stage):
        send, keep, count, land = self.offset[stage]
        self.copy(stage).wait_recv()

        def body(i, carry):
            self.share[keep + i] = (
                self.share[keep + i].astype(jnp.float32) + self.landing[land + i].astype(jnp.float32)
            ).astype(jnp.bfloat16)
            return carry

        lax.fori_loop(0, count, body, 0)

    def finish(self, write):
        send, keep, count, land = self.offset[4]
        self.copy(4).wait_recv()
        for i in range(count):
            write(i, self.share[keep + i].astype(jnp.float32) + self.landing[land + i].astype(jnp.float32))

    def drain(self):
        for stage in range(1, 5):
            self.copy(stage).wait_send()


def landing_tiles(plan):
    n = plan[0]
    return 15 * n + (2 if n == 3 else 1)


def write_narrow(place, out, layer_no, rows, first_row):
    def write(i, tile):
        tile = tile[first_row : first_row + rows]

        @pl.when(place.z1 == i)
        def _():
            out[layer_no, :, 0:128] = tile

        @pl.when(place.z1 == 1 - i)
        def _():
            @pl.when(place.z1 == 0)
            def _():
                out[layer_no, :, 128:192] = tile[:, 0:64]

            @pl.when(place.z1 == 1)
            def _():
                out[layer_no, :, 128:192] = tile[:, 64:128]

    return write


def reduce_kernel(layer_count, *refs):
    names = list(PLANS)
    count = layer_count * len(names)
    sources = refs[:count]
    small_in = refs[count]
    outs = refs[count + 1 : count + 8]
    scratch = refs[count + 8 :]
    shares, landings = scratch[:count], scratch[count : 2 * count]
    small, small_land, sends, receives, own_sems, small_send, small_recv = scratch[2 * count :]
    place = Place()
    greet(place, ("c", "x", "y", "z0", "z1"))
    work = []
    for index in range(count):
        plan = PLANS[names[index % len(names)]]
        red = Reduction(place, plan, shares[index], landings[index], sends.at[index], receives.at[index])
        work.append(red)
        n = plan[0]
        pltpu.make_async_copy(sources[index].at[place.c], shares[index], own_sems.at[index]).start()
        core_copy(red, sources[index]).start()
    small[0] = small_in[...]
    for index, red in enumerate(work):
        pltpu.make_async_copy(sources[index].at[place.c], shares[index], own_sems.at[index]).wait()
        core_copy(red, sources[index]).wait_recv()

        def body(i, carry, red=red):
            red.share[i] = (
                red.share[i].astype(jnp.float32) + red.landing[i].astype(jnp.float32)
            ).astype(jnp.bfloat16)
            return carry

        lax.fori_loop(0, 8 * red.n, body, 0)
        red.start(1)
    for stage in range(1, 4):
        for red in work:
            red.add(stage)
            red.start(stage + 1)
    for index, axis in enumerate(("c", "x", "y", "z0", "z1")):
        copy = pltpu.make_async_remote_copy(
            src_ref=small.at[index],
            dst_ref=small_land.at[index],
            send_sem=small_send.at[index],
            recv_sem=small_recv.at[index],
            device_id=place.other(axis),
            device_id_type=MESH,
        )
        copy.start()
        copy.wait()
        small[index + 1] = small[index] + small_land[index]
    outs[6][...] = small[5]
    for index, red in enumerate(work):
        layer_no, name = index // len(names), names[index % len(names)]
        if name == "down":
            red.finish(write_narrow(place, outs[5], layer_no, 384, 0))
        elif name == "up":

            def write(i, tile):
                for part in range(6):
                    outs[4][layer_no, :, 128 * part : 128 * part + 128] = tile[96 * part : 96 * part + 96]

            red.finish(write)
        elif name == "proj":
            red.finish(write_narrow(place, outs[3], layer_no, 96, 0))
        else:

            def write(i, tile):
                for part in range(3):
                    write_narrow(place, outs[part], layer_no, 96, 96 * part)(i, tile)

            red.finish(write)
    for index, red in enumerate(work):
        red.drain()
        core_copy(red, sources[index]).wait_send()


def core_copy(red, source):
    place = red.place
    return pltpu.make_async_remote_copy(
        src_ref=source.at[1 - place.c],
        dst_ref=red.landing.at[pl.ds(0, 8 * red.n)],
        send_sem=red.sends.at[0],
        recv_sem=red.receives.at[0],
        device_id=place.other("c"),
        device_id_type=MESH,
    )


def narrow_tiles(grad, x_first):
    k = grad.shape[0] // 8
    blocks = grad.reshape(2, 2, 2, k, 4, 192)
    own = blocks[..., :128]
    rest = blocks[..., 128:]
    halves = []
    for z0 in range(2):
        shared = jnp.concatenate([rest[..., z0, :], rest[..., z0 + 2, :]], axis=-1)
        halves.append(jnp.stack([own[..., z0, :], shared, own[..., z0 + 2, :]], axis=3))
    tiles = jnp.stack(halves, axis=3)
    order = (2, 1, 0, 3, 4, 5, 6) if x_first else (2, 0, 1, 3, 4, 5, 6)
    return tiles.transpose(order)


def wide_tiles(grad, x_first):
    k = grad.shape[0] // 8
    blocks = grad.reshape(2, 2, 2, k, 2, 2, 6, 128)
    order = (2, 1, 0, 5, 4, 6, 3, 7) if x_first else (2, 0, 1, 5, 4, 6, 3, 7)
    return blocks.transpose(order)


def reduce_all(grads):
    layer_count = len(grads)
    sources = []
    for entry in grads:
        for name, (n, rows, x_first) in PLANS.items():
            if name == "down":
                tiles = narrow_tiles(entry[5].astype(jnp.bfloat16), x_first)
            elif name == "up":
                tiles = wide_tiles(entry[4].astype(jnp.bfloat16), x_first)
            elif name == "proj":
                tiles = narrow_tiles(entry[3].astype(jnp.bfloat16), x_first)
            else:
                tiles = jnp.concatenate(
                    [narrow_tiles(entry[i].astype(jnp.bfloat16), x_first) for i in range(3)], axis=5
                )
            sources.append(tiles.reshape(2, 8 * n, rows, 128))
    small = jnp.concatenate(
        [
            jnp.concatenate([jnp.stack(entry[6:10]), entry[10].reshape(1, 768), jnp.zeros((3, 768))])
            for entry in grads
        ]
    ).astype(jnp.float32)
    count = len(sources)
    plans = [PLANS[name] for name in PLANS] * layer_count
    sem = pltpu.SemaphoreType.DMA
    results = pl.pallas_call(
        lambda *refs: reduce_kernel(layer_count, *refs),
        out_shape=[jax.ShapeDtypeStruct((layer_count, 96, 192), jnp.float32)] * 4
        + [
            jax.ShapeDtypeStruct((layer_count, 96, 768), jnp.float32),
            jax.ShapeDtypeStruct((layer_count, 384, 192), jnp.float32),
            jax.ShapeDtypeStruct(small.shape, jnp.float32),
        ],
        in_specs=[pl.BlockSpec(memory_space=pl.ANY)] * count + [pl.BlockSpec(memory_space=pltpu.VMEM)],
        out_specs=[pl.BlockSpec(memory_space=pltpu.VMEM)] * 7,
        scratch_shapes=[pltpu.VMEM((8 * plan[0], plan[1], 128), jnp.bfloat16) for plan in plans]
        + [pltpu.VMEM((landing_tiles(plan), plan[1], 128), jnp.bfloat16) for plan in plans]
        + [
            pltpu.VMEM((6,) + small.shape, jnp.float32),
            pltpu.VMEM((5,) + small.shape, jnp.float32),
            sem((count, 5)),
            sem((count, 5)),
            sem((count,)),
            sem((5,)),
            sem((5,)),
        ],
        compiler_params=pltpu.CompilerParams(
            collective_id=0, has_side_effects=True, vmem_limit_bytes=60 * 1024 * 1024
        ),
    )(*sources, small)
    return results


def beyond_eight(result):
    dp_size = lax.axis_size("dp")
    groups = dp_size // 8
    if groups == 1:
        return result
    result = lax.psum(result, "dp", axis_index_groups=[[g * 8 + i for g in range(groups)] for i in range(8)])
    whole = lax.all_gather(
        result, "dp", axis=1, tiled=True, axis_index_groups=[[g * 8 + i for i in range(8)] for g in range(groups)]
    )
    rows = whole.shape[1] // dp_size
    return lax.dynamic_slice_in_dim(whole, lax.axis_index("dp") * rows, rows, axis=1)


def shards(
    patches,
    keep,
    coords,
    query_w,
    key_w,
    value_w,
    proj_w,
    up_w,
    down_w,
    norm1_gain,
    norm1_bias,
    norm2_gain,
    norm2_bias,
    freqs,
    cotangent,
):
    images, patch_rows, model_width = patches.shape
    head_count = freqs.shape[2]
    head_dim = model_width // head_count
    token_rows = images * patch_rows
    layer_count = query_w.shape[0]
    cycle_size = lax.axis_size("blk")
    shape_four = (images, patch_rows, head_count, head_dim)
    kept_low = keep.astype(jnp.bfloat16)
    row_coord = coords[0].astype(jnp.float32)[:, :, None, None]
    column_coord = coords[1].astype(jnp.float32)[:, :, None, None]
    residual = patches.astype(jnp.float32).reshape(token_rows, model_width)
    stored = []
    for layer_no in range(layer_count):
        normed, norm_back = jax.vjp(
            layer_norm, residual, norm1_gain[layer_no], norm1_bias[layer_no]
        )
        normed_low = normed.astype(jnp.bfloat16)
        phase_angle = row_coord * freqs[layer_no, 0] + column_coord * freqs[layer_no, 1]
        cosine = jnp.cos(phase_angle)
        sine_part = jnp.sin(phase_angle)
        query_rot = rotate(
            jnp.dot(normed_low, query_w[layer_no], preferred_element_type=jnp.float32).reshape(
                shape_four
            ),
            cosine,
            sine_part,
        )
        key_rot = rotate(
            jnp.dot(normed_low, key_w[layer_no], preferred_element_type=jnp.float32).reshape(
                shape_four
            ),
            cosine,
            sine_part,
        )
        value_low = (
            jnp.dot(normed_low, value_w[layer_no], preferred_element_type=jnp.float32)
            .astype(jnp.bfloat16)
            .reshape(shape_four)
        )
        query_low = query_rot.astype(jnp.bfloat16)
        key_low = key_rot.astype(jnp.bfloat16)
        start_state = (
            jnp.full((images, head_count, patch_rows), MASKED_SCORE, jnp.float32),
            jnp.zeros((images, head_count, patch_rows), jnp.float32),
            jnp.zeros((images, head_count, patch_rows, head_dim), jnp.float32),
        )
        running = start_state
        held_key, held_value, held_kept = (key_low, value_low, kept_low)
        for cycle_step in range(cycle_size):
            running = merge_block(running, query_low, held_key, held_value, held_kept)
            if cycle_step + 1 < cycle_size:
                held_key, held_value, held_kept = passed_along(
                    (held_key, held_value, held_kept), "blk", 1
                )
        highest, denominator, weighted = running
        attended = (weighted / denominator[..., None]).transpose(0, 2, 1, 3)
        log_total = highest + jnp.log(denominator)
        attended_low = attended.reshape(token_rows, model_width).astype(jnp.bfloat16)
        middle = residual + jnp.dot(
            attended_low, proj_w[layer_no], preferred_element_type=jnp.float32
        )
        normed_two, norm_two_back = jax.vjp(
            layer_norm, middle, norm2_gain[layer_no], norm2_bias[layer_no]
        )
        normed_two_low = normed_two.astype(jnp.bfloat16)
        hidden = jnp.dot(normed_two_low, up_w[layer_no], preferred_element_type=jnp.float32)
        activated, gelu_back = jax.vjp(exact_gelu, hidden)
        activated_low = activated.astype(jnp.bfloat16)
        residual = middle + jnp.dot(
            activated_low, down_w[layer_no], preferred_element_type=jnp.float32
        )
        stored.append(
            (
                norm_back,
                normed_low,
                cosine,
                sine_part,
                query_rot,
                key_rot,
                query_low,
                key_low,
                value_low,
                attended,
                log_total,
                attended_low,
                norm_two_back,
                normed_two_low,
                gelu_back,
                activated_low,
            )
        )
    output = residual.astype(jnp.bfloat16).reshape(images, patch_rows, model_width)
    grad_residual = cotangent.astype(jnp.float32).reshape(token_rows, model_width)
    reduced = [None] * layer_count
    for layer_no in reversed(range(layer_count)):
        (
            norm_back,
            normed_low,
            cosine,
            sine_part,
            query_rot,
            key_rot,
            query_low,
            key_low,
            value_low,
            attended,
            log_total,
            attended_low,
            norm_two_back,
            normed_two_low,
            gelu_back,
            activated_low,
        ) = stored[layer_no]
        grad_branch = grad_residual.astype(jnp.bfloat16)
        grad_down = outer_sum(activated_low, grad_branch)
        grad_active = times_transposed(grad_branch, down_w[layer_no])
        grad_hidden = gelu_back(grad_active)[0].astype(jnp.bfloat16)
        grad_up = outer_sum(normed_two_low, grad_hidden)
        grad_middle_norm, grad_gain_two, grad_bias_two = norm_two_back(
            times_transposed(grad_hidden, up_w[layer_no])
        )
        grad_middle = grad_residual + grad_middle_norm
        grad_branch_one = grad_middle.astype(jnp.bfloat16)
        grad_proj = outer_sum(attended_low, grad_branch_one)
        grad_attended = (
            times_transposed(grad_branch_one, proj_w[layer_no])
            .astype(jnp.bfloat16)
            .reshape(shape_four)
        )
        delta_rows = jnp.sum(grad_attended.astype(jnp.float32) * attended, axis=-1).transpose(
            0, 2, 1
        )
        grad_query_rot = jnp.zeros(shape_four, jnp.float32)
        carried_key = jnp.zeros(shape_four, jnp.float32)
        carried_value = jnp.zeros(shape_four, jnp.float32)
        held_key, held_value, held_kept = (key_low, value_low, kept_low)
        for cycle_step in range(cycle_size):
            query_part, key_part, value_part = block_grads(
                query_low, grad_attended, log_total, delta_rows, held_key, held_value, held_kept
            )
            grad_query_rot = grad_query_rot + query_part
            carried_key = carried_key + key_part
            carried_value = carried_value + value_part
            if cycle_step + 1 < cycle_size:
                held_key, held_value, held_kept = passed_along(
                    (held_key, held_value, held_kept), "blk", 1
                )
            carried_key, carried_value = (
                passed_along(carried_key.astype(jnp.bfloat16), "blk", 1).astype(carried_key.dtype),
                passed_along(carried_value.astype(jnp.bfloat16), "blk", 1).astype(
                    carried_value.dtype
                ),
            )
        grad_key_rot, grad_value_sum = (carried_key, carried_value)
        angle_total = angle_grad(grad_query_rot, query_rot) + angle_grad(grad_key_rot, key_rot)
        grad_freq = jnp.stack(
            [
                jnp.sum(angle_total * row_coord, axis=(0, 1)),
                jnp.sum(angle_total * column_coord, axis=(0, 1)),
            ]
        )
        grad_query_low = (
            unrotate(grad_query_rot, cosine, sine_part)
            .astype(jnp.bfloat16)
            .reshape(token_rows, model_width)
        )
        grad_key_low = (
            unrotate(grad_key_rot, cosine, sine_part)
            .astype(jnp.bfloat16)
            .reshape(token_rows, model_width)
        )
        grad_value_low = grad_value_sum.astype(jnp.bfloat16).reshape(token_rows, model_width)
        grad_query_w = outer_sum(normed_low, grad_query_low)
        grad_key_w = outer_sum(normed_low, grad_key_low)
        grad_value_w = outer_sum(normed_low, grad_value_low)
        grad_normed = (
            times_transposed(grad_query_low, query_w[layer_no])
            + times_transposed(grad_key_low, key_w[layer_no])
            + times_transposed(grad_value_low, value_w[layer_no])
        )
        grad_input_norm, grad_gain_one, grad_bias_one = norm_back(grad_normed)
        grad_residual = grad_middle + grad_input_norm
        grads_now = (
            grad_query_w,
            grad_key_w,
            grad_value_w,
            grad_proj,
            grad_up,
            grad_down,
            grad_gain_one,
            grad_bias_one,
            grad_gain_two,
            grad_bias_two,
            grad_freq,
        )
        reduced[layer_no] = grads_now
    results = reduce_all(reduced)
    large = [beyond_eight(results[i]) for i in range(6)]
    small = results[6].reshape(layer_count, 8, model_width)
    if lax.axis_size("dp") > 8:
        groups = lax.axis_size("dp") // 8
        small = lax.psum(small, "dp", axis_index_groups=[[g * 8 + i for g in range(groups)] for i in range(8)])
    columns = model_width // lax.axis_size("blk")
    mine = lax.dynamic_slice_in_dim(small[:, :4], lax.axis_index("blk") * columns, columns, axis=2)
    freq = small[:, 4].reshape(freqs.shape)
    heads = head_count // lax.axis_size("blk")
    freq = lax.dynamic_slice_in_dim(freq, lax.axis_index("blk") * heads, heads, axis=2)
    return (
        output,
        grad_residual.reshape(images, patch_rows, model_width),
        *large,
        mine[:, 0],
        mine[:, 1],
        mine[:, 2],
        mine[:, 3],
        freq,
    )


def solution(mesh):
    placed = (
        P("dp", "blk", None),
        P("dp", "blk"),
        P(None, "dp", "blk"),
        P(),
        P(),
        P(),
        P(),
        P(),
        P(),
        P(),
        P(),
        P(),
        P(),
        P(),
        P("dp", "blk", None),
    )
    return jax.shard_map(
        shards,
        mesh=mesh,
        in_specs=placed,
        out_specs=(
            P("dp", "blk", None),
            P("dp", "blk", None),
            P(None, "dp", "blk"),
            P(None, "dp", "blk"),
            P(None, "dp", "blk"),
            P(None, "dp", "blk"),
            P(None, "dp", "blk"),
            P(None, "dp", "blk"),
            P(None, "blk"),
            P(None, "blk"),
            P(None, "blk"),
            P(None, "blk"),
            P(None, None, "blk", None),
        ),
        check_vma=False,
    )
```

```python
import jax
import jax.numpy as jnp
from jax import lax
from jax.experimental import pallas as pl
from jax.experimental.pallas import tpu as pltpu
from jax.sharding import PartitionSpec as P

MESH = pl.DeviceIdType.MESH
DP, BLK = "dp", "blk"
C, X, Y, Z0, Z1 = range(5)
BF16, F32 = jnp.bfloat16, jnp.float32
MASKED_SCORE = -1e30
NORM_EPSILON = 1e-06
LANES = 128
VMEM_BYTES = 61 * 1024 * 1024


def rows_by_columns(left, right):
    return lax.dot_general(left, right, (((1,), (0,)), ((), ())), preferred_element_type=F32)


def rows_by_rows(left, right):
    return lax.dot_general(left, right, (((1,), (1,)), ((), ())), preferred_element_type=F32)


def columns_by_columns(left, right):
    return lax.dot_general(left, right, (((0,), (0,)), ((), ())), preferred_element_type=F32)


class Place:
    def __init__(self):
        self.dp = lax.axis_index(DP)
        self.blk = lax.axis_index(BLK)
        self.c = lax.rem(self.dp, 2)
        self.x = lax.rem(self.dp // 2, 2)
        self.y = lax.rem(self.dp // 4, 2)
        self.z0 = lax.rem(self.blk, 2)
        self.z1 = lax.rem(self.blk // 2, 2)
        self.bits = (self.c, self.x, self.y, self.z0, self.z1)
        self.worker = (self.dp - self.c + self.z0, 2 * self.c + self.z1)
        self.owner = (self.dp - self.c + self.z1, 2 * self.z0 + self.c)
        self.stays = (self.worker[0] == self.dp) & (self.worker[1] == self.blk)

    def other(self, axis):
        if axis <= Y:
            return (self.dp + (1 << axis) * (1 - 2 * self.bits[axis]), self.blk)
        return (self.dp, self.blk + (1 << axis - Z0) * (1 - 2 * self.bits[axis]))

    def greet(self, axes):
        barrier = pltpu.get_barrier_semaphore()
        mine = 2 * self.blk + self.c
        for step in range(1, 8):
            them = lax.rem(mine + step, 8)
            pl.semaphore_signal(
                barrier, inc=1, device_id=(self.dp - self.c + lax.rem(them, 2), them // 2), device_id_type=MESH
            )
        for axis in axes:
            pl.semaphore_signal(barrier, inc=1, device_id=self.other(axis), device_id_type=MESH)
        pl.semaphore_wait(barrier, 7 + len(axes))


class Relocation:
    def __init__(self, place, source, target, sems, back=False):
        self.place, self.source, self.target, self.sems = place, source, target, sems
        self.device = place.owner if back else place.worker

    def remote(self):
        return pltpu.make_async_remote_copy(
            src_ref=self.source,
            dst_ref=self.target,
            send_sem=self.sems.at[0],
            recv_sem=self.sems.at[1],
            device_id=self.device,
            device_id_type=MESH,
        )

    def local(self):
        return pltpu.make_async_copy(self.source, self.target, self.sems.at[2])

    def start(self):
        pl.when(self.place.stays)(lambda: self.local().start())
        pl.when(jnp.logical_not(self.place.stays))(lambda: self.remote().start())

    def wait(self):
        pl.when(self.place.stays)(lambda: self.local().wait())
        pl.when(jnp.logical_not(self.place.stays))(lambda: self.remote().wait())


class Gather:
    def __init__(self, place, slots, sends, receives):
        self.place, self.slots, self.sends, self.receives = place, slots, sends, receives

    def copy(self, source, slot, axis):
        return pltpu.make_async_remote_copy(
            src_ref=self.slots.at[source],
            dst_ref=self.slots.at[slot],
            send_sem=self.sends.at[slot],
            recv_sem=self.receives.at[slot],
            device_id=self.place.other(axis),
            device_id_type=MESH,
        )

    def start(self):
        self.copy(0, 2, Z0).start()
        self.copy(0, 1, C).start()

    def near(self):
        self.copy(0, 1, C).wait_recv()

    def far(self):
        self.copy(0, 2, Z0).wait_recv()
        self.copy(2, 3, C).start()

    def last(self):
        self.copy(2, 3, C).wait_recv()

    def drain(self):
        self.copy(0, 1, C).wait_send()
        self.copy(0, 2, Z0).wait_send()
        self.copy(2, 3, C).wait_send()


class Swap:
    def __init__(self, place, axis, source, target, sems):
        self.place, self.axis, self.source, self.target, self.sems = place, axis, source, target, sems

    def copy(self):
        return pltpu.make_async_remote_copy(
            src_ref=self.source,
            dst_ref=self.target,
            send_sem=self.sems.at[0],
            recv_sem=self.sems.at[1],
            device_id=self.place.other(self.axis),
            device_id_type=MESH,
        )

    def start(self):
        self.copy().start()

    def arrive(self):
        self.copy().wait_recv()

    def drain(self):
        self.copy().wait_send()


def lane_index(rows):
    return lax.broadcasted_iota(jnp.int32, (rows, LANES), 1)


def partner_tile(tile, former):
    return jnp.where(former, pltpu.roll(tile, 96, 1), pltpu.roll(tile, 32, 1))


def rotate_tile(tile, cosine, signed_sine, former):
    return tile * cosine + partner_tile(tile, former) * signed_sine


def tile_of(index):
    return slice(LANES * index, LANES * index + LANES)


def normalise(values):
    centre = values - jnp.mean(values, axis=-1, keepdims=True)
    spread = jnp.mean(centre * centre, axis=-1, keepdims=True)
    scale = lax.rsqrt(spread + NORM_EPSILON)
    return centre * scale, scale


QUERY_W, KEY_W, VALUE_W, PROJ_W, UP_W, DOWN_W = range(6)


class Weights:
    def __init__(self, whole, qkv, proj, up, down, sems):
        width = qkv.shape[1] // 3
        self.whole, self.sems = whole, sems
        self.buffers = [qkv.at[:, pl.ds(part * width, width)] for part in range(3)] + [proj, up, down]

    def copy(self, name, layer_no):
        return pltpu.make_async_copy(self.whole[name].at[layer_no], self.buffers[name], self.sems.at[name])

    def load(self, layer_no, *names):
        for name in names:
            self.copy(name, layer_no).start()

    def ready(self, layer_no, *names):
        for name in names:
            self.copy(name, layer_no).wait()


SAVED = range(14)
NORMED, KEYS, VALUES, QUERIES, MIXED, NORMED2, ACTS, FAR_ACTS = range(8)
SLOPES, HAT1, HAT2, SCALES, LOGS, ANGLES = range(8, 14)


def saved_shapes(layers, rows, width, hidden):
    heads_part = hidden // 8
    return {
        NORMED: ((layers, 2, rows, width), BF16),
        KEYS: ((layers, 4, rows, width), BF16),
        VALUES: ((layers, 4, rows, width), BF16),
        QUERIES: ((layers, 4, rows, width + LANES), BF16),
        MIXED: ((layers, 2, rows, width), BF16),
        NORMED2: ((layers, 2, rows, width), BF16),
        ACTS: ((layers, 2, 4, rows, heads_part), BF16),
        FAR_ACTS: ((layers, 4, rows, heads_part), BF16),
        SLOPES: ((layers, rows, hidden), BF16),
        HAT1: ((layers, rows, width), BF16),
        HAT2: ((layers, rows, width), BF16),
        SCALES: ((layers, rows, LANES), F32),
        LOGS: ((layers, rows, LANES), F32),
        ANGLES: ((layers, 2, rows, width), F32),
    }


def forward_kernel(layers, *refs):
    patches, cotangent, norms, freqs = refs[:4]
    whole = refs[4:10]
    out, far_cotangent, marks = refs[10:13]
    saved = dict(zip(SAVED, refs[13 : 13 + len(SAVED)]))
    scratch = refs[13 + len(SAVED) :]
    kept = dict(zip(SAVED, scratch[: len(SAVED)]))
    (qkv_w, proj_w, up_w, down_w, w_sems, start, start_sems, cot_sems, aux, aux_sends, aux_receives) = scratch[
        len(SAVED) : len(SAVED) + 11
    ]
    (normed, h_sends, h_receives, q_sends, q_receives, swap_sems, cosine, sine, residual, result, save_sems) = scratch[
        len(SAVED) + 11 :
    ]
    place = Place()
    rows, width = residual.shape
    hidden = up_w.shape[1]
    pairs = width // LANES
    weights = Weights(whole, qkv_w, proj_w, up_w, down_w, w_sems)
    weights.load(0, KEY_W, VALUE_W, QUERY_W, PROJ_W, UP_W, DOWN_W)
    place.greet((X,))
    arrival = Relocation(place, patches, start, start_sems)
    arrival.start()
    other_arrival = Relocation(place, cotangent, far_cotangent, cot_sems)
    other_arrival.start()
    arrival.wait()
    aux[0] = start[:, width : width + LANES]
    aux_gather = Gather(place, aux, aux_sends, aux_receives)
    aux_gather.start()
    residual[...] = start[:, :width].astype(F32)
    lane = lane_index(rows)
    former = lax.rem(lane, 64) < 32
    first_head = lane < 64
    one_lane = jnp.where(lane == 0, 1.0, 0.0).astype(BF16)
    pending = []

    def save(name, layer_no, source=None, target=None):
        source = kept[name].at[layer_no] if source is None else source
        target = saved[name].at[layer_no] if target is None else target
        copy = pltpu.make_async_copy(source, target, save_sems.at[len(pending)])
        copy.start()
        pending.append(copy)

    def make_angles(layer_no, slot):
        rows_at = aux[slot][:, 1:2].astype(F32)
        columns_at = aux[slot][:, 2:3].astype(F32)
        for index in range(pairs):
            sl = tile_of(index)
            angle = rows_at * freqs[layer_no, 0:1, sl] + columns_at * freqs[layer_no, 1:2, sl]
            cosine[slot, :, sl] = jnp.cos(angle)
            sine[slot, :, sl] = jnp.where(former, -1.0, 1.0) * jnp.sin(angle)

    def rotated(values, slot, index):
        return rotate_tile(values, cosine[slot, :, tile_of(index)], sine[slot, :, tile_of(index)], former)

    def keys_and_values(layer_no, slot, all_three):
        block = normed[layer_no, slot]
        first = 0 if all_three else width
        products = rows_by_columns(block, qkv_w[:, first:])
        if all_three:
            for index in range(pairs):
                turned = rotated(products[:, tile_of(index)], slot, index)
                kept[QUERIES][layer_no, slot, :, tile_of(index)] = (0.125 * turned).astype(BF16)
            products = products[:, width:]
        for index in range(pairs):
            turned = rotated(products[:, tile_of(index)], slot, index)
            kept[KEYS][layer_no, slot, :, tile_of(index)] = turned.astype(BF16)
        kept[VALUES][layer_no, slot] = products[:, width:].astype(BF16)

    gathers, swaps = [aux_gather], []
    for layer_no in range(layers):
        hat, scale = normalise(residual[...])
        kept[HAT1][layer_no] = hat.astype(BF16)
        normed[layer_no, 0] = (hat * norms[layer_no, 0:1] + norms[layer_no, 1:2]).astype(BF16)
        gather = Gather(place, normed.at[layer_no], h_sends.at[layer_no], h_receives.at[layer_no])
        gather.start()
        gathers.append(gather)
        save(HAT1, layer_no)
        make_angles(layer_no, 0)
        weights.ready(layer_no, KEY_W, VALUE_W, QUERY_W)
        keys_and_values(layer_no, 0, True)
        if layer_no == 0:
            aux_gather.near()
            aux_gather.far()
        make_angles(layer_no, 1)
        gather.near()
        keys_and_values(layer_no, 1, False)
        make_angles(layer_no, 2)
        if layer_no == 0:
            aux_gather.last()
        make_angles(layer_no, 3)
        gather.far()
        keys_and_values(layer_no, 2, False)
        gather.last()
        keys_and_values(layer_no, 3, False)
        if layer_no + 1 < layers:
            weights.load(layer_no + 1, KEY_W, VALUE_W, QUERY_W)
        save(NORMED, layer_no, normed.at[layer_no, 0], saved[NORMED].at[layer_no, 0])
        save(NORMED, layer_no, normed.at[layer_no, 2], saved[NORMED].at[layer_no, 1])
        save(KEYS, layer_no)
        save(VALUES, layer_no)
        kept[ANGLES][layer_no, 0] = cosine[0]
        kept[ANGLES][layer_no, 1] = sine[0]
        save(ANGLES, layer_no)
        marks_of_keys = aux[...].reshape(4 * rows, LANES)
        logs = jnp.zeros((rows, LANES), F32)
        for index in range(pairs):
            sl = tile_of(index)
            query_pair = kept[QUERIES][layer_no, 0, :, sl]
            key_pair = kept[KEYS][layer_no, :, :, sl].reshape(4 * rows, LANES)
            value_pair = kept[VALUES][layer_no, :, :, sl].reshape(4 * rows, LANES)
            extended = jnp.concatenate([key_pair, marks_of_keys], axis=1)
            mixed = []
            for member in range(2):
                mine = first_head if member == 0 else jnp.logical_not(first_head)
                query = jnp.where(mine, query_pair, jnp.zeros_like(query_pair))
                scores = rows_by_rows(jnp.concatenate([query, one_lane], axis=1), extended)
                highest = jnp.max(scores, axis=1, keepdims=True)
                weight = jnp.exp(scores - highest)
                total = jnp.sum(weight, axis=1, keepdims=True)
                mixed.append(rows_by_columns(weight.astype(BF16), value_pair) / total)
                logs = jnp.where(lane == 2 * index + member, highest + jnp.log(total), logs)
            kept[MIXED][layer_no, 0, :, sl] = jnp.where(first_head, mixed[0], mixed[1]).astype(BF16)
        kept[LOGS][layer_no] = logs
        save(LOGS, layer_no)
        kept[QUERIES][layer_no, 0, :, width:] = spread_lanes(-logs, lane, 1.0).astype(BF16)
        query_gather = Gather(place, kept[QUERIES].at[layer_no], q_sends.at[layer_no], q_receives.at[layer_no])
        attended_swap = Swap(
            place, Z0, kept[MIXED].at[layer_no, 0], kept[MIXED].at[layer_no, 1], swap_sems.at[layer_no, 0]
        )
        if layer_no == 0:
            query_gather.start()
            gathers.append(query_gather)
            attended_swap.start()
            swaps.append(attended_swap)
        weights.ready(layer_no, PROJ_W)
        middle = residual[...] + rows_by_columns(kept[MIXED][layer_no, 0], proj_w[...])
        if layer_no + 1 < layers:
            weights.load(layer_no + 1, PROJ_W)
        hat, scale_two = normalise(middle)
        kept[HAT2][layer_no] = hat.astype(BF16)
        save(HAT2, layer_no)
        kept[SCALES][layer_no] = jnp.where(lane == 0, scale, scale_two)
        save(SCALES, layer_no)
        kept[NORMED2][layer_no, 0] = (hat * norms[layer_no, 2:3] + norms[layer_no, 3:4]).astype(BF16)
        normed_swap = Swap(
            place, Z0, kept[NORMED2].at[layer_no, 0], kept[NORMED2].at[layer_no, 1], swap_sems.at[layer_no, 1]
        )
        if layer_no == 0:
            normed_swap.start()
            swaps.append(normed_swap)
        residual[...] = middle
        weights.ready(layer_no, UP_W)
        half = hidden // 8
        for quarter in range(4):
            columns = slice(2 * half * quarter, 2 * half * quarter + 2 * half)
            hidden_part = rows_by_columns(kept[NORMED2][layer_no, 0], up_w[:, columns])
            share = 0.5 + 0.5 * lax.erf(hidden_part * 0.7071067811865476)
            active = (hidden_part * share).astype(BF16)
            slope = share + hidden_part * (0.3989422804014327 * jnp.exp(-0.5 * hidden_part * hidden_part))
            kept[SLOPES][layer_no, :, columns] = slope.astype(BF16)
            y, x = quarter // 2, quarter % 2
            kept[ACTS][layer_no, x, 2 * y] = active[:, :half]
            kept[ACTS][layer_no, x, 2 * y + 1] = active[:, half:]
            if quarter == 0:
                weights.ready(layer_no, DOWN_W)
            residual[...] += rows_by_columns(active, down_w[columns, :])
        if layer_no + 1 < layers:
            weights.load(layer_no + 1, UP_W, DOWN_W)
        active_swap = Swap(
            place,
            X,
            kept[ACTS].at[layer_no, 1 - place.x],
            kept[FAR_ACTS].at[layer_no],
            swap_sems.at[layer_no, 2],
        )
        if layer_no == 0:
            active_swap.start()
            swaps.append(active_swap)
        save(SLOPES, layer_no)
        save(ACTS, layer_no)
        if layer_no > 0:
            for name in (QUERIES, MIXED, NORMED2):
                save(name, layer_no, kept[name].at[layer_no, 0], saved[name].at[layer_no, 0])
    result[...] = residual[...].astype(BF16)
    leave = pltpu.make_async_copy(result, out, save_sems.at[len(pending)])
    leave.start()
    pending.append(leave)
    leave = pltpu.make_async_copy(aux, marks, save_sems.at[len(pending)])
    leave.start()
    pending.append(leave)
    query_gather = gathers[2]
    query_gather.near()
    query_gather.far()
    query_gather.last()
    for swap in swaps:
        swap.arrive()
    for name in (QUERIES, MIXED, NORMED2, FAR_ACTS):
        save(name, 0)
    other_arrival.wait()
    for gather in gathers:
        gather.drain()
    for swap in swaps:
        swap.drain()
    for copy in pending:
        copy.wait()


def spread_lanes(columns, lane, last):
    columns = jnp.where(lane < 16, columns, 0.0)
    high = columns.astype(BF16).astype(F32)
    middle = (columns - high).astype(BF16).astype(F32)
    low = columns - high - middle
    spread = high + pltpu.roll(middle, 16, 1) + pltpu.roll(low, 32, 1)
    return jnp.where(lane == 127, last, spread)


def forward_call(patches, cotangent, norms, freqs, whole):
    layers = norms.shape[0]
    rows, padded = patches.shape
    width = padded - LANES
    hidden = whole[4].shape[2]
    shapes = saved_shapes(layers, rows, width, hidden)
    sem = pltpu.SemaphoreType.DMA
    any_spec, vmem_spec = pl.BlockSpec(memory_space=pl.ANY), pl.BlockSpec(memory_space=pltpu.VMEM)
    outs = [
        jax.ShapeDtypeStruct((rows, width), BF16),
        jax.ShapeDtypeStruct((rows, width), BF16),
        jax.ShapeDtypeStruct((4, rows, LANES), BF16),
    ] + [jax.ShapeDtypeStruct(*shapes[name]) for name in SAVED]
    return pl.pallas_call(
        lambda *refs: forward_kernel(layers, *refs),
        out_shape=outs,
        in_specs=[any_spec, any_spec, vmem_spec, vmem_spec] + [any_spec] * 6,
        out_specs=[any_spec] * len(outs),
        scratch_shapes=[pltpu.VMEM(*shapes[name]) for name in SAVED]
        + [
            pltpu.VMEM((width, 3 * width), BF16),
            pltpu.VMEM((width, width), BF16),
            pltpu.VMEM((width, hidden), BF16),
            pltpu.VMEM((hidden, width), BF16),
            sem((6,)),
            pltpu.VMEM((rows, padded), BF16),
            sem((3,)),
            sem((3,)),
            pltpu.VMEM((4, rows, LANES), BF16),
            sem((4,)),
            sem((4,)),
            pltpu.VMEM((layers, 4, rows, width), BF16),
            sem((layers, 4)),
            sem((layers, 4)),
            sem((layers, 4)),
            sem((layers, 4)),
            sem((layers, 3, 2)),
            pltpu.VMEM((4, rows, width), F32),
            pltpu.VMEM((4, rows, width), F32),
            pltpu.VMEM((rows, width), F32),
            pltpu.VMEM((rows, width), BF16),
            sem((64,)),
        ],
        compiler_params=pltpu.CompilerParams(
            collective_id=0, has_side_effects=True, vmem_limit_bytes=VMEM_BYTES
        ),
    )(patches, cotangent, norms, freqs, *whole)


class Reduction:
    def __init__(self, place, axes, n, share, landing, sends, receives):
        self.place, self.axes = place, axes + (Z1,)
        self.share, self.landing, self.sends, self.receives = share, landing, sends, receives
        self.plan = []
        base, half, land = 0, 4 * n, 0
        for axis in axes:
            bit = place.bits[axis]
            self.plan.append((base + (1 - bit) * half, base + bit * half, half, land))
            base, land, half = base + bit * half, land + half, half // 2
        self.plan.append((base + 1 - place.z1, base + place.z1, n - 1, land))

    def copy(self, stage):
        send, _, count, land = self.plan[stage]
        return pltpu.make_async_remote_copy(
            src_ref=self.share.at[pl.ds(send, count)],
            dst_ref=self.landing.at[pl.ds(land, count)],
            send_sem=self.sends.at[stage],
            recv_sem=self.receives.at[stage],
            device_id=self.place.other(self.axes[stage]),
            device_id_type=MESH,
        )

    def start(self, stage=0):
        self.copy(stage).start()

    def step(self, stage):
        _, keep, count, land = self.plan[stage]
        self.copy(stage).wait_recv()

        def body(i, carry):
            total = self.share[keep + i].astype(F32) + self.landing[land + i].astype(F32)
            self.share[keep + i] = total.astype(BF16)
            return carry

        lax.fori_loop(0, count, body, 0)
        self.start(stage + 1)

    def finish(self, write):
        _, keep, count, land = self.plan[3]
        self.copy(3).wait_recv()
        for i in range(count):
            write(i, self.share[keep + i].astype(F32) + self.landing[land + i].astype(F32))

    def drain(self):
        for stage in range(4):
            self.copy(stage).wait_send()


class Doubling:
    AXES = (C, X, Y, Z0, Z1)

    def __init__(self, place, sums, landing, sems):
        self.place, self.sums, self.landing, self.sems = place, sums, landing, sems

    def copy(self, stage):
        return pltpu.make_async_remote_copy(
            src_ref=self.sums.at[stage],
            dst_ref=self.landing.at[stage],
            send_sem=self.sems.at[stage, 0],
            recv_sem=self.sems.at[stage, 1],
            device_id=self.place.other(self.AXES[stage]),
            device_id_type=MESH,
        )

    def start(self):
        self.copy(0).start()

    def step(self, stage):
        self.copy(stage).wait()
        self.sums[stage + 1] = self.sums[stage] + self.landing[stage]
        if stage + 1 < len(self.AXES):
            self.copy(stage + 1).start()


TENSORS = DOWN, UP, PROJ, QKV = range(4)
HALVING = {DOWN: (C, Y, Z0), UP: (C, X, Y), PROJ: (C, X, Y), QKV: (C, Y, X)}


def tile_plan(width, hidden):
    return {
        DOWN: (3, hidden // 8),
        UP: (2, (width // 8) * (hidden // 4 // LANES)),
        PROJ: (3, width // 8),
        QKV: (3, 3 * width // 8),
    }


def landing_count(n):
    return 4 * n + 2 * n + n + n - 1


def by_halves(tiles, first):
    def turned(tile):
        return pltpu.roll(tile, 64, 1)

    return (
        (tiles[0], jnp.where(first, tiles[1], turned(tiles[4])), tiles[3]),
        (
            jnp.where(first, turned(tiles[1]), turned(tiles[2])),
            jnp.where(first, turned(tiles[2]), tiles[5]),
            jnp.where(first, turned(tiles[4]), turned(tiles[5])),
        ),
    )


def narrow_writer(place, out, layer_no, rows, first_row):
    def write(i, tile):
        tile = tile[first_row : first_row + rows]

        @pl.when(place.z1 == i)
        def _():
            out[layer_no, :, 0:LANES] = tile

        @pl.when((place.z1 == 1 - i) & (place.z1 == 0))
        def _():
            out[layer_no, :, LANES : LANES + 64] = tile[:, 0:64]

        @pl.when((place.z1 == 1 - i) & (place.z1 == 1))
        def _():
            out[layer_no, :, LANES : LANES + 64] = tile[:, 64:LANES]

    return write


def backward_kernel(layers, *refs):
    out, cotangent, marks, norms = refs[:4]
    whole = refs[4:10]
    saved = dict(zip(SAVED, refs[10 : 10 + len(SAVED)]))
    refs = refs[10 + len(SAVED) :]
    output, grad_patches, grad_query, grad_key, grad_value, grad_proj, grad_up, grad_down, grad_small = refs[:9]
    refs = refs[9:]
    held = dict(zip(SAVED, refs[: len(SAVED)]))
    refs = refs[len(SAVED) :]
    shares, landings = refs[: layers * 4], refs[layers * 4 : layers * 8]
    refs = refs[layers * 8 :]
    (qkv_w, proj_w, up_w, down_w, w_sems, load_sems, back_sems) = refs[:7]
    (douts, do_sends, do_receives, q_sends, q_receives, swap_sems, sends, receives) = refs[7:15]
    (errors, grad_hidden, far_hidden, grad_middle, far_middle, grad_qkv, half_qkv, far_qkv) = refs[15:23]
    (carried, dq, dk, dv, sums, sums_landing, sums_sems) = refs[23:]
    place = Place()
    rows, width = carried.shape
    hidden = up_w.shape[1]
    half = hidden // 8
    pairs = width // LANES
    last_layer = layers - 1
    weights = Weights(whole, qkv_w, proj_w, up_w, down_w, w_sems)

    def source_of(name, layer_no):
        source = saved[name].at[layer_no]
        target = held[name]
        if name == ACTS:
            return source.at[place.x], target
        if layer_no == last_layer and name in (QUERIES, MIXED, NORMED2):
            return source.at[0], target.at[0]
        return source, target

    def load(layer_no, *names):
        for name in names:
            source, target = source_of(name, layer_no)
            pltpu.make_async_copy(source, target, load_sems.at[name]).start()

    def ready(layer_no, *names):
        for name in names:
            source, target = source_of(name, layer_no)
            pltpu.make_async_copy(source, target, load_sems.at[name]).wait()

    weights.load(last_layer, DOWN_W)
    load(last_layer, SLOPES, QUERIES, MIXED, NORMED2)
    weights.load(last_layer, UP_W)
    load(last_layer, HAT2, SCALES, LOGS)
    weights.load(last_layer, PROJ_W)
    load(last_layer, KEYS, VALUES, ACTS, ANGLES, HAT1, NORMED)
    weights.load(last_layer, QUERY_W, KEY_W, VALUE_W)
    place.greet((X, Y))

    lane = lane_index(rows)
    former = lax.rem(lane, 64) < 32
    first_head = lane < 64
    plans = tile_plan(width, hidden)
    reductions = {}
    for layer_no in range(layers):
        for index, name in enumerate(TENSORS):
            at = layer_no * 4 + index
            reductions[layer_no, name] = Reduction(
                place, HALVING[name], plans[name][0], shares[at], landings[at], sends.at[at], receives.at[at]
            )
    doubling = Doubling(place, sums, sums_landing, sums_sems)
    sums[0] = jnp.zeros(sums.shape[1:], F32)

    def swap(layer_no, number, axis, source, target):
        return Swap(place, axis, source, target, swap_sems.at[layer_no, number])

    error_swaps = [swap(l, 0, X, errors.at[l, 0], errors.at[l, 1]) for l in range(layers)]
    hidden_swaps = [swap(l, 1, Z0, grad_hidden.at[1 - place.z0], far_hidden.at[l]) for l in range(layers)]
    middle_swaps = [swap(l, 2, Z0, grad_middle.at[1 - place.z0], far_middle.at[l]) for l in range(layers)]
    qkv_swaps = [swap(l, 3, Z0, half_qkv.at[1 - place.z0], far_qkv.at[l]) for l in range(layers)]
    obb_swap = swap(last_layer, 4, Z0, held[MIXED].at[0], held[MIXED].at[1])
    gg_swap = swap(last_layer, 5, Z0, held[NORMED2].at[0], held[NORMED2].at[1])
    acts_swap = swap(last_layer, 6, X, saved[ACTS].at[last_layer, 1 - place.x], held[FAR_ACTS])
    query_gather = Gather(place, held[QUERIES], q_sends, q_receives)
    do_gathers = [Gather(place, douts.at[l], do_sends.at[l], do_receives.at[l]) for l in range(layers)]
    out_return = Relocation(place, out, output, back_sems.at[0], back=True)
    grad_return = Relocation(place, carried, grad_patches, back_sems.at[1], back=True)

    def note(layer_no, row, values):
        sums[0, 8 * layer_no + row : 8 * layer_no + row + 1] = jnp.sum(values, axis=0, keepdims=True)

    def norm_back(layer_no, number, grad, hat, scale):
        note(layer_no, 2 * number, grad * hat)
        note(layer_no, 2 * number + 1, grad)
        grad = grad * norms[layer_no, 2 * number : 2 * number + 1]
        mean = jnp.mean(grad, axis=-1, keepdims=True)
        slope = jnp.mean(grad * hat, axis=-1, keepdims=True)
        return scale * (grad - mean - hat * slope)

    def halves_of(values):
        return by_halves([values[:, tile_of(i)] for i in range(pairs)], first_head)

    def send_error(layer_no, values):
        for z0, tiles in enumerate(halves_of(values)):
            for i, tile in enumerate(tiles):
                errors[layer_no, 0, :, tile_of(3 * z0 + i)] = tile.astype(BF16)
        error_swaps[layer_no].start()
        return values.astype(BF16)

    def feed_forward(layer_no, error):
        weights.ready(layer_no, DOWN_W)
        ready(layer_no, SLOPES)
        for quarter in range(4):
            columns = slice(2 * half * quarter, 2 * half * quarter + 2 * half)
            grad = rows_by_rows(error, down_w[columns, :])
            grad = grad * held[SLOPES][:, columns].astype(F32)
            grad_hidden[quarter % 2, quarter // 2] = grad.astype(BF16)
        if layer_no > 0:
            weights.load(layer_no - 1, DOWN_W)
            load(layer_no - 1, SLOPES)
        weights.ready(layer_no, UP_W)
        total = jnp.zeros((rows, width), F32)
        for quarter in range(4):
            columns = slice(2 * half * quarter, 2 * half * quarter + 2 * half)
            total = total + rows_by_rows(grad_hidden[quarter % 2, quarter // 2], up_w[:, columns])
        if layer_no > 0:
            weights.load(layer_no - 1, UP_W)
        ready(layer_no, HAT2, SCALES)
        hat = held[HAT2][...].astype(F32)
        carried[...] += norm_back(layer_no, 1, total, hat, held[SCALES][:, 1:2])
        if layer_no > 0:
            load(layer_no - 1, HAT2)

    def project_back(layer_no):
        middle = carried[...]
        error = middle.astype(BF16)
        weights.ready(layer_no, PROJ_W)
        grad = rows_by_rows(error, proj_w[...])
        if layer_no > 0:
            weights.load(layer_no - 1, PROJ_W)
        ready(layer_no, MIXED)
        deltas = jnp.zeros((rows, LANES), F32)
        for index in range(pairs):
            sl = tile_of(index)
            low = grad[:, sl].astype(BF16)
            douts[layer_no, 0, :, sl] = low
            product = low.astype(F32) * held[MIXED][0, :, sl].astype(F32)
            for member in range(2):
                mine = first_head if member == 0 else jnp.logical_not(first_head)
                delta = jnp.sum(jnp.where(mine, product, 0.0), axis=1, keepdims=True)
                deltas = jnp.where(lane == 2 * index + member, delta, deltas)
        douts[layer_no, 0, :, width:] = spread_lanes(-deltas, lane, 0.0).astype(BF16)
        do_gathers[layer_no].start()
        for z0, tiles in enumerate(halves_of(middle)):
            for i, tile in enumerate(tiles):
                grad_middle[z0, :, tile_of(i)] = tile.astype(BF16)
        hidden_swaps[layer_no].start()
        middle_swaps[layer_no].start()
        return deltas

    def own_queries(layer_no, deltas):
        ready(layer_no, KEYS, VALUES, LOGS)
        one_lane = jnp.where(lane == 0, 1.0, 0.0).astype(BF16)
        key_marks = marks[...].reshape(4 * rows, LANES)
        for index in range(pairs):
            sl = tile_of(index)
            query_pair = held[QUERIES][0, :, sl]
            key_pair = held[KEYS][:, :, sl].reshape(4 * rows, LANES)
            value_pair = held[VALUES][:, :, sl].reshape(4 * rows, LANES)
            grad_pair = douts[layer_no, 0, :, sl]
            extended = jnp.concatenate([key_pair, key_marks], axis=1)
            parts = []
            for member in range(2):
                mine = first_head if member == 0 else jnp.logical_not(first_head)
                head = 2 * index + member
                zero = jnp.zeros_like(query_pair)
                scores = rows_by_rows(
                    jnp.concatenate([jnp.where(mine, query_pair, zero), one_lane], axis=1), extended
                )
                weight = jnp.exp(scores - held[LOGS][:, head : head + 1])
                grad = rows_by_rows(jnp.where(mine, grad_pair, zero), value_pair)
                grad = (weight * (grad - deltas[:, head : head + 1])).astype(BF16)
                parts.append(rows_by_columns(grad, key_pair))
            dq[:, sl] = 0.125 * jnp.where(first_head, parts[0], parts[1])

    def own_keys(layer_no):
        own_marks = marks[0]
        for index in range(pairs):
            sl = tile_of(index)
            key_pair, value_pair = held[KEYS][0, :, sl], held[VALUES][0, :, sl]
            query_pair = held[QUERIES][:, :, sl].reshape(4 * rows, LANES)
            grad_pair = douts[layer_no, :, :, sl].reshape(4 * rows, LANES)
            queries = jnp.concatenate([query_pair, held[QUERIES][:, :, width:].reshape(4 * rows, LANES)], axis=1)
            grads = jnp.concatenate([grad_pair, douts[layer_no, :, :, width:].reshape(4 * rows, LANES)], axis=1)
            key_parts, value_parts = [], []
            for member in range(2):
                mine = first_head if member == 0 else jnp.logical_not(first_head)
                head = 2 * index + member
                zero = jnp.zeros_like(key_pair)
                chosen = jnp.where((lane < 48) & (lax.rem(lane, 16) == head), 1.0, 0.0).astype(BF16)
                marked = jnp.where(lane == 127, jnp.broadcast_to(own_marks[:, 0:1], chosen.shape), chosen)
                weight = jnp.exp(
                    rows_by_rows(jnp.concatenate([jnp.where(mine, key_pair, zero), marked], axis=1), queries)
                )
                grad = rows_by_rows(jnp.concatenate([jnp.where(mine, value_pair, zero), chosen], axis=1), grads)
                grad = (weight * grad).astype(BF16)
                key_parts.append(rows_by_columns(grad, query_pair))
                value_parts.append(rows_by_columns(weight.astype(BF16), grad_pair))
            dk[:, sl] = jnp.where(first_head, key_parts[0], key_parts[1])
            dv[:, sl] = jnp.where(first_head, value_parts[0], value_parts[1])

    def attention_inputs_back(layer_no):
        ready(layer_no, ANGLES)
        row_at = marks[0][:, 1:2].astype(F32)
        column_at = marks[0][:, 2:3].astype(F32)
        parts = [[], [], []]
        for index in range(pairs):
            sl = tile_of(index)
            cosine, sine = held[ANGLES][0, :, sl], held[ANGLES][1, :, sl]
            turn = jnp.zeros((rows, LANES), F32)
            for number, (grad_ref, forward) in enumerate(
                ((dq, 8.0 * held[QUERIES][0, :, sl].astype(F32)), (dk, held[KEYS][0, :, sl].astype(F32)))
            ):
                grad = grad_ref[:, sl]
                turn = turn + grad * partner_tile(forward, former)
                back = grad * cosine - partner_tile(grad, former) * sine
                parts[number].append(back)
                grad_qkv[:, number * width + LANES * index : number * width + LANES * index + LANES] = back.astype(BF16)
            parts[2].append(dv[:, sl])
            grad_qkv[:, 2 * width + LANES * index : 2 * width + LANES * index + LANES] = dv[:, sl].astype(BF16)
            sums[0, 8 * layer_no + 4 : 8 * layer_no + 5, sl] = jnp.sum(turn * row_at, axis=0, keepdims=True)
            sums[0, 8 * layer_no + 5 : 8 * layer_no + 6, sl] = jnp.sum(turn * column_at, axis=0, keepdims=True)
        for number in range(3):
            for z0, tiles in enumerate(by_halves(parts[number], first_head)):
                for i, tile in enumerate(tiles):
                    half_qkv[z0, number, :, tile_of(i)] = tile.astype(BF16)
        qkv_swaps[layer_no].start()
        if layer_no > 0:
            load(layer_no - 1, KEYS, VALUES, ANGLES, LOGS)

    def input_back(layer_no):
        weights.ready(layer_no, QUERY_W, KEY_W, VALUE_W)
        total = rows_by_rows(grad_qkv[...], qkv_w[...])
        if layer_no > 0:
            weights.load(layer_no - 1, QUERY_W, KEY_W, VALUE_W)
        ready(layer_no, HAT1)
        hat = held[HAT1][...].astype(F32)
        carried[...] += norm_back(layer_no, 0, total, hat, held[SCALES][:, 0:1])
        if layer_no > 0:
            load(layer_no - 1, HAT1, SCALES)

    def put(layer_no, name, values, column, blocks):
        share = reductions[layer_no, name].share
        for first_row, count, tile, inner in blocks:
            for i in range(values.shape[1] // LANES):
                piece = values[first_row : first_row + count, tile_of(i)].astype(BF16)
                place_tile, place_row = column(tile, inner, i)
                share[place_tile, place_row : place_row + count] = piece

    def down_product(layer_no):
        ready(layer_no, ACTS)
        error_swaps[layer_no].arrive()
        if layer_no == last_layer:
            acts_swap.arrive()
        else:
            ready(layer_no, FAR_ACTS)
        for y in range(2):
            for c in range(2):
                product = columns_by_columns(held[ACTS][2 * y + c], errors[layer_no, 0]) + columns_by_columns(
                    held[FAR_ACTS][2 * y + c], errors[layer_no, 1]
                )
                put(layer_no, DOWN, product, lambda tile, inner, i: (tile + i, 0), [(0, half, (2 * c + y) * 6, 0)])
        if layer_no > 0:
            load(layer_no - 1, ACTS, FAR_ACTS)
        reductions[layer_no, DOWN].start()

    def blocks_of(axes, n, inner):
        size = width // 8
        blocks = []
        for number in range(8):
            bits = (number % 2, (number // 2) % 2, number // 4)
            tile = ((bits[axes[0]] * 2 + bits[axes[1]]) * 2 + bits[axes[2]]) * n
            blocks.append((number * size, size, tile, inner))
        return blocks

    def up_product(layer_no):
        hidden_swaps[layer_no].arrive()
        if layer_no == last_layer:
            gg_swap.arrive()
        else:
            ready(layer_no, NORMED2)
        size = width // 8
        for z1 in range(2):
            for part in range(2):
                columns = pl.ds(3 * LANES * part, 3 * LANES)
                product = columns_by_columns(
                    held[NORMED2][0], grad_hidden[place.z0, z1, :, columns]
                ) + columns_by_columns(held[NORMED2][1], far_hidden[layer_no, z1, :, columns])
                put(
                    layer_no,
                    UP,
                    product,
                    lambda tile, inner, i: (tile + z1, inner + size * i),
                    blocks_of(HALVING[UP], 2, 3 * size * part),
                )
        reductions[layer_no, UP].start()
        if layer_no == last_layer:
            gg_swap.drain()
        hidden_swaps[layer_no].drain()
        if layer_no > 0:
            load(layer_no - 1, NORMED2)

    def proj_product(layer_no):
        middle_swaps[layer_no].arrive()
        if layer_no == last_layer:
            obb_swap.arrive()
        product = columns_by_columns(held[MIXED][0], grad_middle[place.z0]) + columns_by_columns(
            held[MIXED][1], far_middle[layer_no]
        )
        put(layer_no, PROJ, product, lambda tile, inner, i: (tile + i, 0), blocks_of(HALVING[PROJ], 3, 0))
        reductions[layer_no, PROJ].start()
        middle_swaps[layer_no].drain()
        if layer_no == last_layer:
            obb_swap.drain()
        if layer_no > 0:
            load(layer_no - 1, MIXED)

    def qkv_product(layer_no):
        qkv_swaps[layer_no].arrive()
        ready(layer_no, NORMED)
        size = width // 8
        for number in range(3):
            product = columns_by_columns(held[NORMED][0], half_qkv[place.z0, number]) + columns_by_columns(
                held[NORMED][1], far_qkv[layer_no, number]
            )
            put(
                layer_no,
                QKV,
                product,
                lambda tile, inner, i: (tile + i, inner),
                blocks_of(HALVING[QKV], 3, size * number),
            )
        if layer_no > 0:
            load(layer_no - 1, NORMED)
        reductions[layer_no, QKV].start()
        qkv_swaps[layer_no].drain()

    def finish(layer_no, name):
        red = reductions[layer_no, name]
        size = width // 8
        if name == DOWN:
            red.finish(narrow_writer(place, grad_down, layer_no, half, 0))
        elif name == PROJ:
            red.finish(narrow_writer(place, grad_proj, layer_no, size, 0))
        elif name == UP:

            def write(i, tile):
                for part in range(tile.shape[0] // size):
                    grad_up[layer_no, :, tile_of(part)] = tile[size * part : size * part + size]

            red.finish(write)
        else:

            def write(i, tile):
                for part, ref in enumerate((grad_query, grad_key, grad_value)):
                    narrow_writer(place, ref, layer_no, size, size * part)(i, tile)

            red.finish(write)

    def step(layer_no, name, stage):
        reductions[layer_no, name].step(stage)

    top, low = last_layer, last_layer - 1
    ready(top, QUERIES)
    query_gather.start()
    carried[...] = cotangent[...].astype(F32)
    error = send_error(top, carried[...])
    acts_swap.start()
    feed_forward(top, error)
    deltas = project_back(top)
    obb_swap.start()
    ready(top, NORMED2)
    gg_swap.start()
    out_return.start()
    own_queries(top, deltas)
    query_gather.near()
    query_gather.far()
    query_gather.last()
    do_gathers[top].near()
    do_gathers[top].far()
    down_product(top)
    do_gathers[top].last()
    own_keys(top)
    attention_inputs_back(top)
    query_gather.drain()
    load(low, QUERIES)
    input_back(top)
    error = send_error(low, carried[...])
    step(top, DOWN, 0)
    proj_product(top)
    up_product(top)
    feed_forward(low, error)
    deltas = project_back(low)
    step(top, PROJ, 0)
    step(top, UP, 0)
    qkv_product(top)
    ready(low, QUERIES)
    own_queries(low, deltas)
    step(top, QKV, 0)
    down_product(low)
    do_gathers[low].near()
    do_gathers[low].far()
    step(top, DOWN, 1)
    do_gathers[low].last()
    own_keys(low)
    step(top, PROJ, 1)
    step(low, DOWN, 0)
    attention_inputs_back(low)
    input_back(low)
    doubling.start()
    grad_return.start()
    proj_product(low)
    step(top, UP, 1)
    up_product(low)
    step(low, PROJ, 0)
    step(top, QKV, 1)
    step(top, DOWN, 2)
    doubling.step(0)
    step(low, UP, 0)
    qkv_product(low)
    step(low, DOWN, 1)
    step(top, PROJ, 2)
    step(low, QKV, 0)
    doubling.step(1)
    step(low, PROJ, 1)
    step(top, UP, 2)
    step(top, QKV, 2)
    finish(top, DOWN)
    doubling.step(2)
    step(low, UP, 1)
    step(low, DOWN, 2)
    step(low, PROJ, 2)
    finish(top, PROJ)
    finish(top, UP)
    doubling.step(3)
    step(low, QKV, 1)
    finish(top, QKV)
    finish(low, DOWN)
    finish(low, PROJ)
    doubling.step(4)
    step(low, UP, 2)
    step(low, QKV, 2)
    grad_small[...] = sums[len(Doubling.AXES)]
    finish(low, UP)
    finish(low, QKV)
    out_return.wait()
    grad_return.wait()
    for red in reductions.values():
        red.drain()
    for layer_no in range(layers):
        do_gathers[layer_no].drain()
        error_swaps[layer_no].drain()
    acts_swap.drain()


def backward_call(out, cotangent, marks, norms, whole, saved):
    layers = norms.shape[0]
    rows, width = out.shape
    hidden = whole[4].shape[2]
    shapes = saved_shapes(layers, rows, width, hidden)
    sem = pltpu.SemaphoreType.DMA
    any_spec, vmem_spec = pl.BlockSpec(memory_space=pl.ANY), pl.BlockSpec(memory_space=pltpu.VMEM)
    size, quarter = width // 8, width // 4
    plans = tile_plan(width, hidden)
    held = []
    for name in SAVED:
        shape, dtype = shapes[name]
        held.append(pltpu.VMEM(shape[2:] if name == ACTS else shape[1:], dtype))
    tensors = [plans[name] for name in TENSORS] * layers
    outs = (
        [jax.ShapeDtypeStruct((rows, width), BF16), jax.ShapeDtypeStruct((rows, width), F32)]
        + [jax.ShapeDtypeStruct((layers, size, quarter), F32)] * 4
        + [
            jax.ShapeDtypeStruct((layers, size, hidden // 4), F32),
            jax.ShapeDtypeStruct((layers, hidden // 8, quarter), F32),
            jax.ShapeDtypeStruct((8 * layers, width), F32),
        ]
    )
    return pl.pallas_call(
        lambda *refs: backward_kernel(layers, *refs),
        out_shape=outs,
        in_specs=[any_spec, vmem_spec, vmem_spec, vmem_spec] + [any_spec] * (6 + len(SAVED)),
        out_specs=[any_spec, any_spec] + [vmem_spec] * 7,
        scratch_shapes=held
        + [pltpu.VMEM((8 * n, count, LANES), BF16) for n, count in tensors]
        + [pltpu.VMEM((landing_count(n), count, LANES), BF16) for n, count in tensors]
        + [
            pltpu.VMEM((width, 3 * width), BF16),
            pltpu.VMEM((width, width), BF16),
            pltpu.VMEM((width, hidden), BF16),
            pltpu.VMEM((hidden, width), BF16),
            sem((6,)),
            sem((len(SAVED),)),
            sem((2, 3)),
            pltpu.VMEM((layers, 4, rows, width + LANES), BF16),
            sem((layers, 4)),
            sem((layers, 4)),
            sem((4,)),
            sem((4,)),
            sem((layers, 7, 2)),
            sem((4 * layers, 4)),
            sem((4 * layers, 4)),
            pltpu.VMEM((layers, 2, rows, width), BF16),
            pltpu.VMEM((2, 2, rows, width), BF16),
            pltpu.VMEM((layers, 2, rows, width), BF16),
            pltpu.VMEM((2, rows, width // 2), BF16),
            pltpu.VMEM((layers, rows, width // 2), BF16),
            pltpu.VMEM((rows, 3 * width), BF16),
            pltpu.VMEM((2, 3, rows, width // 2), BF16),
            pltpu.VMEM((layers, 3, rows, width // 2), BF16),
            pltpu.VMEM((rows, width), F32),
            pltpu.VMEM((rows, width), F32),
            pltpu.VMEM((rows, width), F32),
            pltpu.VMEM((rows, width), F32),
            pltpu.VMEM((6, 8 * layers, width), F32),
            pltpu.VMEM((5, 8 * layers, width), F32),
            sem((5, 2)),
        ],
        compiler_params=pltpu.CompilerParams(
            collective_id=1, has_side_effects=True, vmem_limit_bytes=VMEM_BYTES
        ),
    )(out, cotangent, marks, norms, *whole, *saved)


def beyond_eight(result):
    dp_size = lax.axis_size(DP)
    groups = dp_size // 8
    if groups == 1:
        return result
    result = lax.psum(result, DP, axis_index_groups=[[g * 8 + i for g in range(groups)] for i in range(8)])
    whole = lax.all_gather(
        result, DP, axis=1, tiled=True, axis_index_groups=[[g * 8 + i for i in range(8)] for g in range(groups)]
    )
    rows = whole.shape[1] // dp_size
    return lax.dynamic_slice_in_dim(whole, lax.axis_index(DP) * rows, rows, axis=1)


def shards(
    patches,
    keep,
    coords,
    query_w,
    key_w,
    value_w,
    proj_w,
    up_w,
    down_w,
    norm1_gain,
    norm1_bias,
    norm2_gain,
    norm2_bias,
    freqs,
    cotangent,
):
    images, rows, width = patches.shape
    layers = query_w.shape[0]
    parts = lax.axis_size(BLK)
    whole = (query_w, key_w, value_w, proj_w, up_w, down_w)
    bias = jnp.where(keep[0] > 0, 0.0, MASKED_SCORE)
    marks = jnp.stack([bias, coords[0, 0].astype(F32), coords[1, 0].astype(F32)], axis=1)
    marks = jnp.pad(marks, ((0, 0), (0, LANES - 3))).astype(BF16)
    norms = jnp.stack([norm1_gain, norm1_bias, norm2_gain, norm2_bias], axis=1)
    both = jnp.concatenate([freqs, freqs], axis=-1).reshape(layers, 2, width)
    out, far_cotangent, marks, *saved = forward_call(
        jnp.concatenate([patches[0], marks], axis=1), cotangent[0], norms, both, whole
    )
    output, grad_patches, *large, small = backward_call(out, far_cotangent, marks, norms, whole, saved)
    large = [beyond_eight(grad) for grad in large]
    groups = lax.axis_size(DP) // 8
    if groups > 1:
        small = lax.psum(small, DP, axis_index_groups=[[g * 8 + i for g in range(groups)] for i in range(8)])
    small = small.reshape(layers, 8, width)
    at = lax.axis_index(BLK)
    mine = lax.dynamic_slice_in_dim(small[:, :4], at * (width // parts), width // parts, axis=2)
    pairs = small[:, 4:6].reshape(layers, 2, freqs.shape[2], 2, freqs.shape[3])
    heads = freqs.shape[2] // parts
    grad_freqs = lax.dynamic_slice_in_dim(pairs[:, :, :, 1] - pairs[:, :, :, 0], at * heads, heads, axis=2)
    return (output[None], grad_patches[None], *large, mine[:, 0], mine[:, 1], mine[:, 2], mine[:, 3], grad_freqs)


def solution(mesh):
    block = P(DP, BLK, None)
    placed = (block, P(DP, BLK), P(None, DP, BLK)) + (P(),) * 11 + (block,)
    results = (block, block) + (P(None, DP, BLK),) * 6 + (P(None, BLK),) * 4 + (P(None, None, BLK, None),)
    return jax.shard_map(shards, mesh=mesh, in_specs=placed, out_specs=results, check_vma=False)
```

```python
import jax
import jax.numpy as jnp
from jax import lax
from jax.experimental import pallas as pl
from jax.experimental.pallas import tpu as pltpu
from jax.sharding import PartitionSpec as P

MESH = pl.DeviceIdType.MESH
DP, BLK = "dp", "blk"
C, X, Y, Z0, Z1 = range(5)
BF16, F32 = jnp.bfloat16, jnp.float32
MASKED_SCORE = -1e30
NORM_EPSILON = 1e-06
LANES = 128
VMEM_BYTES = 63 * 1024 * 1024


def rows_by_columns(left, right):
    return lax.dot_general(left, right, (((1,), (0,)), ((), ())), preferred_element_type=F32)


def rows_by_rows(left, right):
    return lax.dot_general(left, right, (((1,), (1,)), ((), ())), preferred_element_type=F32)


def columns_by_columns(left, right):
    return lax.dot_general(left, right, (((0,), (0,)), ((), ())), preferred_element_type=F32)


class Place:
    def __init__(self):
        self.dp = lax.axis_index(DP)
        self.blk = lax.axis_index(BLK)
        self.c = lax.rem(self.dp, 2)
        self.x = lax.rem(self.dp // 2, 2)
        self.y = lax.rem(self.dp // 4, 2)
        self.z0 = lax.rem(self.blk, 2)
        self.z1 = lax.rem(self.blk // 2, 2)
        self.bits = (self.c, self.x, self.y, self.z0, self.z1)
        self.worker = (self.dp - self.c + self.z0, 2 * self.c + self.z1)
        self.owner = (self.dp - self.c + self.z1, 2 * self.z0 + self.c)
        self.stays = (self.worker[0] == self.dp) & (self.worker[1] == self.blk)

    def other(self, axis):
        if axis <= Y:
            return (self.dp + (1 << axis) * (1 - 2 * self.bits[axis]), self.blk)
        return (self.dp, self.blk + (1 << axis - Z0) * (1 - 2 * self.bits[axis]))

    def greet(self, axes):
        barrier = pltpu.get_barrier_semaphore()
        mine = 2 * self.blk + self.c
        for step in range(1, 8):
            them = lax.rem(mine + step, 8)
            pl.semaphore_signal(
                barrier, inc=1, device_id=(self.dp - self.c + lax.rem(them, 2), them // 2), device_id_type=MESH
            )
        for axis in axes:
            pl.semaphore_signal(barrier, inc=1, device_id=self.other(axis), device_id_type=MESH)
        pl.semaphore_wait(barrier, 7 + len(axes))


class Relocation:
    def __init__(self, place, source, target, sems, back=False):
        self.place, self.source, self.target, self.sems = place, source, target, sems
        self.device = place.owner if back else place.worker

    def remote(self):
        return pltpu.make_async_remote_copy(
            src_ref=self.source,
            dst_ref=self.target,
            send_sem=self.sems.at[0],
            recv_sem=self.sems.at[1],
            device_id=self.device,
            device_id_type=MESH,
        )

    def local(self):
        return pltpu.make_async_copy(self.source, self.target, self.sems.at[2])

    def start(self):
        pl.when(self.place.stays)(lambda: self.local().start())
        pl.when(jnp.logical_not(self.place.stays))(lambda: self.remote().start())

    def wait(self):
        pl.when(self.place.stays)(lambda: self.local().wait())
        pl.when(jnp.logical_not(self.place.stays))(lambda: self.remote().wait())


class Gather:
    def __init__(self, place, slots, sends, receives):
        self.place, self.slots, self.sends, self.receives = place, slots, sends, receives

    def copy(self, source, slot, axis):
        return pltpu.make_async_remote_copy(
            src_ref=self.slots.at[source],
            dst_ref=self.slots.at[slot],
            send_sem=self.sends.at[slot],
            recv_sem=self.receives.at[slot],
            device_id=self.place.other(axis),
            device_id_type=MESH,
        )

    def start(self):
        self.copy(0, 2, Z0).start()
        self.copy(0, 1, C).start()

    def near(self):
        self.copy(0, 1, C).wait_recv()

    def far(self):
        self.copy(0, 2, Z0).wait_recv()
        self.copy(2, 3, C).start()

    def last(self):
        self.copy(2, 3, C).wait_recv()

    def drain(self):
        self.copy(0, 1, C).wait_send()
        self.copy(0, 2, Z0).wait_send()
        self.copy(2, 3, C).wait_send()


class Swap:
    def __init__(self, place, axis, source, target, sems):
        self.place, self.axis, self.source, self.target, self.sems = place, axis, source, target, sems

    def copy(self):
        return pltpu.make_async_remote_copy(
            src_ref=self.source,
            dst_ref=self.target,
            send_sem=self.sems.at[0],
            recv_sem=self.sems.at[1],
            device_id=self.place.other(self.axis),
            device_id_type=MESH,
        )

    def start(self):
        self.copy().start()

    def arrive(self):
        self.copy().wait_recv()

    def drain(self):
        self.copy().wait_send()


def lane_index(rows):
    return lax.broadcasted_iota(jnp.int32, (rows, LANES), 1)


def partner_tile(tile, former):
    return jnp.where(former, pltpu.roll(tile, 96, 1), pltpu.roll(tile, 32, 1))


def rotate_tile(tile, cosine, signed_sine, former):
    return tile * cosine + partner_tile(tile, former) * signed_sine


def tile_of(index):
    return slice(LANES * index, LANES * index + LANES)


def normalise(values):
    centre = values - jnp.mean(values, axis=-1, keepdims=True)
    spread = jnp.mean(centre * centre, axis=-1, keepdims=True)
    scale = lax.rsqrt(spread + NORM_EPSILON)
    return centre * scale, scale


QUERY_W, KEY_W, VALUE_W, PROJ_W, UP_W, DOWN_W = range(6)


class Weights:
    def __init__(self, whole, qkv, proj, up, down, sems):
        width = qkv.shape[1] // 3
        self.whole, self.sems = whole, sems
        self.buffers = [qkv.at[:, pl.ds(part * width, width)] for part in range(3)] + [proj, up, down]

    def copy(self, name, layer_no):
        return pltpu.make_async_copy(self.whole[name].at[layer_no], self.buffers[name], self.sems.at[name])

    def load(self, layer_no, *names):
        for name in names:
            self.copy(name, layer_no).start()

    def ready(self, layer_no, *names):
        for name in names:
            self.copy(name, layer_no).wait()


SAVED = range(14)
NORMED, KEYS, VALUES, QUERIES, MIXED, NORMED2, ACTS, FAR_ACTS = range(8)
SLOPES, HAT1, HAT2, SCALES, LOGS, ANGLES = range(8, 14)


def saved_shapes(layers, rows, width, hidden):
    heads_part = hidden // 8
    return {
        NORMED: ((layers, 2, rows, width), BF16),
        KEYS: ((layers, 4, rows, width), BF16),
        VALUES: ((layers, 4, rows, width), BF16),
        QUERIES: ((layers, 4, rows, width + LANES), BF16),
        MIXED: ((layers, 2, rows, width), BF16),
        NORMED2: ((layers, 2, rows, width), BF16),
        ACTS: ((layers, 2, 4, rows, heads_part), BF16),
        FAR_ACTS: ((layers, 4, rows, heads_part), BF16),
        SLOPES: ((layers, rows, hidden), BF16),
        HAT1: ((layers, rows, width), BF16),
        HAT2: ((layers, rows, width), BF16),
        SCALES: ((layers, rows, LANES), F32),
        LOGS: ((layers, rows, LANES), F32),
        ANGLES: ((layers, 2, rows, width), F32),
    }


def forward_kernel(layers, *refs):
    patches, cotangent, keep, coords, gain1, bias1, gain2, bias2, freqs = refs[:9]
    whole = refs[9:15]
    out, far_cotangent, marks = refs[15:18]
    saved = refs[18 : 18 + len(SAVED)]
    refs = refs[18 + len(SAVED) :]
    kept = refs[: len(SAVED)]
    refs = refs[len(SAVED) :]
    (qkv_w, proj_w, up_w, down_w, w_sems, start, start_sems, own_marks, mark_sems, cot_sems) = refs[:10]
    (aux, aux_sends, aux_receives, normed, h_sends, h_receives, q_sends, q_receives, swap_sems) = refs[10:19]
    (cosine, sine, residual, result, save_sems) = refs[19:]
    place = Place()
    rows, width = residual.shape
    hidden = up_w.shape[1]
    pairs = width // LANES
    weights = Weights(whole, qkv_w, proj_w, up_w, down_w, w_sems)
    weights.load(0, KEY_W, VALUE_W, QUERY_W, PROJ_W, UP_W, DOWN_W)
    line = lax.broadcasted_iota(jnp.int32, (LANES, rows), 0)
    own = jnp.where(line == 0, jnp.where(keep[...] > 0, 0.0, MASKED_SCORE), 0.0)
    for number in range(2):
        own = jnp.where(line == 1 + number, coords[number].astype(F32), own)
    own_marks[...] = own.T.astype(BF16)
    place.greet((X,))
    mark_arrival = Relocation(place, own_marks, aux.at[0], mark_sems)
    mark_arrival.start()
    arrival = Relocation(place, patches, start, start_sems)
    arrival.start()
    other_arrival = Relocation(place, cotangent, far_cotangent, cot_sems)
    mark_arrival.wait()
    aux_gather = Gather(place, aux, aux_sends, aux_receives)
    aux_gather.start()
    arrival.wait()
    residual[...] = start[...].astype(F32)
    lane = lane_index(rows)
    former = lax.rem(lane, 64) < 32
    first_head = lane < 64
    one_lane = jnp.where(lane == 0, 1.0, 0.0).astype(BF16)
    pending = []

    def save(name, layer_no, source=None, target=None):
        source = kept[name].at[layer_no] if source is None else source
        target = saved[name].at[layer_no] if target is None else target
        copy = pltpu.make_async_copy(source, target, save_sems.at[len(pending)])
        copy.start()
        pending.append(copy)

    def freq_tile(layer_no, which, index):
        pair = [freqs[layer_no, 2 * index + member, which : which + 1] for member in range(2)]
        return jnp.concatenate([pair[0]] * 2 + [pair[1]] * 2, axis=1)

    def make_angles(layer_no, slot):
        rows_at = aux[slot][:, 1:2].astype(F32)
        columns_at = aux[slot][:, 2:3].astype(F32)
        for index in range(pairs):
            sl = tile_of(index)
            angle = rows_at * freq_tile(layer_no, 0, index) + columns_at * freq_tile(layer_no, 1, index)
            cosine[slot, :, sl] = jnp.cos(angle)
            sine[slot, :, sl] = jnp.where(former, -1.0, 1.0) * jnp.sin(angle)

    def rotated(values, slot, index):
        return rotate_tile(values, cosine[slot, :, tile_of(index)], sine[slot, :, tile_of(index)], former)

    def project(layer_no, slot):
        products = rows_by_columns(normed[layer_no, slot], qkv_w[...])
        for index in range(pairs):
            turned = rotated(products[:, tile_of(index)], slot, index)
            kept[QUERIES][layer_no, slot, :, tile_of(index)] = (0.125 * turned).astype(BF16)
        products = products[:, width:]
        for index in range(pairs):
            turned = rotated(products[:, tile_of(index)], slot, index)
            kept[KEYS][layer_no, slot, :, tile_of(index)] = turned.astype(BF16)
        kept[VALUES][layer_no, slot] = products[:, width:].astype(BF16)

    gathers, log_gathers, swaps, deferred = [aux_gather], [], [], []
    for layer_no in range(layers):
        hat, scale = normalise(residual[...])
        kept[HAT1][layer_no] = hat.astype(BF16)
        normed[layer_no, 0] = (hat * gain1[layer_no : layer_no + 1] + bias1[layer_no : layer_no + 1]).astype(BF16)
        gather = Gather(place, normed.at[layer_no], h_sends.at[layer_no], h_receives.at[layer_no])
        gather.start()
        gathers.append(gather)
        for later in deferred:
            later.start()
        deferred.clear()
        save(HAT1, layer_no)
        make_angles(layer_no, 0)
        weights.ready(layer_no, KEY_W, VALUE_W, QUERY_W)
        project(layer_no, 0)
        if layer_no == 0:
            aux_gather.near()
            aux_gather.far()
        make_angles(layer_no, 1)
        gather.near()
        project(layer_no, 1)
        make_angles(layer_no, 2)
        if layer_no == 0:
            aux_gather.last()
        make_angles(layer_no, 3)
        gather.far()
        project(layer_no, 2)
        gather.last()
        project(layer_no, 3)
        if layer_no + 1 < layers:
            weights.load(layer_no + 1, KEY_W, VALUE_W, QUERY_W)
        save(NORMED, layer_no, normed.at[layer_no, 0], saved[NORMED].at[layer_no, 0])
        save(NORMED, layer_no, normed.at[layer_no, 2], saved[NORMED].at[layer_no, 1])
        save(KEYS, layer_no)
        save(VALUES, layer_no)
        if layer_no + 1 == layers:
            queries = pl.ds(0, width)
            save(
                QUERIES,
                layer_no,
                kept[QUERIES].at[layer_no, :, :, queries],
                saved[QUERIES].at[layer_no, :, :, queries],
            )
        kept[ANGLES][layer_no, 0] = cosine[0]
        kept[ANGLES][layer_no, 1] = sine[0]
        save(ANGLES, layer_no)
        marks_of_keys = aux[...].reshape(4 * rows, LANES)
        logs = jnp.zeros((rows, LANES), F32)
        for index in range(pairs):
            sl = tile_of(index)
            query_pair = kept[QUERIES][layer_no, 0, :, sl]
            key_pair = kept[KEYS][layer_no, :, :, sl].reshape(4 * rows, LANES)
            value_pair = kept[VALUES][layer_no, :, :, sl].reshape(4 * rows, LANES)
            extended = jnp.concatenate([key_pair, marks_of_keys], axis=1)
            mixed = []
            for member in range(2):
                mine = first_head if member == 0 else jnp.logical_not(first_head)
                query = jnp.where(mine, query_pair, jnp.zeros_like(query_pair))
                scores = rows_by_rows(jnp.concatenate([query, one_lane], axis=1), extended)
                highest = jnp.max(scores, axis=1, keepdims=True)
                weight = jnp.exp(scores - highest)
                total = jnp.sum(weight, axis=1, keepdims=True)
                mixed.append(rows_by_columns(weight.astype(BF16), value_pair) / total)
                logs = jnp.where(lane == 2 * index + member, highest + jnp.log(total), logs)
            kept[MIXED][layer_no, 0, :, sl] = jnp.where(first_head, mixed[0], mixed[1]).astype(BF16)
        kept[LOGS][layer_no] = logs
        save(LOGS, layer_no)
        attended_swap = Swap(
            place, Z0, kept[MIXED].at[layer_no, 0], kept[MIXED].at[layer_no, 1], swap_sems.at[layer_no, 0]
        )
        if layer_no + 1 < layers:
            extras = kept[QUERIES].at[layer_no, :, :, pl.ds(width, LANES)]
            extras[0] = spread_lanes(-logs, lane, 1.0).astype(BF16)
            log_gather = Gather(place, extras, q_sends.at[layer_no], q_receives.at[layer_no])
            log_gathers.append(log_gather)
            swaps.append(attended_swap)
            deferred += [log_gather, attended_swap]
        weights.ready(layer_no, PROJ_W)
        middle = residual[...] + rows_by_columns(kept[MIXED][layer_no, 0], proj_w[...])
        if layer_no + 1 < layers:
            weights.load(layer_no + 1, PROJ_W)
        hat, scale_two = normalise(middle)
        kept[HAT2][layer_no] = hat.astype(BF16)
        save(HAT2, layer_no)
        kept[SCALES][layer_no] = jnp.where(lane == 0, scale, scale_two)
        save(SCALES, layer_no)
        kept[NORMED2][layer_no, 0] = (hat * gain2[layer_no : layer_no + 1] + bias2[layer_no : layer_no + 1]).astype(BF16)
        normed_swap = Swap(
            place, Z0, kept[NORMED2].at[layer_no, 0], kept[NORMED2].at[layer_no, 1], swap_sems.at[layer_no, 1]
        )
        if layer_no + 1 < layers:
            swaps.append(normed_swap)
            deferred += [normed_swap, other_arrival]
        residual[...] = middle
        weights.ready(layer_no, UP_W)
        half = hidden // 8
        for quarter in range(4):
            columns = slice(2 * half * quarter, 2 * half * quarter + 2 * half)
            hidden_part = rows_by_columns(kept[NORMED2][layer_no, 0], up_w[:, columns])
            share = 0.5 + 0.5 * lax.erf(hidden_part * 0.7071067811865476)
            active = (hidden_part * share).astype(BF16)
            slope = share + hidden_part * (0.3989422804014327 * jnp.exp(-0.5 * hidden_part * hidden_part))
            kept[SLOPES][layer_no, :, columns] = slope.astype(BF16)
            y, x = quarter // 2, quarter % 2
            kept[ACTS][layer_no, x, 2 * y] = active[:, :half]
            kept[ACTS][layer_no, x, 2 * y + 1] = active[:, half:]
            if quarter == 0:
                weights.ready(layer_no, DOWN_W)
            residual[...] += rows_by_columns(active, down_w[columns, :])
        if layer_no + 1 < layers:
            weights.load(layer_no + 1, UP_W, DOWN_W)
        active_swap = Swap(
            place,
            X,
            kept[ACTS].at[layer_no, 1 - place.x],
            kept[FAR_ACTS].at[layer_no],
            swap_sems.at[layer_no, 2],
        )
        if layer_no + 1 < layers:
            active_swap.start()
            swaps.append(active_swap)
        save(SLOPES, layer_no)
        save(ACTS, layer_no)
        if layer_no + 1 == layers:
            for name in (MIXED, NORMED2):
                save(name, layer_no, kept[name].at[layer_no, 0], saved[name].at[layer_no, 0])
    result[...] = residual[...].astype(BF16)
    leave = pltpu.make_async_copy(result, out, save_sems.at[len(pending)])
    leave.start()
    pending.append(leave)
    leave = pltpu.make_async_copy(aux, marks, save_sems.at[len(pending)])
    leave.start()
    pending.append(leave)
    for gather in log_gathers:
        gather.near()
        gather.far()
        gather.last()
    for swap in swaps:
        swap.arrive()
    for name in (QUERIES, MIXED, NORMED2, FAR_ACTS):
        save(name, 0)
    other_arrival.wait()
    for gather in gathers + log_gathers:
        gather.drain()
    for swap in swaps:
        swap.drain()
    for copy in pending:
        copy.wait()


def spread_lanes(columns, lane, last):
    columns = jnp.where(lane < 16, columns, 0.0)
    high = columns.astype(BF16).astype(F32)
    middle = (columns - high).astype(BF16).astype(F32)
    low = columns - high - middle
    spread = high + pltpu.roll(middle, 16, 1) + pltpu.roll(low, 32, 1)
    return jnp.where(lane == 127, last, spread)


def forward_call(patches, cotangent, keep, coords, norms, freqs, whole):
    layers = freqs.shape[0]
    rows, width = patches.shape
    hidden = whole[4].shape[2]
    shapes = saved_shapes(layers, rows, width, hidden)
    sem = pltpu.SemaphoreType.DMA
    any_spec, vmem_spec = pl.BlockSpec(memory_space=pl.ANY), pl.BlockSpec(memory_space=pltpu.VMEM)
    outs = [
        jax.ShapeDtypeStruct((rows, width), BF16),
        jax.ShapeDtypeStruct((rows, width), BF16),
        jax.ShapeDtypeStruct((4, rows, LANES), BF16),
    ] + [jax.ShapeDtypeStruct(*shapes[name]) for name in SAVED]
    return pl.pallas_call(
        lambda *refs: forward_kernel(layers, *refs),
        out_shape=outs,
        in_specs=[any_spec, any_spec] + [vmem_spec] * 7 + [any_spec] * 6,
        out_specs=[any_spec] * len(outs),
        scratch_shapes=[pltpu.VMEM(*shapes[name]) for name in SAVED]
        + [
            pltpu.VMEM((width, 3 * width), BF16),
            pltpu.VMEM((width, width), BF16),
            pltpu.VMEM((width, hidden), BF16),
            pltpu.VMEM((hidden, width), BF16),
            sem((6,)),
            pltpu.VMEM((rows, width), BF16),
            sem((3,)),
            pltpu.VMEM((rows, LANES), BF16),
            sem((3,)),
            sem((3,)),
            pltpu.VMEM((4, rows, LANES), BF16),
            sem((4,)),
            sem((4,)),
            pltpu.VMEM((layers, 4, rows, width), BF16),
            sem((layers, 4)),
            sem((layers, 4)),
            sem((layers, 4)),
            sem((layers, 4)),
            sem((layers, 3, 2)),
            pltpu.VMEM((4, rows, width), F32),
            pltpu.VMEM((4, rows, width), F32),
            pltpu.VMEM((rows, width), F32),
            pltpu.VMEM((rows, width), BF16),
            sem((64,)),
        ],
        compiler_params=pltpu.CompilerParams(
            collective_id=0, has_side_effects=True, vmem_limit_bytes=VMEM_BYTES
        ),
    )(patches, cotangent, keep, coords, *norms, freqs, *whole)


class Reduction:
    def __init__(self, place, axes, n, share, landing, sends, receives):
        self.place, self.axes = place, axes + (Z1, Z1)
        self.share, self.landing, self.sends, self.receives = share, landing, sends, receives
        self.n, self.rows = n, share.shape[1]
        self.plan = []
        base, half, land = 0, 4 * n, 0
        for axis in axes:
            bit = place.bits[axis]
            self.plan.append((base + (1 - bit) * half, base + bit * half, half, land))
            base, land, half = base + bit * half, land + half, half // 2
        self.base, self.land = base, land
        self.plan.append((base + (n - 1) * (1 - place.z1), base + (n - 1) * place.z1, 1, land))

    def copy(self, stage):
        if stage < 4:
            send, _, count, land = self.plan[stage]
            source, target = self.share.at[pl.ds(send, count)], self.landing.at[pl.ds(land, count)]
        else:
            half = pl.ds(0, self.rows // 2)
            source, target = self.landing.at[0, half], self.landing.at[self.land + 1, half]
        return pltpu.make_async_remote_copy(
            src_ref=source,
            dst_ref=target,
            send_sem=self.sends.at[stage],
            recv_sem=self.receives.at[stage],
            device_id=self.place.other(self.axes[stage]),
            device_id_type=MESH,
        )

    def start(self, stage=0):
        self.copy(stage).start()

    def step(self, stage):
        _, keep, count, land = self.plan[stage]
        self.copy(stage).wait_recv()

        def body(i, carry):
            self.share[keep + i] = self.share[keep + i] + self.landing[land + i]
            return carry

        lax.fori_loop(0, count, body, 0)
        self.start(stage + 1)
        if stage == 2 and self.n == 3:
            half = self.rows // 2
            shared = self.share[self.base + 1].astype(F32)
            upper, lower = shared[:half], shared[half:]
            first = lane_index(half) < 64
            low_lanes = jnp.where(first, upper, pltpu.roll(lower, 64, 1))
            high_lanes = jnp.where(first, pltpu.roll(upper, 64, 1), lower)
            self.landing[0, :half] = jnp.where(self.place.z1 == 1, low_lanes, high_lanes).astype(BF16)
            self.start(4)

    def finish(self, write):
        self.copy(3).wait_recv()
        _, keep, _, land = self.plan[3]
        own = self.share[keep].astype(F32) + self.landing[land].astype(F32)
        if self.n == 2:
            write(own)
            return
        self.copy(4).wait_recv()
        half = self.rows // 2
        packed = self.landing[self.land + 1, :half].astype(F32)
        shared = self.share[self.base + 1].astype(F32)
        shared = jnp.where(self.place.z1 == 0, shared, pltpu.roll(shared, 64, 1))
        rest = shared + jnp.concatenate([packed, pltpu.roll(packed, 64, 1)], axis=0)
        write(own, rest[:, :64])

    def drain(self):
        for stage in range(4 if self.n == 2 else 5):
            self.copy(stage).wait_send()


class Doubling:
    AXES = (C, X, Y, Z0, Z1)

    def __init__(self, place, sums, landing, sems):
        self.place, self.sums, self.landing, self.sems = place, sums, landing, sems

    def copy(self, stage):
        return pltpu.make_async_remote_copy(
            src_ref=self.sums.at[stage],
            dst_ref=self.landing.at[stage],
            send_sem=self.sems.at[stage, 0],
            recv_sem=self.sems.at[stage, 1],
            device_id=self.place.other(self.AXES[stage]),
            device_id_type=MESH,
        )

    def start(self):
        self.copy(0).start()

    def step(self, stage):
        self.copy(stage).wait()
        self.sums[stage + 1] = self.sums[stage] + self.landing[stage]
        if stage + 1 < len(self.AXES):
            self.copy(stage + 1).start()


TENSORS = DOWN, UP, PROJ, QUERY, KEY, VALUE = range(6)
HALVING = ((C, Y, Z0), (C, X, Y), (C, X, Y), (C, Y, X), (C, X, Y), (C, Y, X))


def tile_plan(width, hidden):
    size = width // 8
    return ((3, hidden // 8), (2, size * (hidden // 4 // LANES))) + ((3, size),) * 4


def landing_count(n):
    return 4 * n + 2 * n + n + n - 1


def by_halves(tiles, first):
    def turned(tile):
        return pltpu.roll(tile, 64, 1)

    return (
        (tiles[0], jnp.where(first, tiles[1], turned(tiles[4])), tiles[3]),
        (
            jnp.where(first, turned(tiles[1]), turned(tiles[2])),
            jnp.where(first, turned(tiles[2]), tiles[5]),
            jnp.where(first, turned(tiles[4]), turned(tiles[5])),
        ),
    )


def backward_kernel(layers, *refs):
    out, cotangent, marks = refs[:3]
    gains = refs[3:5]
    whole = refs[5:11]
    saved = refs[11 : 11 + len(SAVED)]
    refs = refs[11 + len(SAVED) :]
    output, grad_patches, grad_up, grad_down, grad_proj, grad_query, grad_key, grad_value, grad_small = refs[:9]
    refs = refs[9:]
    held = refs[: len(SAVED)]
    refs = refs[len(SAVED) :]
    count = layers * len(TENSORS)
    shares, landings = refs[:count], refs[count : 2 * count]
    refs = refs[2 * count :]
    (qkv_w, proj_w, up_w, down_w, w_sems, load_sems, back_sems) = refs[:7]
    (douts, do_sends, do_receives, q_sends, q_receives, swap_sems, sends, receives) = refs[7:15]
    (errors, grad_hidden, far_hidden, grad_middle, far_middle, grad_qkv, half_qkv, far_qkv) = refs[15:23]
    (carried, returned, sums, sums_landing, sums_sems) = refs[23:]
    place = Place()
    rows, width = carried.shape
    hidden = up_w.shape[1]
    half = hidden // 8
    size = width // 8
    pairs = width // LANES
    top, low = layers - 1, layers - 2
    weights = Weights(whole, qkv_w, proj_w, up_w, down_w, w_sems)

    def loading(name, layer_no):
        source, target = saved[name].at[layer_no], held[name]
        if name == ACTS:
            source = source.at[place.x]
        if name == QUERIES and layer_no == top:
            source, target = source.at[:, :, pl.ds(0, width)], target.at[:, :, pl.ds(0, width)]
        if name in (MIXED, NORMED2) and layer_no == top:
            source, target = source.at[0], target.at[0]
        return pltpu.make_async_copy(source, target, load_sems.at[name])

    def load(layer_no, *names):
        for name in names:
            loading(name, layer_no).start()

    def ready(layer_no, *names):
        for name in names:
            loading(name, layer_no).wait()

    load(top, LOGS, MIXED, NORMED2)
    weights.load(top, DOWN_W)
    load(top, SLOPES)
    weights.load(top, UP_W)
    load(top, HAT2, SCALES)
    weights.load(top, PROJ_W)
    load(top, QUERIES, KEYS, VALUES, ANGLES, ACTS, HAT1, NORMED)
    weights.load(top, QUERY_W, KEY_W, VALUE_W)
    place.greet((X, Y))

    lane = lane_index(rows)
    former = lax.rem(lane, 64) < 32
    first_head = lane < 64
    heads_lanes = (first_head, jnp.logical_not(first_head))
    plans = tile_plan(width, hidden)
    reductions = {}
    for layer_no in range(layers):
        for name in TENSORS:
            at = layer_no * len(TENSORS) + name
            reductions[layer_no, name] = Reduction(
                place, HALVING[name], plans[name][0], shares[at], landings[at], sends.at[at], receives.at[at]
            )
    doubling = Doubling(place, sums, sums_landing, sums_sems)
    sums[0] = jnp.zeros(sums.shape[1:], F32)

    def swap(layer_no, number, axis, source, target):
        return Swap(place, axis, source, target, swap_sems.at[layer_no, number])

    away = 1 - place.z0
    error_swaps = [swap(l, 0, X, errors.at[l, 0], errors.at[l, 1]) for l in range(layers)]
    hidden_swaps = [swap(l, 1, Z0, grad_hidden.at[l, away], far_hidden.at[l]) for l in range(layers)]
    middle_swaps = [swap(l, 2, Z0, grad_middle.at[away], far_middle.at[l]) for l in range(layers)]
    qkv_swaps = [
        [swap(l, 3 + part, Z0, half_qkv.at[part, away], far_qkv.at[l, part]) for part in range(3)] for l in range(layers)
    ]
    mixed_swap = swap(top, 6, Z0, held[MIXED].at[0], held[MIXED].at[1])
    normed_swap = swap(top, 7, Z0, held[NORMED2].at[0], held[NORMED2].at[1])
    acts_swap = swap(top, 8, X, saved[ACTS].at[top, 1 - place.x], held[FAR_ACTS])
    extras = held[QUERIES].at[:, :, pl.ds(width, LANES)]
    log_gather = Gather(place, extras, q_sends, q_receives)
    do_gathers = [Gather(place, douts.at[l], do_sends.at[l], do_receives.at[l]) for l in range(layers)]
    out_return = Relocation(place, out, output, back_sems.at[0], back=True)
    grad_return = Relocation(place, returned, grad_patches, back_sems.at[1], back=True)

    def note(layer_no, row, values):
        sums[0, 8 * layer_no + row : 8 * layer_no + row + 1] = jnp.sum(values, axis=0, keepdims=True)

    def norm_back(layer_no, number, grad, hat, scale):
        note(layer_no, 2 * number, grad * hat)
        note(layer_no, 2 * number + 1, grad)
        grad = grad * gains[number][layer_no : layer_no + 1]
        mean = jnp.mean(grad, axis=-1, keepdims=True)
        slope = jnp.mean(grad * hat, axis=-1, keepdims=True)
        return scale * (grad - mean - hat * slope)

    def halves_of(values):
        return by_halves([values[:, tile_of(i)] for i in range(pairs)], first_head)

    def send_error(layer_no):
        for z0, tiles in enumerate(halves_of(carried[...])):
            for i, tile in enumerate(tiles):
                errors[layer_no, 0, :, tile_of(3 * z0 + i)] = tile.astype(BF16)
        error_swaps[layer_no].start()

    def quarter_of(quarter):
        return slice(2 * half * quarter, 2 * half * quarter + 2 * half)

    def hidden_back(layer_no):
        error = carried[...].astype(BF16)
        weights.ready(layer_no, DOWN_W)
        ready(layer_no, SLOPES)
        for quarter in range(4):
            grad = rows_by_rows(error, down_w[quarter_of(quarter), :])
            grad = grad * held[SLOPES][:, quarter_of(quarter)].astype(F32)
            grad_hidden[layer_no, quarter % 2, quarter // 2] = grad.astype(BF16)
        if layer_no > 0:
            weights.load(layer_no - 1, DOWN_W)
            load(layer_no - 1, SLOPES)

    def middle_back(layer_no):
        weights.ready(layer_no, UP_W)
        total = jnp.zeros((rows, width), F32)
        for quarter in range(4):
            total = total + rows_by_rows(grad_hidden[layer_no, quarter % 2, quarter // 2], up_w[:, quarter_of(quarter)])
        if layer_no > 0:
            weights.load(layer_no - 1, UP_W)
        ready(layer_no, HAT2, SCALES)
        hat = held[HAT2][...].astype(F32)
        carried[...] += norm_back(layer_no, 1, total, hat, held[SCALES][:, 1:2])
        if layer_no > 0:
            load(layer_no - 1, HAT2)

    def project_back(layer_no):
        weights.ready(layer_no, PROJ_W)
        grad = rows_by_rows(carried[...].astype(BF16), proj_w[...])
        if layer_no > 0:
            weights.load(layer_no - 1, PROJ_W)
        if layer_no < top:
            ready(layer_no, MIXED)
        deltas = jnp.zeros((rows, LANES), F32)
        for index in range(pairs):
            sl = tile_of(index)
            low_grad = grad[:, sl].astype(BF16)
            douts[layer_no, 0, :, sl] = low_grad
            product = low_grad.astype(F32) * held[MIXED][0, :, sl].astype(F32)
            for member, mine in enumerate(heads_lanes):
                delta = jnp.sum(jnp.where(mine, product, 0.0), axis=1, keepdims=True)
                deltas = jnp.where(lane == 2 * index + member, delta, deltas)
        douts[layer_no, 0, :, width:] = spread_lanes(-deltas, lane, 0.0).astype(BF16)
        do_gathers[layer_no].start()
        kept_deltas.append(deltas)

    kept_deltas = []

    def middle_send(layer_no):
        for z0, tiles in enumerate(halves_of(carried[...])):
            for i, tile in enumerate(tiles):
                grad_middle[z0, :, tile_of(i)] = tile.astype(BF16)
        middle_swaps[layer_no].start()

    def turned_back(layer_no, part, index, grad, forward):
        sl = tile_of(index)
        back = grad * held[ANGLES][0, :, sl] - partner_tile(grad, former) * held[ANGLES][1, :, sl]
        grad_qkv[:, part * width + LANES * index : part * width + LANES * index + LANES] = back.astype(BF16)
        return back, grad * partner_tile(forward.astype(F32), former)

    def note_turn(layer_no, index, turn, first):
        for row in range(2):
            at = 8 * layer_no + 4 + row
            total = jnp.sum(turn * marks[0][:, 1 + row : 2 + row].astype(F32), axis=0, keepdims=True)
            if not first:
                total = total + sums[0, at : at + 1, tile_of(index)]
            sums[0, at : at + 1, tile_of(index)] = total

    def split_half(part, tiles):
        for z0, group in enumerate(by_halves(tiles, first_head)):
            for i, tile in enumerate(group):
                half_qkv[part, z0, :, tile_of(i)] = tile.astype(BF16)

    def own_queries(layer_no):
        ready(layer_no, KEYS, VALUES, ANGLES, QUERIES)
        if layer_no < top:
            ready(layer_no, LOGS)
        deltas = kept_deltas[-1]
        one_lane = jnp.where(lane == 0, 1.0, 0.0).astype(BF16)
        key_marks = marks[...].reshape(4 * rows, LANES)
        backs = []
        for index in range(pairs):
            sl = tile_of(index)
            query_pair = held[QUERIES][0, :, sl]
            key_pair = held[KEYS][:, :, sl].reshape(4 * rows, LANES)
            value_pair = held[VALUES][:, :, sl].reshape(4 * rows, LANES)
            grad_pair = douts[layer_no, 0, :, sl]
            extended = jnp.concatenate([key_pair, key_marks], axis=1)
            parts = []
            for member, mine in enumerate(heads_lanes):
                head = 2 * index + member
                zero = jnp.zeros_like(query_pair)
                scores = rows_by_rows(
                    jnp.concatenate([jnp.where(mine, query_pair, zero), one_lane], axis=1), extended
                )
                weight = jnp.exp(scores - held[LOGS][:, head : head + 1])
                grad = rows_by_rows(jnp.where(mine, grad_pair, zero), value_pair)
                grad = (weight * (grad - deltas[:, head : head + 1])).astype(BF16)
                parts.append(rows_by_columns(grad, key_pair))
            grad = 0.125 * jnp.where(first_head, parts[0], parts[1])
            back, turn = turned_back(layer_no, 0, index, grad, 8.0 * query_pair.astype(F32))
            note_turn(layer_no, index, turn, True)
            backs.append(back)
        split_half(0, backs)

    def own_keys(layer_no):
        do_gathers[layer_no].near()
        do_gathers[layer_no].last()
        if layer_no == top:
            log_gather.near()
            log_gather.last()
        own_marks = marks[0]
        key_backs, value_backs = [], []
        for index in range(pairs):
            sl = tile_of(index)
            key_pair, value_pair = held[KEYS][0, :, sl], held[VALUES][0, :, sl]
            query_pair = held[QUERIES][:, :, sl].reshape(4 * rows, LANES)
            grad_pair = douts[layer_no, :, :, sl].reshape(4 * rows, LANES)
            queries = jnp.concatenate([query_pair, held[QUERIES][:, :, width:].reshape(4 * rows, LANES)], axis=1)
            grads = jnp.concatenate([grad_pair, douts[layer_no, :, :, width:].reshape(4 * rows, LANES)], axis=1)
            key_parts, value_parts = [], []
            for member, mine in enumerate(heads_lanes):
                head = 2 * index + member
                zero = jnp.zeros_like(key_pair)
                chosen = jnp.where((lane < 48) & (lax.rem(lane, 16) == head), 1.0, 0.0).astype(BF16)
                marked = jnp.where(lane == 127, jnp.broadcast_to(own_marks[:, 0:1], chosen.shape), chosen)
                weight = jnp.exp(
                    rows_by_rows(jnp.concatenate([jnp.where(mine, key_pair, zero), marked], axis=1), queries)
                )
                grad = rows_by_rows(jnp.concatenate([jnp.where(mine, value_pair, zero), chosen], axis=1), grads)
                grad = (weight * grad).astype(BF16)
                key_parts.append(rows_by_columns(grad, query_pair))
                value_parts.append(rows_by_columns(weight.astype(BF16), grad_pair))
            grad = jnp.where(first_head, key_parts[0], key_parts[1])
            back, turn = turned_back(layer_no, 1, index, grad, key_pair)
            note_turn(layer_no, index, turn, False)
            key_backs.append(back)
            grad = jnp.where(first_head, value_parts[0], value_parts[1])
            grad_qkv[:, 2 * width + LANES * index : 2 * width + LANES * index + LANES] = grad.astype(BF16)
            value_backs.append(grad)
        split_half(1, key_backs)
        split_half(2, value_backs)
        if layer_no == top:
            log_gather.drain()
        if layer_no > 0:
            load(layer_no - 1, KEYS, VALUES, ANGLES, LOGS, QUERIES)

    def input_back(layer_no):
        weights.ready(layer_no, QUERY_W, KEY_W, VALUE_W)
        total = rows_by_rows(grad_qkv[...], qkv_w[...])
        if layer_no > 0:
            weights.load(layer_no - 1, QUERY_W, KEY_W, VALUE_W)
        ready(layer_no, HAT1)
        hat = held[HAT1][...].astype(F32)
        carried[...] += norm_back(layer_no, 0, total, hat, held[SCALES][:, 0:1])
        if layer_no > 0:
            load(layer_no - 1, HAT1, SCALES)
            send_error(layer_no - 1)

    def put(layer_no, name, values, column, blocks):
        share = reductions[layer_no, name].share
        for first_row, count, tile in blocks:
            for i in range(values.shape[1] // LANES):
                piece = values[first_row : first_row + count, tile_of(i)].astype(BF16)
                at_tile, at_row = column(tile, i)
                share[at_tile, at_row : at_row + count] = piece

    def blocks_of(name):
        n, axes = plans[name][0], HALVING[name]
        blocks = []
        for number in range(8):
            bits = (number % 2, (number // 2) % 2, number // 4)
            tile = ((bits[axes[0]] * 2 + bits[axes[1]]) * 2 + bits[axes[2]]) * n
            blocks.append((number * size, size, tile))
        return blocks

    def down_product(layer_no):
        ready(layer_no, ACTS)
        error_swaps[layer_no].arrive()
        if layer_no == top:
            acts_swap.arrive()
        else:
            ready(layer_no, FAR_ACTS)
        for y in range(2):
            for c in range(2):
                product = columns_by_columns(held[ACTS][2 * y + c], errors[layer_no, 0]) + columns_by_columns(
                    held[FAR_ACTS][2 * y + c], errors[layer_no, 1]
                )
                put(layer_no, DOWN, product, lambda tile, i: (tile + i, 0), [(0, half, (2 * c + y) * 6)])
        if layer_no > 0:
            load(layer_no - 1, ACTS, FAR_ACTS)
        reductions[layer_no, DOWN].start()

    def up_product(layer_no):
        hidden_swaps[layer_no].arrive()
        if layer_no == top:
            normed_swap.arrive()
        else:
            ready(layer_no, NORMED2)
        for z1 in range(2):
            for part in range(2):
                columns = pl.ds(3 * LANES * part, 3 * LANES)
                product = columns_by_columns(
                    held[NORMED2][0], grad_hidden[layer_no, place.z0, z1, :, columns]
                ) + columns_by_columns(held[NORMED2][1], far_hidden[layer_no, z1, :, columns])
                put(layer_no, UP, product, lambda tile, i: (tile + z1, size * (3 * part + i)), blocks_of(UP))
        reductions[layer_no, UP].start()
        if layer_no == top:
            normed_swap.drain()
        hidden_swaps[layer_no].drain()
        if layer_no > 0:
            load(layer_no - 1, NORMED2)

    def narrow_product(layer_no, name, left, right, far):
        product = columns_by_columns(left[0], right) + columns_by_columns(left[1], far)
        put(layer_no, name, product, lambda tile, i: (tile + i, 0), blocks_of(name))
        reductions[layer_no, name].start()

    def proj_product(layer_no):
        middle_swaps[layer_no].arrive()
        if layer_no == top:
            mixed_swap.arrive()
        narrow_product(layer_no, PROJ, held[MIXED], grad_middle[place.z0], far_middle[layer_no])
        middle_swaps[layer_no].drain()
        if layer_no == top:
            mixed_swap.drain()
        if layer_no > 0:
            load(layer_no - 1, MIXED)

    used = []

    def part_product(layer_no, part):
        qkv_swaps[layer_no][part].arrive()
        if len(used) == 3 * (top - layer_no):
            ready(layer_no, NORMED)
        used.append(part)
        narrow_product(layer_no, QUERY + part, held[NORMED], half_qkv[part, place.z0], far_qkv[layer_no, part])
        qkv_swaps[layer_no][part].drain()
        if len(used) == 3 * (top - layer_no) + 3 and layer_no > 0:
            load(layer_no - 1, NORMED)

    results = (grad_down, grad_up, grad_proj, grad_query, grad_key, grad_value)

    def finish(layer_no, name):
        target = results[name]

        def write(own, rest=None):
            if rest is None:
                for part in range(own.shape[0] // size):
                    target[layer_no, :, tile_of(part)] = own[size * part : size * part + size]
            else:
                target[layer_no, :, :LANES] = own
                target[layer_no, :, LANES : LANES + 64] = rest

        reductions[layer_no, name].finish(write)

    def step(layer_no, name, stage):
        reductions[layer_no, name].step(stage)

    def return_grad():
        returned[...] = carried[...].astype(BF16)
        grad_return.start()

    ready(top, LOGS, MIXED, NORMED2)
    extras[0] = spread_lanes(-held[LOGS][...], lane, 1.0).astype(BF16)
    carried[...] = cotangent[...].astype(F32)
    send_error(top)
    acts_swap.start()
    normed_swap.start()
    hidden_back(top)
    hidden_swaps[top].start()
    middle_back(top)
    project_back(top)
    log_gather.start()
    own_queries(top)
    qkv_swaps[top][0].start()
    out_return.start()
    middle_send(top)
    mixed_swap.start()
    up_product(top)
    down_product(top)
    step(top, UP, 0)
    do_gathers[top].far()
    log_gather.far()
    step(top, DOWN, 0)
    own_keys(top)
    part_product(top, 0)
    input_back(top)
    hidden_back(low)
    hidden_swaps[low].start()
    step(top, QUERY, 0)
    middle_back(low)
    qkv_swaps[top][1].start()
    qkv_swaps[top][2].start()
    step(top, UP, 1)
    proj_product(top)
    project_back(low)
    step(top, DOWN, 1)
    own_queries(low)
    down_product(low)
    step(top, PROJ, 0)
    qkv_swaps[low][0].start()
    step(top, QUERY, 1)
    middle_send(low)
    up_product(low)
    step(top, UP, 2)
    part_product(top, 1)
    step(low, DOWN, 0)
    part_product(top, 2)
    step(low, UP, 0)
    step(top, KEY, 0)
    step(top, PROJ, 1)
    step(top, VALUE, 0)
    step(top, QUERY, 2)
    do_gathers[low].far()
    finish(top, UP)
    own_keys(low)
    qkv_swaps[low][1].start()
    qkv_swaps[low][2].start()
    step(top, DOWN, 2)
    input_back(low)
    part_product(low, 0)
    return_grad()
    doubling.start()
    finish(top, QUERY)
    step(low, DOWN, 1)
    step(top, PROJ, 2)
    step(low, UP, 1)
    doubling.step(0)
    proj_product(low)
    step(low, QUERY, 0)
    step(top, VALUE, 1)
    step(low, PROJ, 0)
    step(top, KEY, 1)
    doubling.step(1)
    part_product(low, 1)
    finish(top, DOWN)
    finish(top, PROJ)
    step(top, VALUE, 2)
    step(low, KEY, 0)
    part_product(low, 2)
    step(low, UP, 2)
    step(low, PROJ, 1)
    step(low, VALUE, 0)
    finish(top, VALUE)
    step(low, QUERY, 1)
    step(low, KEY, 1)
    step(top, KEY, 2)
    doubling.step(2)
    step(low, QUERY, 2)
    step(low, PROJ, 2)
    finish(low, UP)
    step(low, VALUE, 1)
    finish(top, KEY)
    step(low, DOWN, 2)
    finish(low, QUERY)
    step(low, KEY, 2)
    finish(low, PROJ)
    step(low, VALUE, 2)
    doubling.step(3)
    finish(low, DOWN)
    finish(low, KEY)
    finish(low, VALUE)
    doubling.step(4)
    grad_small[...] = sums[len(Doubling.AXES)]
    out_return.wait()
    grad_return.wait()
    for red in reductions.values():
        red.drain()
    for layer_no in range(layers):
        do_gathers[layer_no].drain()
        error_swaps[layer_no].drain()
    acts_swap.drain()


def backward_call(out, cotangent, marks, gains, whole, saved):
    layers = gains[0].shape[0]
    rows, width = out.shape
    hidden = whole[4].shape[2]
    shapes = saved_shapes(layers, rows, width, hidden)
    sem = pltpu.SemaphoreType.DMA
    any_spec, vmem_spec = pl.BlockSpec(memory_space=pl.ANY), pl.BlockSpec(memory_space=pltpu.VMEM)
    size, quarter = width // 8, width // 4
    plans = tile_plan(width, hidden)
    held = [pltpu.VMEM(shapes[name][0][2 if name == ACTS else 1 :], shapes[name][1]) for name in SAVED]
    tensors = plans * layers
    outs = (
        [jax.ShapeDtypeStruct((rows, width), BF16)] * 2
        + [
            jax.ShapeDtypeStruct((layers, size, hidden // 4), F32),
            jax.ShapeDtypeStruct((layers, hidden // 8, quarter), F32),
        ]
        + [jax.ShapeDtypeStruct((layers, size, quarter), F32)] * 4
        + [jax.ShapeDtypeStruct((8 * layers, width), F32)]
    )
    return pl.pallas_call(
        lambda *refs: backward_kernel(layers, *refs),
        out_shape=outs,
        in_specs=[any_spec] + [vmem_spec] * 4 + [any_spec] * (6 + len(SAVED)),
        out_specs=[any_spec, any_spec] + [vmem_spec] * 7,
        scratch_shapes=held
        + [pltpu.VMEM((8 * n, count, LANES), BF16) for n, count in tensors]
        + [pltpu.VMEM((landing_count(n), count, LANES), BF16) for n, count in tensors]
        + [
            pltpu.VMEM((width, 3 * width), BF16),
            pltpu.VMEM((width, width), BF16),
            pltpu.VMEM((width, hidden), BF16),
            pltpu.VMEM((hidden, width), BF16),
            sem((6,)),
            sem((len(SAVED),)),
            sem((2, 3)),
            pltpu.VMEM((layers, 4, rows, width + LANES), BF16),
            sem((layers, 4)),
            sem((layers, 4)),
            sem((4,)),
            sem((4,)),
            sem((layers, 9, 2)),
            sem((len(tensors), 5)),
            sem((len(tensors), 5)),
            pltpu.VMEM((layers, 2, rows, width), BF16),
            pltpu.VMEM((layers, 2, 2, rows, width), BF16),
            pltpu.VMEM((layers, 2, rows, width), BF16),
            pltpu.VMEM((2, rows, width // 2), BF16),
            pltpu.VMEM((layers, rows, width // 2), BF16),
            pltpu.VMEM((rows, 3 * width), BF16),
            pltpu.VMEM((3, 2, rows, width // 2), BF16),
            pltpu.VMEM((layers, 3, rows, width // 2), BF16),
            pltpu.VMEM((rows, width), F32),
            pltpu.VMEM((rows, width), BF16),
            pltpu.VMEM((6, 8 * layers, width), F32),
            pltpu.VMEM((5, 8 * layers, width), F32),
            sem((5, 2)),
        ],
        compiler_params=pltpu.CompilerParams(
            collective_id=1, has_side_effects=True, vmem_limit_bytes=VMEM_BYTES
        ),
    )(out, cotangent, marks, *gains, *whole, *saved)


def beyond_eight(result):
    dp_size = lax.axis_size(DP)
    groups = dp_size // 8
    if groups == 1:
        return result
    result = lax.psum(result, DP, axis_index_groups=[[g * 8 + i for g in range(groups)] for i in range(8)])
    whole = lax.all_gather(
        result, DP, axis=1, tiled=True, axis_index_groups=[[g * 8 + i for i in range(8)] for g in range(groups)]
    )
    rows = whole.shape[1] // dp_size
    return lax.dynamic_slice_in_dim(whole, lax.axis_index(DP) * rows, rows, axis=1)


def final_kernel(count, *refs):
    output, grad_patches, small = refs[:3]
    large = refs[3 : 3 + count]
    refs = refs[3 + count :]
    out_copy, grad_copy = refs[:2]
    large_copies = refs[2 : 2 + count]
    norms, turns = refs[2 + count : 6 + count], refs[6 + count]
    out_copy[...] = output[...]
    grad_copy[...] = grad_patches[...].astype(F32)
    for source, target in zip(large[:-1], large_copies[:-1]):
        target[...] = source[...]
    layers, columns = norms[0].shape
    for layer_no in range(layers):
        large_copies[-1][layer_no] = large[-1][layer_no].T
    at = lax.axis_index(BLK)
    half = turns.shape[3]
    for blk in range(small.shape[1] // columns):

        @pl.when(at == blk)
        def _(blk=blk):
            for layer_no in range(layers):
                mine = small[8 * layer_no : 8 * layer_no + 8, blk * columns : blk * columns + columns]
                for row, norm in enumerate(norms):
                    norm[layer_no : layer_no + 1] = mine[row : row + 1]
                for row in range(2):
                    for head in range(turns.shape[1]):
                        pair = mine[4 + row : 5 + row, 2 * half * head : 2 * half * head + 2 * half]
                        turns[layer_no, head, row : row + 1] = pair[:, half:] - pair[:, :half]


def final_call(output, grad_patches, small, large, half):
    vmem_spec = pl.BlockSpec(memory_space=pltpu.VMEM)
    layers = small.shape[0] // 8
    columns = small.shape[1] // lax.axis_size(BLK)
    return pl.pallas_call(
        lambda *refs: final_kernel(len(large), *refs),
        out_shape=[
            jax.ShapeDtypeStruct(output.shape, output.dtype),
            jax.ShapeDtypeStruct(grad_patches.shape, F32),
        ]
        + [jax.ShapeDtypeStruct(a.shape, F32) for a in large[:-1]]
        + [jax.ShapeDtypeStruct((layers,) + large[-1].shape[:0:-1], F32)]
        + [jax.ShapeDtypeStruct((layers, columns), F32)] * 4
        + [jax.ShapeDtypeStruct((layers, columns // (2 * half), 2, half), F32)],
        in_specs=[vmem_spec] * (3 + len(large)),
        out_specs=[vmem_spec] * (7 + len(large)),
    )(output, grad_patches, small, *large)


def shards(
    patches,
    keep,
    coords,
    query_w,
    key_w,
    value_w,
    proj_w,
    up_w,
    down_w,
    norm1_gain,
    norm1_bias,
    norm2_gain,
    norm2_bias,
    freqs,
    cotangent,
):
    whole = (query_w, key_w, value_w, proj_w, up_w, down_w)
    norms = (norm1_gain, norm1_bias, norm2_gain, norm2_bias)
    out, far_cotangent, marks, *saved = forward_call(
        patches[0], cotangent[0], keep, coords, norms, jnp.swapaxes(freqs, 1, 2), whole
    )
    results = backward_call(out, far_cotangent, marks, (norm1_gain, norm2_gain), whole, saved)
    output, grad_patches, grad_up, grad_down, *others, small = results
    large = [beyond_eight(grad) for grad in (*others[1:], others[0], grad_up, grad_down)]
    groups = lax.axis_size(DP) // 8
    if groups > 1:
        small = lax.psum(small, DP, axis_index_groups=[[g * 8 + i for g in range(groups)] for i in range(8)])
    output, grad_patches, *rest = final_call(output, grad_patches, small, large, freqs.shape[3])
    rest[5], rest[-1] = jnp.swapaxes(rest[5], 1, 2), jnp.swapaxes(rest[-1], 1, 2)
    return (output[None], grad_patches[None], *rest)


def solution(mesh):
    block = P(DP, BLK, None)
    placed = (block, P(DP, BLK), P(None, DP, BLK)) + (P(),) * 11 + (block,)
    results = (block, block) + (P(None, DP, BLK),) * 6 + (P(None, BLK),) * 4 + (P(None, None, BLK, None),)
    return jax.shard_map(shards, mesh=mesh, in_specs=placed, out_specs=results, check_vma=False)
```

```python
import jax
import jax.numpy as jnp
from jax import lax
from jax.experimental import pallas as pl
from jax.experimental.pallas import tpu as pltpu
from jax.sharding import PartitionSpec as P

MESH = pl.DeviceIdType.MESH
DP, BLK = "dp", "blk"
C, X, Y, Z0, Z1 = range(5)
BF16, F32 = jnp.bfloat16, jnp.float32
MASKED_SCORE = -1e30
NORM_EPSILON = 1e-06
LANES = 128
SCALE_LANE = 64
VMEM_BYTES = 127 * 512 * 1024


def rows_by_columns(left, right):
    return lax.dot_general(left, right, (((1,), (0,)), ((), ())), preferred_element_type=F32)


def rows_by_rows(left, right):
    return lax.dot_general(left, right, (((1,), (1,)), ((), ())), preferred_element_type=F32)


def columns_by_columns(left, right):
    return lax.dot_general(left, right, (((0,), (0,)), ((), ())), preferred_element_type=F32)


class Place:
    def __init__(self):
        self.dp = lax.axis_index(DP)
        self.blk = lax.axis_index(BLK)
        self.c = lax.rem(self.dp, 2)
        self.x = lax.rem(self.dp // 2, 2)
        self.y = lax.rem(self.dp // 4, 2)
        self.z0 = lax.rem(self.blk, 2)
        self.z1 = lax.rem(self.blk // 2, 2)
        self.bits = (self.c, self.x, self.y, self.z0, self.z1)
        self.worker = (self.dp - self.c + self.z0, 2 * self.c + self.z1)
        self.owner = (self.dp - self.c + self.z1, 2 * self.z0 + self.c)
        self.stays = (self.worker[0] == self.dp) & (self.worker[1] == self.blk)

    def other(self, axis):
        if axis <= Y:
            return (self.dp + (1 << axis) * (1 - 2 * self.bits[axis]), self.blk)
        return (self.dp, self.blk + (1 << axis - Z0) * (1 - 2 * self.bits[axis]))

    def greet(self, axes):
        barrier = pltpu.get_barrier_semaphore()
        mine = 2 * self.blk + self.c
        for step in range(1, 8):
            them = lax.rem(mine + step, 8)
            pl.semaphore_signal(
                barrier, inc=1, device_id=(self.dp - self.c + lax.rem(them, 2), them // 2), device_id_type=MESH
            )
        for axis in axes:
            pl.semaphore_signal(barrier, inc=1, device_id=self.other(axis), device_id_type=MESH)
        pl.semaphore_wait(barrier, 7 + len(axes))


class Relocation:
    def __init__(self, place, source, target, sems, back=False):
        self.place, self.source, self.target, self.sems = place, source, target, sems
        self.device = place.owner if back else place.worker

    def remote(self):
        return pltpu.make_async_remote_copy(
            src_ref=self.source,
            dst_ref=self.target,
            send_sem=self.sems.at[0],
            recv_sem=self.sems.at[1],
            device_id=self.device,
            device_id_type=MESH,
        )

    def local(self):
        return pltpu.make_async_copy(self.source, self.target, self.sems.at[2])

    def start(self):
        pl.when(self.place.stays)(lambda: self.local().start())
        pl.when(jnp.logical_not(self.place.stays))(lambda: self.remote().start())

    def wait(self):
        pl.when(self.place.stays)(lambda: self.local().wait())
        pl.when(jnp.logical_not(self.place.stays))(lambda: self.remote().wait())


class Gather:
    def __init__(self, place, slots, sends, receives):
        self.place, self.slots, self.sends, self.receives = place, slots, sends, receives

    def copy(self, source, slot, axis):
        return pltpu.make_async_remote_copy(
            src_ref=self.slots.at[source],
            dst_ref=self.slots.at[slot],
            send_sem=self.sends.at[slot],
            recv_sem=self.receives.at[slot],
            device_id=self.place.other(axis),
            device_id_type=MESH,
        )

    def start(self):
        self.copy(0, 2, Z0).start()
        self.copy(0, 1, C).start()

    def near(self):
        self.copy(0, 1, C).wait_recv()

    def far(self):
        self.copy(0, 2, Z0).wait_recv()
        self.copy(2, 3, C).start()

    def last(self):
        self.copy(2, 3, C).wait_recv()

    def drain(self):
        self.copy(0, 1, C).wait_send()
        self.copy(0, 2, Z0).wait_send()
        self.copy(2, 3, C).wait_send()


class Swap:
    def __init__(self, place, axis, source, target, sems):
        self.place, self.axis, self.source, self.target, self.sems = place, axis, source, target, sems

    def copy(self):
        return pltpu.make_async_remote_copy(
            src_ref=self.source,
            dst_ref=self.target,
            send_sem=self.sems.at[0],
            recv_sem=self.sems.at[1],
            device_id=self.place.other(self.axis),
            device_id_type=MESH,
        )

    def start(self):
        self.copy().start()

    def arrive(self):
        self.copy().wait_recv()

    def drain(self):
        self.copy().wait_send()


def lane_index(rows):
    return lax.broadcasted_iota(jnp.int32, (rows, LANES), 1)


def partner_tile(tile, former):
    return jnp.where(former, pltpu.roll(tile, 96, 1), pltpu.roll(tile, 32, 1))


def rotate_tile(tile, cosine, signed_sine, former):
    return tile * cosine + partner_tile(tile, former) * signed_sine


def tile_of(index):
    return slice(LANES * index, LANES * index + LANES)


def normalise(values):
    centre = values - jnp.mean(values, axis=-1, keepdims=True)
    spread = jnp.mean(centre * centre, axis=-1, keepdims=True)
    scale = lax.rsqrt(spread + NORM_EPSILON)
    return centre * scale, scale


QUERY_W, KEY_W, VALUE_W, PROJ_W, UP_W, DOWN_W = range(6)


class Weights:
    def __init__(self, whole, qkv, proj, up, down, sems):
        width = qkv.shape[1] // 3
        self.whole, self.sems = whole, sems
        self.buffers = [qkv.at[:, pl.ds(part * width, width)] for part in range(3)] + [proj, up, down]

    def copy(self, name, layer_no):
        return pltpu.make_async_copy(self.whole[name].at[layer_no], self.buffers[name], self.sems.at[name])

    def load(self, layer_no, *names):
        for name in names:
            self.copy(name, layer_no).start()

    def ready(self, layer_no, *names):
        for name in names:
            self.copy(name, layer_no).wait()


def spread_lanes(columns, lane, last):
    columns = jnp.where(lane < 16, columns, 0.0)
    high = columns.astype(BF16).astype(F32)
    middle = (columns - high).astype(BF16).astype(F32)
    low = columns - high - middle
    spread = high + pltpu.roll(middle, 16, 1) + pltpu.roll(low, 32, 1)
    return jnp.where(lane == 127, last, spread)


class Reduction:
    def __init__(self, place, axes, n, share, first_landing, landing, sends, receives, credit, gives, takes):
        self.place, self.axes = place, axes + (Z1, Z1)
        self.share, self.first_landing, self.landing = share, first_landing, landing
        self.sends, self.receives = sends, receives
        self.credit, self.gives, self.takes = credit, gives, takes
        self.n, self.rows = n, share.shape[1]
        self.plan = []
        base, half, land = 0, 4 * n, 0
        for axis in axes:
            bit = place.bits[axis]
            self.plan.append((base + (1 - bit) * half, base + bit * half, half, land))
            base, land, half = base + bit * half, land + half if self.plan[1:] else 0, half // 2
        self.spare = self.plan[0][0]
        self.base, self.land = base, land
        self.plan.append((base + (n - 1) * (1 - place.z1), base + (n - 1) * place.z1, 1, land))

    def copy(self, stage):
        if stage < 4:
            send, _, count, land = self.plan[stage]
            landing = self.first_landing if stage == 0 else self.landing
            source, target = self.share.at[pl.ds(send, count)], landing.at[pl.ds(land, count)]
        else:
            half = pl.ds(0, self.rows // 2)
            source, target = self.share.at[self.spare, half], self.landing.at[self.land + 1, half]
        return pltpu.make_async_remote_copy(
            src_ref=source,
            dst_ref=target,
            send_sem=self.sends.at[stage],
            recv_sem=self.receives.at[stage],
            device_id=self.place.other(self.axes[stage]),
            device_id_type=MESH,
        )

    def start(self, stage=0):
        if stage == 0 and self.takes:
            pl.semaphore_wait(self.credit, 1)
        self.copy(stage).start()

    def step(self, stage):
        _, keep, count, land = self.plan[stage]
        self.copy(stage).wait_recv()

        landing = self.first_landing if stage == 0 else self.landing

        def body(i, carry):
            self.share[keep + i] = self.share[keep + i] + landing[land + i]
            return carry

        lax.fori_loop(0, count, body, 0)
        self.start(stage + 1)
        if stage == 0:
            self.copy(0).wait_send()
            if self.gives:
                pl.semaphore_signal(self.credit, inc=1, device_id=self.place.other(C), device_id_type=MESH)
        if stage == 2 and self.n == 3:
            half = self.rows // 2
            shared = self.share[self.base + 1].astype(F32)
            upper, lower = shared[:half], shared[half:]
            first = lane_index(half) < 64
            low_lanes = jnp.where(first, upper, pltpu.roll(lower, 64, 1))
            high_lanes = jnp.where(first, pltpu.roll(upper, 64, 1), lower)
            self.share[self.spare, :half] = jnp.where(self.place.z1 == 1, low_lanes, high_lanes).astype(BF16)
            self.start(4)

    def finish(self, write):
        self.copy(3).wait_recv()
        _, keep, _, land = self.plan[3]
        own = self.share[keep].astype(F32) + self.landing[land].astype(F32)
        if self.n == 2:
            write(own)
            return
        self.copy(4).wait_recv()
        half = self.rows // 2
        packed = self.landing[self.land + 1, :half].astype(F32)
        shared = self.share[self.base + 1].astype(F32)
        shared = jnp.where(self.place.z1 == 0, shared, pltpu.roll(shared, 64, 1))
        rest = shared + jnp.concatenate([packed, pltpu.roll(packed, 64, 1)], axis=0)
        write(own, rest[:, :64])

    def drain(self):
        for stage in range(1, 4 if self.n == 2 else 5):
            self.copy(stage).wait_send()


class Doubling:
    AXES = (C, X, Y, Z0, Z1)

    def __init__(self, place, sums, landing, sems):
        self.place, self.sums, self.landing, self.sems = place, sums, landing, sems

    def copy(self, stage):
        return pltpu.make_async_remote_copy(
            src_ref=self.sums,
            dst_ref=self.landing.at[stage],
            send_sem=self.sems.at[stage, 0],
            recv_sem=self.sems.at[stage, 1],
            device_id=self.place.other(self.AXES[stage]),
            device_id_type=MESH,
        )

    def start(self):
        self.copy(0).start()

    def step(self, stage):
        self.copy(stage).wait()
        self.sums[...] += self.landing[stage]
        if stage + 1 < len(self.AXES):
            self.copy(stage + 1).start()


TENSORS = DOWN, UP, PROJ, QUERY, KEY, VALUE = range(6)
HALVING = ((C, Y, Z0), (C, X, Y), (C, X, Y), (C, Y, X), (C, X, Y), (C, Y, X))


def tile_plan(width, hidden):
    size = width // 8
    return ((3, hidden // 8), (2, size * (hidden // 4 // LANES))) + ((3, size),) * 4


def landing_count(n):
    return 2 * n + n + n - 1


def by_halves(tiles, first):
    def turned(tile):
        return pltpu.roll(tile, 64, 1)

    return (
        (tiles[0], jnp.where(first, tiles[1], turned(tiles[4])), tiles[3]),
        (
            jnp.where(first, turned(tiles[1]), turned(tiles[2])),
            jnp.where(first, turned(tiles[2]), tiles[5]),
            jnp.where(first, turned(tiles[4]), turned(tiles[5])),
        ),
    )


KEYS, VALUES, QUERIES, ANGLES, SLOPES = SPILLED = range(5)


def spilled_shapes(rows, width, hidden):
    return (
        ((4, rows, width), BF16),
        ((4, rows, width), BF16),
        ((4, rows, width), BF16),
        ((2, rows, width), F32),
        ((rows, hidden), BF16),
    )


def encoder_kernel(layers, *refs):
    patches, cotangent, keep, coords, gain1, bias1, gain2, bias2, freqs = refs[:9]
    whole = refs[9:15]
    output, grad_patches = refs[15:17]
    results = refs[17:23]
    grad_small = refs[23]
    saved = refs[24:29]
    held = refs[29:34]
    refs = refs[34:]
    count = layers * len(TENSORS)
    shares, landings, first_landings = refs[:count], refs[count : 2 * count], refs[2 * count : 2 * count + len(TENSORS)]
    refs = refs[2 * count + len(TENSORS) :]
    stagings = refs[: len(TENSORS)]
    refs = refs[len(TENSORS) :]
    (qkv_w, proj_w, up_w, down_w, w_sems, spill_sems, load_sems, stage_sems) = refs[:8]
    (normed, logs_low, mixed, normed2, acts, far_acts, hat1, hat2, stats) = refs[8:17]
    (start, own_marks, marks, returned, relocation_sems) = refs[17:22]
    (h_sends, h_receives, do_sends, do_receives, q_sends, q_receives, m_sends, m_receives) = refs[22:30]
    (douts, errors, grad_hidden, far_hidden, far_middle, grad_qkv, half_qkv, far_qkv) = refs[30:38]
    (swap_sems, sends, receives, credits, carried, sums, sums_landing, sums_sems) = refs[38:]
    place = Place()
    rows, width = carried.shape
    hidden = up_w.shape[1]
    half = hidden // 8
    size = width // 8
    pairs = width // LANES
    top, low = layers - 1, layers - 2
    weights = Weights(whole, qkv_w, proj_w, up_w, down_w, w_sems)
    weights.load(0, KEY_W, VALUE_W, QUERY_W, PROJ_W, UP_W, DOWN_W)
    line = lax.broadcasted_iota(jnp.int32, (LANES, rows), 0)
    own = jnp.where(line == 0, jnp.where(keep[...] > 0, 0.0, MASKED_SCORE), 0.0)
    for number in range(2):
        own = jnp.where(line == 1 + number, coords[number].astype(F32), own)
    own_marks[...] = own.T.astype(BF16)
    place.greet((X, Y))

    lane = lane_index(rows)
    former = lax.rem(lane, 64) < 32
    first_head = lane < 64
    heads_lanes = (first_head, jnp.logical_not(first_head))
    one_lane = jnp.where(lane == 0, 1.0, 0.0).astype(BF16)
    plans = tile_plan(width, hidden)
    away = 1 - place.z0

    def relocation(number, source, target, back=False):
        return Relocation(place, source, target, relocation_sems.at[number], back)

    def swap(layer_no, number, axis, source, target):
        return Swap(place, axis, source, target, swap_sems.at[layer_no, number])

    every = range(layers)

    def grad_middle(z0):
        return normed.at[top, 1, :, pl.ds(pl.multiple_of(z0 * (width // 2), LANES), width // 2)]

    mark_arrival = relocation(0, own_marks, marks.at[0])
    arrival = relocation(1, patches, start)
    other_arrival = relocation(2, cotangent, returned)
    out_return = relocation(3, start, output, True)
    grad_return = relocation(4, returned, grad_patches, True)
    mark_gather = Gather(place, marks, m_sends, m_receives)
    h_gathers = [Gather(place, normed.at[l], h_sends.at[l], h_receives.at[l]) for l in every]
    log_gathers = [Gather(place, logs_low.at[l], q_sends.at[l], q_receives.at[l]) for l in every]
    do_gathers = [Gather(place, douts.at[l], do_sends.at[l], do_receives.at[l]) for l in every]
    own_errors = [normed.at[0, 1 + 2 * l] for l in every]
    error_swaps = [swap(l, 0, X, own_errors[l], errors.at[l]) for l in every]
    hidden_swaps = [swap(l, 1, Z0, grad_hidden.at[l, away], far_hidden.at[l]) for l in every]
    middle_swaps = [swap(l, 2, Z0, grad_middle(away), far_middle.at[l]) for l in every]
    qkv_swaps = [[swap(l, 3 + part, Z0, half_qkv.at[part, away], far_qkv.at[l, part]) for part in range(3)] for l in every]
    mixed_swaps = [swap(l, 6, Z0, mixed.at[l, 0], mixed.at[l, 1]) for l in every]
    normed_swaps = [swap(l, 7, Z0, normed2.at[l, 0], normed2.at[l, 1]) for l in every]
    acts_swaps = [
        [
            swap(l, 8 + y, X, acts.at[l, 1 - place.x, pl.ds(2 * y, 2)], far_acts.at[l, pl.ds(2 * y, 2)])
            for y in range(2)
        ]
        for l in every
    ]
    doubling = Doubling(place, sums, sums_landing, sums_sems)
    reductions = {}
    for layer_no in every:
        for name in TENSORS:
            at = layer_no * len(TENSORS) + name
            reductions[layer_no, name] = Reduction(
                place,
                HALVING[name],
                plans[name][0],
                shares[at],
                first_landings[name],
                landings[at],
                sends.at[at],
                receives.at[at],
                credits.at[name],
                layer_no > 0,
                layer_no < top,
            )

    def spill(name):
        return pltpu.make_async_copy(held[name], saved[name], spill_sems.at[name])

    def loading(name):
        return pltpu.make_async_copy(saved[name], held[name], load_sems.at[name])

    def load(layer_no, *names):
        for name in names:
            loading(name).start()

    def ready(layer_no, *names):
        if layer_no < top:
            for name in names:
                loading(name).wait()


    def freq_tile(layer_no, which, index):
        pair = [freqs[layer_no, 2 * index + member, which : which + 1] for member in range(2)]
        return jnp.concatenate([pair[0]] * 2 + [pair[1]] * 2, axis=1)

    def angle_refs(slot):
        if slot == 0:
            return held[ANGLES].at[0], held[ANGLES].at[1]
        return grad_hidden.at[0, slot // 2, slot % 2], grad_hidden.at[1, slot // 2, slot % 2]

    def make_angles(layer_no, slot):
        rows_at = marks[slot][:, 1:2].astype(F32)
        columns_at = marks[slot][:, 2:3].astype(F32)
        cosine, sine = angle_refs(slot)
        for index in range(pairs):
            sl = tile_of(index)
            angle = rows_at * freq_tile(layer_no, 0, index) + columns_at * freq_tile(layer_no, 1, index)
            cosine[:, sl] = jnp.cos(angle).astype(cosine.dtype)
            sine[:, sl] = (jnp.where(former, -1.0, 1.0) * jnp.sin(angle)).astype(sine.dtype)

    def project(layer_no, slot):
        cosine, sine = angle_refs(slot)
        block = normed[layer_no, slot]
        for name, part, scale in ((QUERIES, 0, 0.125), (KEYS, 1, 1.0)):
            products = rows_by_columns(block, qkv_w[:, part * width : part * width + width])
            for index in range(pairs):
                sl = tile_of(index)
                turned = rotate_tile(products[:, sl], cosine[:, sl].astype(F32), sine[:, sl].astype(F32), former)
                held[name][slot, :, sl] = (scale * turned).astype(BF16)
        held[VALUES][slot] = rows_by_columns(block, qkv_w[:, 2 * width :]).astype(BF16)

    def normalise_first(layer_no):
        hat, scale = normalise(carried[...])
        hat1[layer_no] = hat.astype(BF16)
        stats[layer_no] = jnp.where(lane == SCALE_LANE, scale, 0.0)
        normed[layer_no, 0] = (hat * gain1[layer_no : layer_no + 1] + bias1[layer_no : layer_no + 1]).astype(BF16)
        h_gathers[layer_no].start()

    def attend(layer_no):
        marks_of_keys = marks[...].reshape(4 * rows, LANES)
        sums_of_rows = jnp.zeros((rows, LANES), F32)
        for index in range(pairs):
            sl = tile_of(index)
            query_pair = held[QUERIES][0, :, sl]
            key_pair = held[KEYS][:, :, sl].reshape(4 * rows, LANES)
            value_pair = held[VALUES][:, :, sl].reshape(4 * rows, LANES)
            extended = jnp.concatenate([key_pair, marks_of_keys], axis=1)
            parts = []
            for member, mine in enumerate(heads_lanes):
                query = jnp.where(mine, query_pair, jnp.zeros_like(query_pair))
                scores = rows_by_rows(jnp.concatenate([query, one_lane], axis=1), extended)
                highest = jnp.max(scores, axis=1, keepdims=True)
                weight = jnp.exp(scores - highest)
                total = jnp.sum(weight, axis=1, keepdims=True)
                parts.append(rows_by_columns(weight.astype(BF16), value_pair) / total)
                sums_of_rows = jnp.where(lane == 2 * index + member, highest + jnp.log(total), sums_of_rows)
            mixed[layer_no, 0, :, sl] = jnp.where(first_head, parts[0], parts[1]).astype(BF16)
        stats[layer_no] = jnp.where(lane < 16, sums_of_rows, stats[layer_no])
        logs_low[layer_no, 0] = spread_lanes(-sums_of_rows, lane, 1.0).astype(BF16)

    def project_out(layer_no):
        weights.ready(layer_no, PROJ_W)
        middle = carried[...] + rows_by_columns(mixed[layer_no, 0], proj_w[...])
        carried[...] = middle
        if layer_no < top:
            weights.load(layer_no + 1, PROJ_W)
        hat, scale = normalise(middle)
        hat2[layer_no] = hat.astype(BF16)
        stats[layer_no] = jnp.where(lane == SCALE_LANE + 1, scale, stats[layer_no])
        normed2[layer_no, 0] = (hat * gain2[layer_no : layer_no + 1] + bias2[layer_no : layer_no + 1]).astype(BF16)

    def quarter_of(quarter):
        return slice(2 * half * quarter, 2 * half * quarter + 2 * half)

    def feed_forward(layer_no, quarter):
        if quarter == 0:
            weights.ready(layer_no, UP_W)
        columns = quarter_of(quarter)
        hidden_part = rows_by_columns(normed2[layer_no, 0], up_w[:, columns])
        share = 0.5 + 0.5 * lax.erf(hidden_part * 0.7071067811865476)
        active = (hidden_part * share).astype(BF16)
        slope = share + hidden_part * (0.3989422804014327 * jnp.exp(-0.5 * hidden_part * hidden_part))
        held[SLOPES][:, columns] = slope.astype(BF16)
        y, x = quarter // 2, quarter % 2
        acts[layer_no, x, 2 * y] = active[:, :half]
        acts[layer_no, x, 2 * y + 1] = active[:, half:]
        if quarter == 0:
            weights.ready(layer_no, DOWN_W)
        carried[...] += rows_by_columns(active, down_w[columns, :])


    def note(layer_no, row, values):
        sums[8 * layer_no + row : 8 * layer_no + row + 1] = jnp.sum(values, axis=0, keepdims=True)

    def norm_back(layer_no, number, grad, hat, scale):
        note(layer_no, 2 * number, grad * hat)
        note(layer_no, 2 * number + 1, grad)
        grad = grad * (gain1, gain2)[number][layer_no : layer_no + 1]
        mean = jnp.mean(grad, axis=-1, keepdims=True)
        slope = jnp.mean(grad * hat, axis=-1, keepdims=True)
        return scale * (grad - mean - hat * slope)

    def halves_of(values):
        return by_halves([values[:, tile_of(i)] for i in range(pairs)], first_head)

    def send_error(layer_no, values):
        for z0, tiles in enumerate(halves_of(values)):
            for i, tile in enumerate(tiles):
                own_errors[layer_no][:, tile_of(3 * z0 + i)] = tile.astype(BF16)
        error_swaps[layer_no].start()

    def hidden_back(layer_no):
        error = carried[...].astype(BF16)
        if layer_no < top:
            weights.ready(layer_no, DOWN_W)
        ready(layer_no, SLOPES)
        for quarter in range(4):
            grad = rows_by_rows(error, down_w[quarter_of(quarter), :])
            grad = grad * held[SLOPES][:, quarter_of(quarter)].astype(F32)
            grad_hidden[layer_no, quarter % 2, quarter // 2] = grad.astype(BF16)
        if layer_no > 0:
            weights.load(layer_no - 1, DOWN_W)
            load(layer_no - 1, SLOPES)

    def middle_back(layer_no):
        if layer_no < top:
            weights.ready(layer_no, UP_W)
        total = jnp.zeros((rows, width), F32)
        for quarter in range(4):
            total = total + rows_by_rows(grad_hidden[layer_no, quarter % 2, quarter // 2], up_w[:, quarter_of(quarter)])
        if layer_no > 0:
            weights.load(layer_no - 1, UP_W)
        carried[...] += norm_back(layer_no, 1, total, hat2[layer_no].astype(F32), stats[layer_no][:, SCALE_LANE + 1 : SCALE_LANE + 2])

    def project_back(layer_no):
        if layer_no < top:
            weights.ready(layer_no, PROJ_W)
        grad = rows_by_rows(carried[...].astype(BF16), proj_w[...])
        if layer_no > 0:
            weights.load(layer_no - 1, PROJ_W)
        deltas = jnp.zeros((rows, LANES), F32)
        for index in range(pairs):
            sl = tile_of(index)
            low_grad = grad[:, sl].astype(BF16)
            douts[layer_no, 0, :, sl] = low_grad
            product = low_grad.astype(F32) * mixed[layer_no, 0, :, sl].astype(F32)
            for member, mine in enumerate(heads_lanes):
                delta = jnp.sum(jnp.where(mine, product, 0.0), axis=1, keepdims=True)
                deltas = jnp.where(lane == 2 * index + member, delta, deltas)
        douts[layer_no, 0, :, width:] = spread_lanes(-deltas, lane, 0.0).astype(BF16)
        do_gathers[layer_no].start()
        kept_deltas.append(deltas)

    kept_deltas = []

    def middle_send(layer_no):
        for z0, tiles in enumerate(halves_of(carried[...])):
            for i, tile in enumerate(tiles):
                grad_middle(z0)[:, tile_of(i)] = tile.astype(BF16)
        middle_swaps[layer_no].start()

    def turned_back(layer_no, part, index, grad, forward):
        sl = tile_of(index)
        back = grad * held[ANGLES][0, :, sl] - partner_tile(grad, former) * held[ANGLES][1, :, sl]
        grad_qkv[:, part * width + LANES * index : part * width + LANES * index + LANES] = back.astype(BF16)
        return back, grad * partner_tile(forward.astype(F32), former)

    def note_turn(layer_no, index, turn, first):
        for row in range(2):
            at = 8 * layer_no + 4 + row
            total = jnp.sum(turn * marks[0][:, 1 + row : 2 + row].astype(F32), axis=0, keepdims=True)
            if not first:
                total = total + sums[at : at + 1, tile_of(index)]
            sums[at : at + 1, tile_of(index)] = total

    def split_half(part, tiles):
        for z0, group in enumerate(by_halves(tiles, first_head)):
            for i, tile in enumerate(group):
                half_qkv[part, z0, :, tile_of(i)] = tile.astype(BF16)

    def own_queries(layer_no):
        ready(layer_no, KEYS, VALUES, ANGLES, QUERIES)
        deltas = kept_deltas[-1]
        key_marks = marks[...].reshape(4 * rows, LANES)
        backs = []
        for index in range(pairs):
            sl = tile_of(index)
            query_pair = held[QUERIES][0, :, sl]
            key_pair = held[KEYS][:, :, sl].reshape(4 * rows, LANES)
            value_pair = held[VALUES][:, :, sl].reshape(4 * rows, LANES)
            grad_pair = douts[layer_no, 0, :, sl]
            extended = jnp.concatenate([key_pair, key_marks], axis=1)
            parts = []
            for member, mine in enumerate(heads_lanes):
                head = 2 * index + member
                zero = jnp.zeros_like(query_pair)
                scores = rows_by_rows(
                    jnp.concatenate([jnp.where(mine, query_pair, zero), one_lane], axis=1), extended
                )
                weight = jnp.exp(scores - stats[layer_no][:, head : head + 1])
                grad = rows_by_rows(jnp.where(mine, grad_pair, zero), value_pair)
                grad = (weight * (grad - deltas[:, head : head + 1])).astype(BF16)
                parts.append(rows_by_columns(grad, key_pair))
            grad = 0.125 * jnp.where(first_head, parts[0], parts[1])
            back, turn = turned_back(layer_no, 0, index, grad, 8.0 * query_pair.astype(F32))
            note_turn(layer_no, index, turn, True)
            backs.append(back)
        split_half(0, backs)

    def own_keys(layer_no):
        do_gathers[layer_no].near()
        do_gathers[layer_no].last()
        if layer_no == top:
            log_gathers[layer_no].near()
            log_gathers[layer_no].last()
        own_marks = marks[0]
        key_backs, value_backs = [], []
        for index in range(pairs):
            sl = tile_of(index)
            key_pair, value_pair = held[KEYS][0, :, sl], held[VALUES][0, :, sl]
            query_pair = held[QUERIES][:, :, sl].reshape(4 * rows, LANES)
            grad_pair = douts[layer_no, :, :, sl].reshape(4 * rows, LANES)
            queries = jnp.concatenate([query_pair, logs_low[layer_no].reshape(4 * rows, LANES)], axis=1)
            grads = jnp.concatenate([grad_pair, douts[layer_no, :, :, width:].reshape(4 * rows, LANES)], axis=1)
            key_parts, value_parts = [], []
            for member, mine in enumerate(heads_lanes):
                head = 2 * index + member
                zero = jnp.zeros_like(key_pair)
                chosen = jnp.where((lane < 48) & (lax.rem(lane, 16) == head), 1.0, 0.0).astype(BF16)
                marked = jnp.where(lane == 127, jnp.broadcast_to(own_marks[:, 0:1], chosen.shape), chosen)
                weight = jnp.exp(
                    rows_by_rows(jnp.concatenate([jnp.where(mine, key_pair, zero), marked], axis=1), queries)
                )
                grad = rows_by_rows(jnp.concatenate([jnp.where(mine, value_pair, zero), chosen], axis=1), grads)
                grad = (weight * grad).astype(BF16)
                key_parts.append(rows_by_columns(grad, query_pair))
                value_parts.append(rows_by_columns(weight.astype(BF16), grad_pair))
            grad = jnp.where(first_head, key_parts[0], key_parts[1])
            back, turn = turned_back(layer_no, 1, index, grad, key_pair)
            note_turn(layer_no, index, turn, False)
            key_backs.append(back)
            grad = jnp.where(first_head, value_parts[0], value_parts[1])
            grad_qkv[:, 2 * width + LANES * index : 2 * width + LANES * index + LANES] = grad.astype(BF16)
            value_backs.append(grad)
        split_half(1, key_backs)
        split_half(2, value_backs)
        if layer_no > 0:
            load(layer_no - 1, KEYS, VALUES, ANGLES, QUERIES)

    def input_back(layer_no):
        if layer_no < top:
            weights.ready(layer_no, QUERY_W, KEY_W, VALUE_W)
        total = rows_by_rows(grad_qkv[...], qkv_w[...])
        if layer_no > 0:
            weights.load(layer_no - 1, QUERY_W, KEY_W, VALUE_W)
        carried[...] += norm_back(layer_no, 0, total, hat1[layer_no].astype(F32), stats[layer_no][:, SCALE_LANE : SCALE_LANE + 1])
        if layer_no > 0:
            send_error(layer_no - 1, carried[...])

    def put(layer_no, name, values, column, blocks, skipped=0):
        share = reductions[layer_no, name].share
        for first_row, count, tile in blocks:
            for i in range(values.shape[1] // LANES):
                piece = values[first_row - skipped : first_row - skipped + count, tile_of(i)].astype(BF16)
                at_tile, at_row = column(tile, i)
                share[at_tile, at_row : at_row + count] = piece

    def blocks_of(name):
        n, axes = plans[name][0], HALVING[name]
        blocks = []
        for number in range(8):
            bits = (number % 2, (number // 2) % 2, number // 4)
            tile = ((bits[axes[0]] * 2 + bits[axes[1]]) * 2 + bits[axes[2]]) * n
            blocks.append((number * size, size, tile))
        return blocks

    def down_product(layer_no):
        error_swaps[layer_no].arrive()
        if layer_no == top:
            for part in acts_swaps[layer_no]:
                part.arrive()
        for y in range(2):
            for c in range(2):
                for z0 in range(2):
                    columns = slice(z0 * width // 2, (z0 + 1) * width // 2)
                    product = columns_by_columns(
                        acts[layer_no, place.x, 2 * y + c], own_errors[layer_no][:, columns]
                    ) + columns_by_columns(far_acts[layer_no, 2 * y + c], errors[layer_no, :, columns])
                    put(layer_no, DOWN, product, lambda tile, i: (tile + i, 0), [(0, half, ((2 * c + y) * 2 + z0) * 3)])
        reductions[layer_no, DOWN].start()

    def up_product(layer_no):
        hidden_swaps[layer_no].arrive()
        if layer_no == top:
            normed_swaps[layer_no].arrive()
        for z1 in range(2):
            for part in range(2):
                columns = pl.ds(3 * LANES * part, 3 * LANES)
                for side in range(2):
                    product = columns_by_columns(
                        normed2[layer_no, 0, :, side * 4 * size : side * 4 * size + 4 * size],
                        grad_hidden[layer_no, place.z0, z1, :, columns],
                    ) + columns_by_columns(
                        normed2[layer_no, 1, :, side * 4 * size : side * 4 * size + 4 * size],
                        far_hidden[layer_no, z1, :, columns],
                    )
                    put(
                        layer_no,
                        UP,
                        product,
                        lambda tile, i: (tile + z1, size * (3 * part + i)),
                        blocks_of(UP)[4 * side : 4 * side + 4],
                        4 * size * side,
                    )
        reductions[layer_no, UP].start()
        hidden_swaps[layer_no].drain()

    def narrow_product(layer_no, name, left, right, far):
        blocks = blocks_of(name)
        for side in range(2):
            columns = slice(side * 4 * size, side * 4 * size + 4 * size)
            product = columns_by_columns(left[0][:, columns], right) + columns_by_columns(left[1][:, columns], far)
            put(layer_no, name, product, lambda tile, i: (tile + i, 0), blocks[4 * side : 4 * side + 4], 4 * size * side)
        reductions[layer_no, name].start()

    def proj_product(layer_no):
        middle_swaps[layer_no].arrive()
        if layer_no == top:
            mixed_swaps[layer_no].arrive()
        left = (mixed.at[layer_no, 0], mixed.at[layer_no, 1])
        narrow_product(layer_no, PROJ, left, grad_middle(place.z0)[...], far_middle[layer_no])
        middle_swaps[layer_no].drain()

    def part_product(layer_no, part):
        qkv_swaps[layer_no][part].arrive()
        left = (normed.at[layer_no, 0], normed.at[layer_no, 2])
        narrow_product(layer_no, QUERY + part, left, half_qkv[part, place.z0], far_qkv[layer_no, part])
        qkv_swaps[layer_no][part].drain()

    def hand_out(layer_no, name):
        return pltpu.make_async_copy(stagings[name], results[name].at[layer_no], stage_sems.at[name])

    def finish(layer_no, name):
        target = stagings[name]
        if layer_no < top:
            hand_out(layer_no + 1, name).wait()

        def write(own, rest=None):
            if rest is None:
                for part in range(own.shape[0] // size):
                    target[:, tile_of(part)] = own[size * part : size * part + size]
            else:
                target[:, :LANES] = own
                target[:, LANES : LANES + 64] = rest

        reductions[layer_no, name].finish(write)
        hand_out(layer_no, name).start()

    def step(layer_no, name, stage):
        reductions[layer_no, name].step(stage)

    def return_grad():
        out_return.wait()
        returned[...] = carried[...].astype(BF16)
        grad_return.start()

    def low_arrivals():
        log_gathers[low].last()
        for one in [mixed_swaps[low], normed_swaps[low]] + acts_swaps[low]:
            one.arrive()

    mark_arrival.start()
    arrival.start()
    sums[...] = jnp.zeros(sums.shape, F32)
    mark_arrival.wait()
    mark_gather.start()
    make_angles(0, 0)
    arrival.wait()
    carried[...] = start[...].astype(F32)
    normalise_first(0)
    weights.ready(0, KEY_W, VALUE_W, QUERY_W)
    project(0, 0)
    mark_gather.near()
    mark_gather.far()
    make_angles(0, 1)
    h_gathers[0].near()
    project(0, 1)
    make_angles(0, 2)
    mark_gather.last()
    make_angles(0, 3)
    h_gathers[0].far()
    other_arrival.start()
    project(0, 2)
    h_gathers[0].last()
    project(0, 3)
    weights.load(1, KEY_W, VALUE_W, QUERY_W)
    for name in (KEYS, VALUES, QUERIES, ANGLES):
        spill(name).start()
    attend(0)
    mixed_swaps[0].start()
    project_out(0)
    for quarter in range(4):
        feed_forward(0, quarter)
    weights.load(1, UP_W, DOWN_W)
    spill(SLOPES).start()
    for part in acts_swaps[0]:
        part.start()
    normalise_first(1)
    normed_swaps[0].start()
    log_gathers[0].start()
    for name in (KEYS, VALUES, QUERIES, ANGLES):
        spill(name).wait()
    make_angles(1, 0)
    weights.ready(1, KEY_W, VALUE_W, QUERY_W)
    project(1, 0)
    make_angles(1, 1)
    h_gathers[1].near()
    project(1, 1)
    make_angles(1, 2)
    make_angles(1, 3)
    other_arrival.wait()
    send_error(1, returned[...].astype(F32))
    h_gathers[1].far()
    project(1, 2)
    h_gathers[1].last()
    project(1, 3)
    log_gathers[0].near()
    log_gathers[0].far()
    attend(1)
    log_gathers[1].start()
    mixed_swaps[1].start()
    project_out(1)
    normed_swaps[1].start()
    spill(SLOPES).wait()
    feed_forward(1, 0)
    feed_forward(1, 1)
    acts_swaps[1][0].start()
    feed_forward(1, 2)
    feed_forward(1, 3)
    acts_swaps[1][1].start()
    start[...] = carried[...].astype(BF16)
    carried[...] = returned[...].astype(F32)
    low_arrivals()
    out_return.start()
    log_gathers[top].far()
    hidden_back(top)
    middle_back(top)
    project_back(top)
    middle_send(top)
    own_queries(top)
    qkv_swaps[top][0].start()
    down_product(top)
    hidden_swaps[top].start()
    step(top, DOWN, 0)
    do_gathers[top].far()
    own_keys(top)
    input_back(top)
    qkv_swaps[top][1].start()
    qkv_swaps[top][2].start()
    part_product(top, 0)
    hidden_back(low)
    step(top, QUERY, 0)
    middle_back(low)
    hidden_swaps[low].start()
    up_product(top)
    down_product(low)
    step(top, DOWN, 1)
    step(top, QUERY, 1)
    part_product(top, 1)
    part_product(top, 2)
    step(top, UP, 0)
    project_back(low)
    step(low, DOWN, 0)
    step(top, KEY, 0)
    step(top, VALUE, 0)
    step(top, QUERY, 2)
    proj_product(top)
    middle_send(low)
    own_queries(low)
    qkv_swaps[low][0].start()
    finish(top, QUERY)
    step(top, PROJ, 0)
    up_product(low)
    step(low, UP, 0)
    step(top, DOWN, 2)
    step(top, UP, 1)
    step(low, DOWN, 1)
    step(top, KEY, 1)
    do_gathers[low].far()
    step(top, VALUE, 1)
    own_keys(low)
    qkv_swaps[low][1].start()
    qkv_swaps[low][2].start()
    step(top, PROJ, 1)
    input_back(low)
    return_grad()
    step(top, KEY, 2)
    doubling.start()
    part_product(low, 0)
    step(top, UP, 2)
    finish(top, DOWN)
    proj_product(low)
    doubling.step(0)
    step(top, PROJ, 2)
    step(low, QUERY, 0)
    step(low, PROJ, 0)
    finish(top, KEY)
    step(low, UP, 1)
    step(low, DOWN, 2)
    step(top, VALUE, 2)
    doubling.step(1)
    step(low, QUERY, 1)
    part_product(low, 1)
    part_product(low, 2)
    step(low, PROJ, 1)
    finish(top, UP)
    step(low, KEY, 0)
    finish(top, PROJ)
    step(low, VALUE, 0)
    step(low, QUERY, 2)
    step(low, UP, 2)
    doubling.step(2)
    step(low, PROJ, 2)
    step(low, KEY, 1)
    finish(low, DOWN)
    finish(top, VALUE)
    step(low, VALUE, 1)
    step(low, KEY, 2)
    finish(low, QUERY)
    step(low, VALUE, 2)
    finish(low, UP)
    doubling.step(3)
    finish(low, PROJ)
    finish(low, KEY)
    finish(low, VALUE)
    doubling.step(4)
    grad_small[...] = sums[...]
    grad_return.wait()
    for name in TENSORS:
        hand_out(low, name).wait()
    for red in reductions.values():
        red.drain()
    for gather in [mark_gather] + h_gathers + log_gathers + do_gathers:
        gather.drain()
    for one in error_swaps + mixed_swaps + normed_swaps + acts_swaps[low] + acts_swaps[top]:
        one.drain()


def encoder_call(patches, cotangent, keep, coords, norms, freqs, whole):
    layers = freqs.shape[0]
    rows, width = patches.shape
    hidden = whole[4].shape[2]
    size, quarter = width // 8, width // 4
    plans = tile_plan(width, hidden)
    tensors = plans * layers
    sem = pltpu.SemaphoreType.DMA
    any_spec, vmem_spec = pl.BlockSpec(memory_space=pl.ANY), pl.BlockSpec(memory_space=pltpu.VMEM)
    finals = [(hidden // 8, quarter), (size, hidden // 4)] + [(size, quarter)] * 4
    outs = (
        [jax.ShapeDtypeStruct((rows, width), BF16)] * 2
        + [jax.ShapeDtypeStruct((layers,) + shape, F32) for shape in finals]
        + [jax.ShapeDtypeStruct((8 * layers, width), F32)]
        + [jax.ShapeDtypeStruct(*shape) for shape in spilled_shapes(rows, width, hidden)]
    )

    def low(*shape):
        return pltpu.VMEM(shape, BF16)

    def full(*shape):
        return pltpu.VMEM(shape, F32)

    return pl.pallas_call(
        lambda *refs: encoder_kernel(layers, *refs),
        out_shape=outs,
        in_specs=[any_spec, any_spec] + [vmem_spec] * 7 + [any_spec] * 6,
        out_specs=[any_spec] * 8 + [vmem_spec] + [any_spec] * 5,
        scratch_shapes=[pltpu.VMEM(*shape) for shape in spilled_shapes(rows, width, hidden)]
        + [low(8 * n, count, LANES) for n, count in tensors]
        + [low(landing_count(n), count, LANES) for n, count in tensors]
        + [low(4 * n, count, LANES) for n, count in plans]
        + [full(*shape) for shape in finals]
        + [low(width, 3 * width), low(width, width), low(width, hidden), low(hidden, width)]
        + [sem((6,)), sem((5,)), sem((5,)), sem((6,))]
        + [
            low(layers, 4, rows, width),
            low(layers, 4, rows, LANES),
            low(layers, 2, rows, width),
            low(layers, 2, rows, width),
            low(layers, 2, 4, rows, hidden // 8),
            low(layers, 4, rows, hidden // 8),
            low(layers, rows, width),
            low(layers, rows, width),
            full(layers, rows, LANES),
        ]
        + [low(rows, width), low(rows, LANES), low(4, rows, LANES), low(rows, width), sem((5, 3))]
        + [sem((layers, 4))] * 6
        + [sem((4,))] * 2
        + [
            low(layers, 4, rows, width + LANES),
            low(layers, rows, width),
            low(layers, 2, 2, rows, width),
            low(layers, 2, rows, width),
            low(layers, rows, width // 2),
            low(rows, 3 * width),
            low(3, 2, rows, width // 2),
            low(layers, 3, rows, width // 2),
        ]
        + [sem((layers, 10, 2)), sem((len(tensors), 5)), sem((len(tensors), 5))]
        + [pltpu.SemaphoreType.REGULAR((len(plans),))]
        + [full(rows, width), full(8 * layers, width), full(5, 8 * layers, width), sem((5, 2))],
        compiler_params=pltpu.CompilerParams(
            collective_id=0, has_side_effects=True, vmem_limit_bytes=VMEM_BYTES
        ),
    )(patches, cotangent, keep, coords, *norms, freqs, *whole)


def beyond_eight(result):
    dp_size = lax.axis_size(DP)
    groups = dp_size // 8
    if groups == 1:
        return result
    result = lax.psum(result, DP, axis_index_groups=[[g * 8 + i for g in range(groups)] for i in range(8)])
    whole = lax.all_gather(
        result, DP, axis=1, tiled=True, axis_index_groups=[[g * 8 + i for i in range(8)] for g in range(groups)]
    )
    rows = whole.shape[1] // dp_size
    return lax.dynamic_slice_in_dim(whole, lax.axis_index(DP) * rows, rows, axis=1)


def final_kernel(count, *refs):
    output, grad_patches, small = refs[:3]
    large = refs[3 : 3 + count]
    refs = refs[3 + count :]
    out_copy, grad_copy = refs[:2]
    large_copies = refs[2 : 2 + count]
    norms, turns = refs[2 + count : 6 + count], refs[6 + count]
    out_copy[...] = output[...]
    grad_copy[...] = grad_patches[...].astype(F32)
    for source, target in zip(large[:-1], large_copies[:-1]):
        target[...] = source[...]
    layers, columns = norms[0].shape
    for layer_no in range(layers):
        large_copies[-1][layer_no] = large[-1][layer_no].T
    at = lax.axis_index(BLK)
    half = turns.shape[3]
    for blk in range(small.shape[1] // columns):

        @pl.when(at == blk)
        def _(blk=blk):
            for layer_no in range(layers):
                mine = small[8 * layer_no : 8 * layer_no + 8, blk * columns : blk * columns + columns]
                for row, norm in enumerate(norms):
                    norm[layer_no : layer_no + 1] = mine[row : row + 1]
                for row in range(2):
                    for head in range(turns.shape[1]):
                        pair = mine[4 + row : 5 + row, 2 * half * head : 2 * half * head + 2 * half]
                        turns[layer_no, head, row : row + 1] = pair[:, half:] - pair[:, :half]


def final_call(output, grad_patches, small, large, half):
    vmem_spec = pl.BlockSpec(memory_space=pltpu.VMEM)
    layers = small.shape[0] // 8
    columns = small.shape[1] // lax.axis_size(BLK)
    return pl.pallas_call(
        lambda *refs: final_kernel(len(large), *refs),
        out_shape=[
            jax.ShapeDtypeStruct(output.shape, output.dtype),
            jax.ShapeDtypeStruct(grad_patches.shape, F32),
        ]
        + [jax.ShapeDtypeStruct(a.shape, F32) for a in large[:-1]]
        + [jax.ShapeDtypeStruct((layers,) + large[-1].shape[:0:-1], F32)]
        + [jax.ShapeDtypeStruct((layers, columns), F32)] * 4
        + [jax.ShapeDtypeStruct((layers, columns // (2 * half), 2, half), F32)],
        in_specs=[vmem_spec] * (3 + len(large)),
        out_specs=[vmem_spec] * (7 + len(large)),
    )(output, grad_patches, small, *large)


def shards(
    patches,
    keep,
    coords,
    query_w,
    key_w,
    value_w,
    proj_w,
    up_w,
    down_w,
    norm1_gain,
    norm1_bias,
    norm2_gain,
    norm2_bias,
    freqs,
    cotangent,
):
    whole = (query_w, key_w, value_w, proj_w, up_w, down_w)
    norms = (norm1_gain, norm1_bias, norm2_gain, norm2_bias)
    results = encoder_call(patches[0], cotangent[0], keep, coords, norms, jnp.swapaxes(freqs, 1, 2), whole)
    output, grad_patches, grad_down, grad_up, *others, small = results[:9]
    large = [beyond_eight(grad) for grad in (*others[1:], others[0], grad_up, grad_down)]
    groups = lax.axis_size(DP) // 8
    if groups > 1:
        small = lax.psum(small, DP, axis_index_groups=[[g * 8 + i for g in range(groups)] for i in range(8)])
    output, grad_patches, *rest = final_call(output, grad_patches, small, large, freqs.shape[3])
    rest[5], rest[-1] = jnp.swapaxes(rest[5], 1, 2), jnp.swapaxes(rest[-1], 1, 2)
    return (output[None], grad_patches[None], *rest)


def solution(mesh):
    block = P(DP, BLK, None)
    placed = (block, P(DP, BLK), P(None, DP, BLK)) + (P(),) * 11 + (block,)
    results = (block, block) + (P(None, DP, BLK),) * 6 + (P(None, BLK),) * 4 + (P(None, None, BLK, None),)
    return jax.shard_map(shards, mesh=mesh, in_specs=placed, out_specs=results, check_vma=False)
```

```python
import jax
import jax.numpy as jnp
from jax import lax
from jax.experimental import pallas as pl
from jax.experimental.pallas import tpu as pltpu
from jax.sharding import PartitionSpec as P

MESH = pl.DeviceIdType.MESH
DP, BLK = "dp", "blk"
C, X, Y, Z0, Z1 = range(5)
BF16, F32 = jnp.bfloat16, jnp.float32
MASKED_SCORE = -1e30
NORM_EPSILON = 1e-06
LANES = 128
SCALE_LANE = 64
VMEM_BYTES = 127 * 512 * 1024


def rows_by_columns(left, right):
    return lax.dot_general(left, right, (((1,), (0,)), ((), ())), preferred_element_type=F32)


def rows_by_rows(left, right):
    return lax.dot_general(left, right, (((1,), (1,)), ((), ())), preferred_element_type=F32)


def columns_by_columns(left, right):
    return lax.dot_general(left, right, (((0,), (0,)), ((), ())), preferred_element_type=F32)


class Place:
    def __init__(self):
        self.dp = lax.axis_index(DP)
        self.blk = lax.axis_index(BLK)
        self.c = lax.rem(self.dp, 2)
        self.x = lax.rem(self.dp // 2, 2)
        self.y = lax.rem(self.dp // 4, 2)
        self.z0 = lax.rem(self.blk, 2)
        self.z1 = lax.rem(self.blk // 2, 2)
        self.bits = (self.c, self.x, self.y, self.z0, self.z1)
        self.worker = (self.dp - self.c + self.z0, 2 * self.c + self.z1)
        self.owner = (self.dp - self.c + self.z1, 2 * self.z0 + self.c)
        self.stays = (self.worker[0] == self.dp) & (self.worker[1] == self.blk)

    def other(self, axis):
        if axis <= Y:
            return (self.dp + (1 << axis) * (1 - 2 * self.bits[axis]), self.blk)
        return (self.dp, self.blk + (1 << axis - Z0) * (1 - 2 * self.bits[axis]))

    def greet(self, axes):
        barrier = pltpu.get_barrier_semaphore()
        mine = 2 * self.blk + self.c
        for step in range(1, 8):
            them = lax.rem(mine + step, 8)
            pl.semaphore_signal(
                barrier, inc=1, device_id=(self.dp - self.c + lax.rem(them, 2), them // 2), device_id_type=MESH
            )
        for axis in axes:
            pl.semaphore_signal(barrier, inc=1, device_id=self.other(axis), device_id_type=MESH)
        pl.semaphore_wait(barrier, 7 + len(axes))


class Relocation:
    def __init__(self, place, source, target, sems, back=False):
        self.place, self.source, self.target, self.sems = place, source, target, sems
        self.device = place.owner if back else place.worker

    def remote(self):
        return pltpu.make_async_remote_copy(
            src_ref=self.source,
            dst_ref=self.target,
            send_sem=self.sems.at[0],
            recv_sem=self.sems.at[1],
            device_id=self.device,
            device_id_type=MESH,
        )

    def local(self):
        return pltpu.make_async_copy(self.source, self.target, self.sems.at[2])

    def start(self):
        pl.when(self.place.stays)(lambda: self.local().start())
        pl.when(jnp.logical_not(self.place.stays))(lambda: self.remote().start())

    def wait(self):
        pl.when(self.place.stays)(lambda: self.local().wait())
        pl.when(jnp.logical_not(self.place.stays))(lambda: self.remote().wait())


class Gather:
    def __init__(self, place, slots, sends, receives):
        self.place, self.slots, self.sends, self.receives = place, slots, sends, receives

    def copy(self, source, slot, axis):
        return pltpu.make_async_remote_copy(
            src_ref=self.slots.at[source],
            dst_ref=self.slots.at[slot],
            send_sem=self.sends.at[slot],
            recv_sem=self.receives.at[slot],
            device_id=self.place.other(axis),
            device_id_type=MESH,
        )

    def start(self):
        self.copy(0, 2, Z0).start()
        self.copy(0, 1, C).start()

    def near(self):
        self.copy(0, 1, C).wait_recv()

    def far(self):
        self.copy(0, 2, Z0).wait_recv()
        self.copy(2, 3, C).start()

    def last(self):
        self.copy(2, 3, C).wait_recv()

    def drain(self):
        self.copy(0, 1, C).wait_send()
        self.copy(0, 2, Z0).wait_send()
        self.copy(2, 3, C).wait_send()


class Swap:
    def __init__(self, place, axis, source, target, sems):
        self.place, self.axis, self.source, self.target, self.sems = place, axis, source, target, sems

    def copy(self):
        return pltpu.make_async_remote_copy(
            src_ref=self.source,
            dst_ref=self.target,
            send_sem=self.sems.at[0],
            recv_sem=self.sems.at[1],
            device_id=self.place.other(self.axis),
            device_id_type=MESH,
        )

    def start(self):
        self.copy().start()

    def arrive(self):
        self.copy().wait_recv()

    def drain(self):
        self.copy().wait_send()


def lane_index(rows):
    return lax.broadcasted_iota(jnp.int32, (rows, LANES), 1)


def partner_tile(tile, former):
    return jnp.where(former, pltpu.roll(tile, 96, 1), pltpu.roll(tile, 32, 1))


def rotate_tile(tile, cosine, signed_sine, former):
    return tile * cosine + partner_tile(tile, former) * signed_sine


def tile_of(index):
    return slice(LANES * index, LANES * index + LANES)


def normalise(values):
    centre = values - jnp.mean(values, axis=-1, keepdims=True)
    spread = jnp.mean(centre * centre, axis=-1, keepdims=True)
    scale = lax.rsqrt(spread + NORM_EPSILON)
    return centre * scale, scale


QUERY_W, KEY_W, VALUE_W, PROJ_W, UP_W, DOWN_W = range(6)


class Weights:
    def __init__(self, whole, qkv, proj, up, down, sems):
        width = qkv.shape[1] // 3
        self.whole, self.sems = whole, sems
        self.buffers = [qkv.at[:, pl.ds(part * width, width)] for part in range(3)] + [proj, up, down]

    def copy(self, name, layer_no):
        return pltpu.make_async_copy(self.whole[name].at[layer_no], self.buffers[name], self.sems.at[name])

    def load(self, layer_no, *names):
        for name in names:
            self.copy(name, layer_no).start()

    def ready(self, layer_no, *names):
        for name in names:
            self.copy(name, layer_no).wait()


def spread_lanes(columns, lane, last):
    columns = jnp.where(lane < 16, columns, 0.0)
    high = columns.astype(BF16).astype(F32)
    middle = (columns - high).astype(BF16).astype(F32)
    low = columns - high - middle
    spread = high + pltpu.roll(middle, 16, 1) + pltpu.roll(low, 32, 1)
    return jnp.where(lane == 127, last, spread)


class Reduction:
    def __init__(self, place, axes, n, share, first_landing, landing, sends, receives, credit, gives, takes):
        self.place, self.axes = place, axes + (Z1, Z1)
        self.share, self.first_landing, self.landing = share, first_landing, landing
        self.sends, self.receives = sends, receives
        self.credit, self.gives, self.takes = credit, gives, takes
        self.n, self.rows = n, share.shape[1]
        self.plan = []
        base, half, land = 0, 4 * n, 0
        for axis in axes:
            bit = place.bits[axis]
            self.plan.append((base + (1 - bit) * half, base + bit * half, half, land))
            base, land, half = base + bit * half, land + half if self.plan[1:] else 0, half // 2
        self.spare = self.plan[0][0]
        self.base, self.land = base, land
        self.plan.append((base + (n - 1) * (1 - place.z1), base + (n - 1) * place.z1, 1, land))

    def copy(self, stage):
        if stage < 4:
            send, _, count, land = self.plan[stage]
            landing = self.first_landing if stage == 0 else self.landing
            source, target = self.share.at[pl.ds(send, count)], landing.at[pl.ds(land, count)]
        else:
            half = pl.ds(0, self.rows // 2)
            source, target = self.share.at[self.spare, half], self.landing.at[self.land + 1, half]
        return pltpu.make_async_remote_copy(
            src_ref=source,
            dst_ref=target,
            send_sem=self.sends.at[stage],
            recv_sem=self.receives.at[stage],
            device_id=self.place.other(self.axes[stage]),
            device_id_type=MESH,
        )

    def start(self, stage=0):
        if stage == 0 and self.takes:
            pl.semaphore_wait(self.credit, 1)
        self.copy(stage).start()

    def step(self, stage):
        _, keep, count, land = self.plan[stage]
        self.copy(stage).wait_recv()

        landing = self.first_landing if stage == 0 else self.landing

        def body(i, carry):
            self.share[keep + i] = self.share[keep + i] + landing[land + i]
            return carry

        lax.fori_loop(0, count, body, 0)
        self.start(stage + 1)
        if stage == 0:
            self.copy(0).wait_send()
            if self.gives:
                pl.semaphore_signal(self.credit, inc=1, device_id=self.place.other(C), device_id_type=MESH)
        if stage == 2 and self.n == 3:
            half = self.rows // 2
            shared = self.share[self.base + 1].astype(F32)
            upper, lower = shared[:half], shared[half:]
            first = lane_index(half) < 64
            low_lanes = jnp.where(first, upper, pltpu.roll(lower, 64, 1))
            high_lanes = jnp.where(first, pltpu.roll(upper, 64, 1), lower)
            self.share[self.spare, :half] = jnp.where(self.place.z1 == 1, low_lanes, high_lanes).astype(BF16)
            self.start(4)

    def finish(self, write):
        self.copy(3).wait_recv()
        _, keep, _, land = self.plan[3]
        own = self.share[keep].astype(F32) + self.landing[land].astype(F32)
        if self.n == 2:
            write(own)
            return
        self.copy(4).wait_recv()
        half = self.rows // 2
        packed = self.landing[self.land + 1, :half].astype(F32)
        shared = self.share[self.base + 1].astype(F32)
        shared = jnp.where(self.place.z1 == 0, shared, pltpu.roll(shared, 64, 1))
        rest = shared + jnp.concatenate([packed, pltpu.roll(packed, 64, 1)], axis=0)
        write(own, rest[:, :64])

    def drain(self):
        for stage in range(1, 4 if self.n == 2 else 5):
            self.copy(stage).wait_send()


class Doubling:
    AXES = (C, X, Y, Z0, Z1)

    def __init__(self, place, sums, landing, sems):
        self.place, self.sums, self.landing, self.sems = place, sums, landing, sems

    def copy(self, stage):
        return pltpu.make_async_remote_copy(
            src_ref=self.sums,
            dst_ref=self.landing.at[stage],
            send_sem=self.sems.at[stage, 0],
            recv_sem=self.sems.at[stage, 1],
            device_id=self.place.other(self.AXES[stage]),
            device_id_type=MESH,
        )

    def start(self):
        self.copy(0).start()

    def step(self, stage):
        self.copy(stage).wait()
        self.sums[...] += self.landing[stage]
        if stage + 1 < len(self.AXES):
            self.copy(stage + 1).start()


TENSORS = DOWN_A, DOWN_B, UP_A, UP_B, PROJ, QUERY, KEY, VALUE = range(8)
HALVING = ((C, Y, Z0),) * 2 + ((C, X, Y),) * 3 + ((C, Y, X), (C, X, Y), (C, Y, X))


def tile_plan(width, hidden):
    size = width // 8
    return ((3, hidden // 16),) * 2 + ((2, size * (hidden // 8 // LANES)),) * 2 + ((3, size),) * 4


def landing_count(n):
    return 2 * n + n + n - 1


def by_halves(tiles, first):
    def turned(tile):
        return pltpu.roll(tile, 64, 1)

    return (
        (tiles[0], jnp.where(first, tiles[1], turned(tiles[4])), tiles[3]),
        (
            jnp.where(first, turned(tiles[1]), turned(tiles[2])),
            jnp.where(first, turned(tiles[2]), tiles[5]),
            jnp.where(first, turned(tiles[4]), turned(tiles[5])),
        ),
    )


KEYS, VALUES, QUERIES, ANGLES, SLOPES = SPILLED = range(5)


def spilled_shapes(rows, width, hidden):
    return (
        ((4, rows, width), BF16),
        ((4, rows, width), BF16),
        ((4, rows, width), BF16),
        ((2, rows, width), F32),
        ((rows, hidden), BF16),
    )


def encoder_kernel(layers, *refs):
    patches, cotangent, keep, coords, gain1, bias1, gain2, bias2, freqs = refs[:9]
    whole = refs[9:15]
    output, grad_patches = refs[15:17]
    results = refs[17:23]
    grad_small = refs[23]
    saved = refs[24:29]
    held = refs[29:34]
    refs = refs[34:]
    count = layers * len(TENSORS)
    shares, landings, first_landings = refs[:count], refs[count : 2 * count], refs[2 * count : 2 * count + len(TENSORS)]
    refs = refs[2 * count + len(TENSORS) :]
    stagings = refs[: len(TENSORS)]
    refs = refs[len(TENSORS) :]
    (qkv_w, proj_w, up_w, down_w, w_sems, spill_sems, load_sems, stage_sems) = refs[:8]
    (normed, logs_low, mixed, normed2, acts, far_acts, hat1, hat2, stats) = refs[8:17]
    (start, own_marks, marks, returned, relocation_sems) = refs[17:22]
    (h_sends, h_receives, do_sends, do_receives, q_sends, q_receives, m_sends, m_receives) = refs[22:30]
    (douts, errors, grad_hidden, far_hidden, far_middle, grad_qkv, half_qkv, far_qkv) = refs[30:38]
    (swap_sems, sends, receives, credits, carried, sums, sums_landing, sums_sems) = refs[38:]
    place = Place()
    rows, width = carried.shape
    hidden = up_w.shape[1]
    half = hidden // 8
    size = width // 8
    pairs = width // LANES
    top, low = layers - 1, layers - 2
    weights = Weights(whole, qkv_w, proj_w, up_w, down_w, w_sems)
    weights.load(0, KEY_W, VALUE_W, QUERY_W, PROJ_W, UP_W, DOWN_W)
    line = lax.broadcasted_iota(jnp.int32, (LANES, rows), 0)
    own = jnp.where(line == 0, jnp.where(keep[...] > 0, 0.0, MASKED_SCORE), 0.0)
    for number in range(2):
        own = jnp.where(line == 1 + number, coords[number].astype(F32), own)
    own_marks[...] = own.T.astype(BF16)
    place.greet((X, Y))

    lane = lane_index(rows)
    former = lax.rem(lane, 64) < 32
    first_head = lane < 64
    heads_lanes = (first_head, jnp.logical_not(first_head))
    one_lane = jnp.where(lane == 0, 1.0, 0.0).astype(BF16)
    plans = tile_plan(width, hidden)
    away = 1 - place.z0

    def relocation(number, source, target, back=False):
        return Relocation(place, source, target, relocation_sems.at[number], back)

    def swap(layer_no, number, axis, source, target):
        return Swap(place, axis, source, target, swap_sems.at[layer_no, number])

    every = range(layers)

    def grad_middle(z0):
        return normed.at[top, 1, :, pl.ds(pl.multiple_of(z0 * (width // 2), LANES), width // 2)]

    mark_arrival = relocation(0, own_marks, marks.at[0])
    arrival = relocation(1, patches, start)
    other_arrival = relocation(2, cotangent, returned)
    out_return = relocation(3, start, output, True)
    grad_return = relocation(4, returned, grad_patches, True)
    mark_gather = Gather(place, marks, m_sends, m_receives)
    h_gathers = [Gather(place, normed.at[l], h_sends.at[l], h_receives.at[l]) for l in every]
    log_gathers = [Gather(place, logs_low.at[l], q_sends.at[l], q_receives.at[l]) for l in every]
    do_gathers = [Gather(place, douts.at[l], do_sends.at[l], do_receives.at[l]) for l in every]
    own_errors = [normed.at[0, 1 + 2 * l] for l in every]
    error_swaps = [swap(l, 0, X, own_errors[l], errors.at[l]) for l in every]
    hidden_swaps = [
        [
            swap(l, 1 + part, Z0, grad_hidden.at[l, away, :, :, columns], far_hidden.at[l, :, :, columns])
            for part, columns in enumerate((pl.ds(0, half), pl.ds(half, half)))
        ]
        for l in every
    ]
    middle_swaps = [swap(l, 3, Z0, grad_middle(away), far_middle.at[l]) for l in every]
    qkv_swaps = [[swap(l, 4 + part, Z0, half_qkv.at[part, away], far_qkv.at[l, part]) for part in range(3)] for l in every]
    mixed_swaps = [swap(l, 7, Z0, mixed.at[l, 0], mixed.at[l, 1]) for l in every]
    normed_swaps = [swap(l, 8, Z0, normed2.at[l, 0], normed2.at[l, 1]) for l in every]
    acts_swaps = [
        [
            swap(l, 9 + y, X, acts.at[l, 1 - place.x, pl.ds(2 * y, 2)], far_acts.at[l, pl.ds(2 * y, 2)])
            for y in range(2)
        ]
        for l in every
    ]
    doubling = Doubling(place, sums, sums_landing, sums_sems)
    reductions = {}
    for layer_no in every:
        for name in TENSORS:
            at = layer_no * len(TENSORS) + name
            reductions[layer_no, name] = Reduction(
                place,
                HALVING[name],
                plans[name][0],
                shares[at],
                first_landings[name],
                landings[at],
                sends.at[at],
                receives.at[at],
                credits.at[name],
                layer_no > 0,
                layer_no < top,
            )

    def spill(name):
        return pltpu.make_async_copy(held[name], saved[name], spill_sems.at[name])

    def loading(name):
        return pltpu.make_async_copy(saved[name], held[name], load_sems.at[name])

    def load(layer_no, *names):
        for name in names:
            loading(name).start()

    def ready(layer_no, *names):
        if layer_no < top:
            for name in names:
                loading(name).wait()


    def freq_tile(layer_no, which, index):
        return jnp.concatenate(
            [freqs[layer_no, 4 * index + member, which : which + 1] for member in range(4)], axis=1
        )

    def twice(tile):
        once, half_way, back = (pltpu.roll(tile, shift, 1) for shift in (32, 64, 96))
        quarter, last = lane < 32, lane >= 96
        return (
            jnp.where(quarter, tile, jnp.where(last, half_way, once)),
            jnp.where(quarter, half_way, jnp.where(last, tile, back)),
        )

    def angle_refs(slot):
        if slot == 0:
            return held[ANGLES].at[0], held[ANGLES].at[1]
        return grad_hidden.at[0, slot // 2, slot % 2], grad_hidden.at[1, slot // 2, slot % 2]

    def make_angles(layer_no, slot):
        rows_at = marks[slot][:, 1:2].astype(F32)
        columns_at = marks[slot][:, 2:3].astype(F32)
        cosine, sine = angle_refs(slot)
        sign = jnp.where(former, -1.0, 1.0)
        for index in range(pairs // 2):
            angle = rows_at * freq_tile(layer_no, 0, index) + columns_at * freq_tile(layer_no, 1, index)
            for member, (even, odd) in enumerate(zip(twice(jnp.cos(angle)), twice(jnp.sin(angle)))):
                cosine[:, tile_of(2 * index + member)] = even.astype(cosine.dtype)
                sine[:, tile_of(2 * index + member)] = (sign * odd).astype(sine.dtype)

    def project(layer_no, slot):
        cosine, sine = angle_refs(slot)
        block = normed[layer_no, slot]
        for name, part, scale in ((QUERIES, 0, 0.125), (KEYS, 1, 1.0)):
            products = rows_by_columns(block, qkv_w[:, part * width : part * width + width])
            for index in range(pairs):
                sl = tile_of(index)
                turned = rotate_tile(products[:, sl], cosine[:, sl].astype(F32), sine[:, sl].astype(F32), former)
                held[name][slot, :, sl] = (scale * turned).astype(BF16)
        held[VALUES][slot] = rows_by_columns(block, qkv_w[:, 2 * width :]).astype(BF16)

    def normalise_first(layer_no):
        hat, scale = normalise(carried[...])
        hat1[layer_no] = hat.astype(BF16)
        stats[layer_no] = jnp.where(lane == SCALE_LANE, scale, 0.0)
        normed[layer_no, 0] = (hat * gain1[layer_no : layer_no + 1] + bias1[layer_no : layer_no + 1]).astype(BF16)
        h_gathers[layer_no].start()

    def attend(layer_no):
        marks_of_keys = marks[...].reshape(4 * rows, LANES)
        sums_of_rows = jnp.zeros((rows, LANES), F32)
        for index in range(pairs):
            sl = tile_of(index)
            query_pair = held[QUERIES][0, :, sl]
            key_pair = held[KEYS][:, :, sl].reshape(4 * rows, LANES)
            value_pair = held[VALUES][:, :, sl].reshape(4 * rows, LANES)
            extended = jnp.concatenate([key_pair, marks_of_keys], axis=1)
            parts = []
            for member, mine in enumerate(heads_lanes):
                query = jnp.where(mine, query_pair, jnp.zeros_like(query_pair))
                scores = rows_by_rows(jnp.concatenate([query, one_lane], axis=1), extended)
                highest = jnp.max(scores, axis=1, keepdims=True)
                weight = jnp.exp(scores - highest)
                total = jnp.sum(weight, axis=1, keepdims=True)
                parts.append(rows_by_columns(weight.astype(BF16), value_pair) / total)
                sums_of_rows = jnp.where(lane == 2 * index + member, highest + jnp.log(total), sums_of_rows)
            mixed[layer_no, 0, :, sl] = jnp.where(first_head, parts[0], parts[1]).astype(BF16)
        stats[layer_no] = jnp.where(lane < 16, sums_of_rows, stats[layer_no])
        logs_low[layer_no, 0] = spread_lanes(-sums_of_rows, lane, 1.0).astype(BF16)

    def project_out(layer_no):
        weights.ready(layer_no, PROJ_W)
        middle = carried[...] + rows_by_columns(mixed[layer_no, 0], proj_w[...])
        carried[...] = middle
        if layer_no < top:
            weights.load(layer_no + 1, PROJ_W)
        hat, scale = normalise(middle)
        hat2[layer_no] = hat.astype(BF16)
        stats[layer_no] = jnp.where(lane == SCALE_LANE + 1, scale, stats[layer_no])
        normed2[layer_no, 0] = (hat * gain2[layer_no : layer_no + 1] + bias2[layer_no : layer_no + 1]).astype(BF16)

    def quarter_of(quarter):
        return slice(2 * half * quarter, 2 * half * quarter + 2 * half)

    def feed_forward(layer_no, quarter):
        if quarter == 0:
            weights.ready(layer_no, UP_W)
        columns = quarter_of(quarter)
        hidden_part = rows_by_columns(normed2[layer_no, 0], up_w[:, columns])
        share = 0.5 + 0.5 * lax.erf(hidden_part * 0.7071067811865476)
        active = (hidden_part * share).astype(BF16)
        slope = share + hidden_part * (0.3989422804014327 * jnp.exp(-0.5 * hidden_part * hidden_part))
        held[SLOPES][:, columns] = slope.astype(BF16)
        y, x = quarter // 2, quarter % 2
        acts[layer_no, x, 2 * y] = active[:, :half]
        acts[layer_no, x, 2 * y + 1] = active[:, half:]
        if quarter == 0:
            weights.ready(layer_no, DOWN_W)
        carried[...] += rows_by_columns(active, down_w[columns, :])


    def note(layer_no, row, values):
        sums[8 * layer_no + row : 8 * layer_no + row + 1] = jnp.sum(values, axis=0, keepdims=True)

    def norm_back(layer_no, number, grad, hat, scale):
        note(layer_no, 2 * number, grad * hat)
        note(layer_no, 2 * number + 1, grad)
        grad = grad * (gain1, gain2)[number][layer_no : layer_no + 1]
        mean = jnp.mean(grad, axis=-1, keepdims=True)
        slope = jnp.mean(grad * hat, axis=-1, keepdims=True)
        return scale * (grad - mean - hat * slope)

    def halves_of(values):
        return by_halves([values[:, tile_of(i)] for i in range(pairs)], first_head)

    def send_error(layer_no, values):
        for z0, tiles in enumerate(halves_of(values)):
            for i, tile in enumerate(tiles):
                own_errors[layer_no][:, tile_of(3 * z0 + i)] = tile.astype(BF16)
        error_swaps[layer_no].start()

    def hidden_back(layer_no):
        error = carried[...].astype(BF16)
        if layer_no < top:
            weights.ready(layer_no, DOWN_W)
        ready(layer_no, SLOPES)
        for quarter in range(4):
            grad = rows_by_rows(error, down_w[quarter_of(quarter), :])
            grad = grad * held[SLOPES][:, quarter_of(quarter)].astype(F32)
            grad_hidden[layer_no, quarter % 2, quarter // 2] = grad.astype(BF16)
        if layer_no > 0:
            weights.load(layer_no - 1, DOWN_W)
            load(layer_no - 1, SLOPES)

    def middle_back(layer_no):
        if layer_no < top:
            weights.ready(layer_no, UP_W)
        total = jnp.zeros((rows, width), F32)
        for quarter in range(4):
            total = total + rows_by_rows(grad_hidden[layer_no, quarter % 2, quarter // 2], up_w[:, quarter_of(quarter)])
        if layer_no > 0:
            weights.load(layer_no - 1, UP_W)
        carried[...] += norm_back(layer_no, 1, total, hat2[layer_no].astype(F32), stats[layer_no][:, SCALE_LANE + 1 : SCALE_LANE + 2])

    def project_back(layer_no):
        if layer_no < top:
            weights.ready(layer_no, PROJ_W)
        grad = rows_by_rows(carried[...].astype(BF16), proj_w[...])
        if layer_no > 0:
            weights.load(layer_no - 1, PROJ_W)
        deltas = jnp.zeros((rows, LANES), F32)
        for index in range(pairs):
            sl = tile_of(index)
            low_grad = grad[:, sl].astype(BF16)
            douts[layer_no, 0, :, sl] = low_grad
            product = low_grad.astype(F32) * mixed[layer_no, 0, :, sl].astype(F32)
            for member, mine in enumerate(heads_lanes):
                delta = jnp.sum(jnp.where(mine, product, 0.0), axis=1, keepdims=True)
                deltas = jnp.where(lane == 2 * index + member, delta, deltas)
        douts[layer_no, 0, :, width:] = spread_lanes(-deltas, lane, 0.0).astype(BF16)
        do_gathers[layer_no].start()
        kept_deltas.append(deltas)

    kept_deltas = []

    def middle_send(layer_no):
        for z0, tiles in enumerate(halves_of(carried[...])):
            for i, tile in enumerate(tiles):
                grad_middle(z0)[:, tile_of(i)] = tile.astype(BF16)
        middle_swaps[layer_no].start()

    def turned_back(layer_no, part, index, grad, forward):
        sl = tile_of(index)
        back = grad * held[ANGLES][0, :, sl] - partner_tile(grad, former) * held[ANGLES][1, :, sl]
        grad_qkv[:, part * width + LANES * index : part * width + LANES * index + LANES] = back.astype(BF16)
        return back, grad * partner_tile(forward.astype(F32), former)

    def note_turn(layer_no, index, turn, first):
        for row in range(2):
            at = 8 * layer_no + 4 + row
            total = jnp.sum(turn * marks[0][:, 1 + row : 2 + row].astype(F32), axis=0, keepdims=True)
            if not first:
                total = total + sums[at : at + 1, tile_of(index)]
            sums[at : at + 1, tile_of(index)] = total

    def split_half(part, tiles):
        for z0, group in enumerate(by_halves(tiles, first_head)):
            for i, tile in enumerate(group):
                half_qkv[part, z0, :, tile_of(i)] = tile.astype(BF16)

    def own_queries(layer_no):
        ready(layer_no, KEYS, VALUES, ANGLES, QUERIES)
        deltas = kept_deltas[-1]
        key_marks = marks[...].reshape(4 * rows, LANES)
        backs = []
        for index in range(pairs):
            sl = tile_of(index)
            query_pair = held[QUERIES][0, :, sl]
            key_pair = held[KEYS][:, :, sl].reshape(4 * rows, LANES)
            value_pair = held[VALUES][:, :, sl].reshape(4 * rows, LANES)
            grad_pair = douts[layer_no, 0, :, sl]
            extended = jnp.concatenate([key_pair, key_marks], axis=1)
            parts = []
            for member, mine in enumerate(heads_lanes):
                head = 2 * index + member
                zero = jnp.zeros_like(query_pair)
                scores = rows_by_rows(
                    jnp.concatenate([jnp.where(mine, query_pair, zero), one_lane], axis=1), extended
                )
                weight = jnp.exp(scores - stats[layer_no][:, head : head + 1])
                grad = rows_by_rows(jnp.where(mine, grad_pair, zero), value_pair)
                grad = (weight * (grad - deltas[:, head : head + 1])).astype(BF16)
                parts.append(rows_by_columns(grad, key_pair))
            grad = 0.125 * jnp.where(first_head, parts[0], parts[1])
            back, turn = turned_back(layer_no, 0, index, grad, 8.0 * query_pair.astype(F32))
            note_turn(layer_no, index, turn, True)
            backs.append(back)
        split_half(0, backs)

    def own_keys(layer_no):
        do_gathers[layer_no].near()
        do_gathers[layer_no].last()
        if layer_no == top:
            log_gathers[layer_no].near()
            log_gathers[layer_no].last()
        own_marks = marks[0]
        key_backs, value_backs = [], []
        for index in range(pairs):
            sl = tile_of(index)
            key_pair, value_pair = held[KEYS][0, :, sl], held[VALUES][0, :, sl]
            query_pair = held[QUERIES][:, :, sl].reshape(4 * rows, LANES)
            grad_pair = douts[layer_no, :, :, sl].reshape(4 * rows, LANES)
            queries = jnp.concatenate([query_pair, logs_low[layer_no].reshape(4 * rows, LANES)], axis=1)
            grads = jnp.concatenate([grad_pair, douts[layer_no, :, :, width:].reshape(4 * rows, LANES)], axis=1)
            key_parts, value_parts = [], []
            for member, mine in enumerate(heads_lanes):
                head = 2 * index + member
                zero = jnp.zeros_like(key_pair)
                chosen = jnp.where((lane < 48) & (lax.rem(lane, 16) == head), 1.0, 0.0).astype(BF16)
                marked = jnp.where(lane == 127, jnp.broadcast_to(own_marks[:, 0:1], chosen.shape), chosen)
                weight = jnp.exp(
                    rows_by_rows(jnp.concatenate([jnp.where(mine, key_pair, zero), marked], axis=1), queries)
                )
                grad = rows_by_rows(jnp.concatenate([jnp.where(mine, value_pair, zero), chosen], axis=1), grads)
                grad = (weight * grad).astype(BF16)
                key_parts.append(rows_by_columns(grad, query_pair))
                value_parts.append(rows_by_columns(weight.astype(BF16), grad_pair))
            grad = jnp.where(first_head, key_parts[0], key_parts[1])
            back, turn = turned_back(layer_no, 1, index, grad, key_pair)
            note_turn(layer_no, index, turn, False)
            key_backs.append(back)
            grad = jnp.where(first_head, value_parts[0], value_parts[1])
            grad_qkv[:, 2 * width + LANES * index : 2 * width + LANES * index + LANES] = grad.astype(BF16)
            value_backs.append(grad)
        split_half(1, key_backs)
        split_half(2, value_backs)
        if layer_no > 0:
            load(layer_no - 1, KEYS, VALUES, ANGLES, QUERIES)

    def input_back(layer_no):
        if layer_no < top:
            weights.ready(layer_no, QUERY_W, KEY_W, VALUE_W)
        total = rows_by_rows(grad_qkv[...], qkv_w[...])
        if layer_no > 0:
            weights.load(layer_no - 1, QUERY_W, KEY_W, VALUE_W)
        carried[...] += norm_back(layer_no, 0, total, hat1[layer_no].astype(F32), stats[layer_no][:, SCALE_LANE : SCALE_LANE + 1])
        if layer_no > 0:
            send_error(layer_no - 1, carried[...])

    def put(layer_no, name, values, column, blocks, skipped=0):
        share = reductions[layer_no, name].share
        for first_row, count, tile in blocks:
            for i in range(values.shape[1] // LANES):
                piece = values[first_row - skipped : first_row - skipped + count, tile_of(i)].astype(BF16)
                at_tile, at_row = column(tile, i)
                share[at_tile, at_row : at_row + count] = piece

    def blocks_of(name):
        n, axes = plans[name][0], HALVING[name]
        blocks = []
        for number in range(8):
            bits = (number % 2, (number // 2) % 2, number // 4)
            tile = ((bits[axes[0]] * 2 + bits[axes[1]]) * 2 + bits[axes[2]]) * n
            blocks.append((number * size, size, tile))
        return blocks

    def down_product(layer_no):
        error_swaps[layer_no].arrive()
        if layer_no == top:
            for part in acts_swaps[layer_no]:
                part.arrive()
        for y in range(2):
            for c in range(2):
                for z0 in range(2):
                    columns = slice(z0 * width // 2, (z0 + 1) * width // 2)
                    product = columns_by_columns(
                        acts[layer_no, place.x, 2 * y + c], own_errors[layer_no][:, columns]
                    ) + columns_by_columns(far_acts[layer_no, 2 * y + c], errors[layer_no, :, columns])
                    tile = ((2 * c + y) * 2 + z0) * 3
                    for part in range(2):
                        block = (half // 2 * part, half // 2, tile)
                        put(layer_no, DOWN_A + part, product, lambda tile, i: (tile + i, 0), [block])
        reductions[layer_no, DOWN_A].start()
        reductions[layer_no, DOWN_B].start()

    def up_product(layer_no, part):
        hidden_swaps[layer_no][part].arrive()
        if layer_no == top and part == 0:
            normed_swaps[layer_no].arrive()
        columns = pl.ds(half * part, half)
        for z1 in range(2):
            for side in range(2):
                inputs = slice(side * 4 * size, side * 4 * size + 4 * size)
                product = columns_by_columns(
                    normed2[layer_no, 0, :, inputs], grad_hidden[layer_no, place.z0, z1, :, columns]
                ) + columns_by_columns(normed2[layer_no, 1, :, inputs], far_hidden[layer_no, z1, :, columns])
                put(
                    layer_no,
                    UP_A + part,
                    product,
                    lambda tile, i: (tile + z1, size * i),
                    blocks_of(UP_A + part)[4 * side : 4 * side + 4],
                    4 * size * side,
                )
        reductions[layer_no, UP_A + part].start()
        hidden_swaps[layer_no][part].drain()

    def narrow_product(layer_no, name, left, right, far):
        blocks = blocks_of(name)
        for side in range(2):
            columns = slice(side * 4 * size, side * 4 * size + 4 * size)
            product = columns_by_columns(left[0][:, columns], right) + columns_by_columns(left[1][:, columns], far)
            put(layer_no, name, product, lambda tile, i: (tile + i, 0), blocks[4 * side : 4 * side + 4], 4 * size * side)
        reductions[layer_no, name].start()

    def proj_product(layer_no):
        middle_swaps[layer_no].arrive()
        if layer_no == top:
            mixed_swaps[layer_no].arrive()
        left = (mixed.at[layer_no, 0], mixed.at[layer_no, 1])
        narrow_product(layer_no, PROJ, left, grad_middle(place.z0)[...], far_middle[layer_no])
        middle_swaps[layer_no].drain()

    def part_product(layer_no, part):
        qkv_swaps[layer_no][part].arrive()
        left = (normed.at[layer_no, 0], normed.at[layer_no, 2])
        narrow_product(layer_no, QUERY + part, left, half_qkv[part, place.z0], far_qkv[layer_no, part])
        qkv_swaps[layer_no][part].drain()

    def hand_out(layer_no, name):
        if name < UP_A:
            target = results[0].at[layer_no, pl.ds(half // 2 * (name - DOWN_A), half // 2)]
        elif name < PROJ:
            target = results[1].at[layer_no, :, pl.ds(half * (name - UP_A), half)]
        else:
            target = results[name - 2].at[layer_no]
        return pltpu.make_async_copy(stagings[name], target, stage_sems.at[name])

    def finish(layer_no, name):
        target = stagings[name]
        if layer_no < top:
            hand_out(layer_no + 1, name).wait()

        def write(own, rest=None):
            if rest is None:
                for part in range(own.shape[0] // size):
                    target[:, tile_of(part)] = own[size * part : size * part + size]
            else:
                target[:, :LANES] = own
                target[:, LANES : LANES + 64] = rest

        reductions[layer_no, name].finish(write)
        hand_out(layer_no, name).start()

    def step(layer_no, name, stage):
        reductions[layer_no, name].step(stage)

    def return_grad():
        out_return.wait()
        returned[...] = carried[...].astype(BF16)
        grad_return.start()

    def low_arrivals():
        log_gathers[low].last()
        for one in [mixed_swaps[low], normed_swaps[low]] + acts_swaps[low]:
            one.arrive()

    mark_arrival.start()
    arrival.start()
    sums[...] = jnp.zeros(sums.shape, F32)
    mark_arrival.wait()
    mark_gather.start()
    make_angles(0, 0)
    arrival.wait()
    carried[...] = start[...].astype(F32)
    normalise_first(0)
    weights.ready(0, KEY_W, VALUE_W, QUERY_W)
    project(0, 0)
    mark_gather.near()
    mark_gather.far()
    make_angles(0, 1)
    h_gathers[0].near()
    project(0, 1)
    make_angles(0, 2)
    mark_gather.last()
    make_angles(0, 3)
    h_gathers[0].far()
    other_arrival.start()
    project(0, 2)
    h_gathers[0].last()
    project(0, 3)
    weights.load(1, KEY_W, VALUE_W, QUERY_W)
    for name in (KEYS, VALUES, QUERIES, ANGLES):
        spill(name).start()
    attend(0)
    mixed_swaps[0].start()
    project_out(0)
    for quarter in range(4):
        feed_forward(0, quarter)
    weights.load(1, UP_W, DOWN_W)
    spill(SLOPES).start()
    for part in acts_swaps[0]:
        part.start()
    normalise_first(1)
    normed_swaps[0].start()
    log_gathers[0].start()
    for name in (KEYS, VALUES, QUERIES, ANGLES):
        spill(name).wait()
    make_angles(1, 0)
    weights.ready(1, KEY_W, VALUE_W, QUERY_W)
    project(1, 0)
    make_angles(1, 1)
    h_gathers[1].near()
    project(1, 1)
    make_angles(1, 2)
    make_angles(1, 3)
    other_arrival.wait()
    send_error(1, returned[...].astype(F32))
    h_gathers[1].far()
    project(1, 2)
    h_gathers[1].last()
    project(1, 3)
    log_gathers[0].near()
    log_gathers[0].far()
    attend(1)
    log_gathers[1].start()
    mixed_swaps[1].start()
    project_out(1)
    normed_swaps[1].start()
    spill(SLOPES).wait()
    feed_forward(1, 0)
    feed_forward(1, 1)
    acts_swaps[1][0].start()
    feed_forward(1, 2)
    feed_forward(1, 3)
    acts_swaps[1][1].start()
    start[...] = carried[...].astype(BF16)
    carried[...] = returned[...].astype(F32)
    low_arrivals()
    hidden_back(top)
    middle_back(top)
    project_back(top)
    own_queries(top)
    hidden_swaps[top][0].start()
    middle_send(top)
    log_gathers[top].far()
    qkv_swaps[top][0].start()
    out_return.start()
    hidden_swaps[top][1].start()
    down_product(top)
    do_gathers[top].far()
    step(top, DOWN_A, 0)
    step(top, DOWN_B, 0)
    own_keys(top)
    up_product(top, 0)
    qkv_swaps[top][1].start()
    qkv_swaps[top][2].start()
    input_back(top)
    hidden_back(low)
    middle_back(low)
    project_back(low)
    step(top, DOWN_A, 1)
    hidden_swaps[low][1].start()
    part_product(top, 0)
    step(top, UP_A, 0)
    hidden_swaps[low][0].start()
    own_queries(low)
    step(top, DOWN_B, 1)
    qkv_swaps[low][0].start()
    step(top, QUERY, 0)
    down_product(low)
    up_product(top, 1)
    proj_product(top)
    part_product(top, 1)
    middle_send(low)
    step(low, DOWN_A, 0)
    step(low, DOWN_B, 0)
    part_product(top, 2)
    step(top, QUERY, 1)
    step(top, UP_A, 1)
    step(top, UP_B, 0)
    step(top, PROJ, 0)
    step(top, KEY, 0)
    step(top, VALUE, 0)
    do_gathers[low].far()
    step(top, QUERY, 2)
    own_keys(low)
    finish(top, QUERY)
    step(low, DOWN_A, 1)
    qkv_swaps[low][1].start()
    qkv_swaps[low][2].start()
    step(top, DOWN_A, 2)
    step(top, UP_B, 1)
    input_back(low)
    doubling.start()
    up_product(low, 1)
    return_grad()
    doubling.step(0)
    step(top, PROJ, 1)
    step(low, DOWN_B, 1)
    step(low, UP_B, 0)
    step(top, UP_A, 2)
    step(top, KEY, 1)
    up_product(low, 0)
    finish(top, DOWN_A)
    doubling.step(1)
    step(low, UP_A, 0)
    step(top, VALUE, 1)
    step(top, DOWN_B, 2)
    part_product(low, 0)
    step(top, UP_B, 2)
    finish(top, UP_A)
    step(low, UP_B, 1)
    proj_product(low)
    step(low, QUERY, 0)
    step(top, PROJ, 2)
    step(top, KEY, 2)
    step(low, PROJ, 0)
    doubling.step(2)
    finish(top, DOWN_B)
    step(low, DOWN_A, 2)
    finish(top, UP_B)
    step(low, UP_B, 2)
    part_product(low, 1)
    step(low, UP_A, 1)
    finish(top, PROJ)
    step(top, VALUE, 2)
    step(low, KEY, 0)
    step(low, QUERY, 1)
    finish(top, KEY)
    part_product(low, 2)
    step(low, PROJ, 1)
    step(low, VALUE, 0)
    finish(low, DOWN_A)
    step(low, UP_A, 2)
    step(low, KEY, 1)
    finish(low, UP_B)
    step(low, PROJ, 2)
    step(low, QUERY, 2)
    finish(top, VALUE)
    step(low, VALUE, 1)
    step(low, DOWN_B, 2)
    step(low, KEY, 2)
    finish(low, UP_A)
    finish(low, PROJ)
    step(low, VALUE, 2)
    finish(low, QUERY)
    doubling.step(3)
    finish(low, DOWN_B)
    finish(low, KEY)
    finish(low, VALUE)
    doubling.step(4)
    grad_small[...] = sums[...]
    grad_return.wait()
    for name in TENSORS:
        hand_out(low, name).wait()
    for red in reductions.values():
        red.drain()
    for gather in [mark_gather] + h_gathers + log_gathers + do_gathers:
        gather.drain()
    for one in error_swaps + mixed_swaps + normed_swaps + acts_swaps[low] + acts_swaps[top]:
        one.drain()


def encoder_call(patches, cotangent, keep, coords, norms, freqs, whole):
    layers = freqs.shape[0]
    rows, width = patches.shape
    hidden = whole[4].shape[2]
    size, quarter = width // 8, width // 4
    plans = tile_plan(width, hidden)
    tensors = plans * layers
    sem = pltpu.SemaphoreType.DMA
    any_spec, vmem_spec = pl.BlockSpec(memory_space=pl.ANY), pl.BlockSpec(memory_space=pltpu.VMEM)
    finals = [(hidden // 8, quarter), (size, hidden // 4)] + [(size, quarter)] * 4
    parts = [(hidden // 16, quarter)] * 2 + [(size, hidden // 8)] * 2 + [(size, quarter)] * 4
    outs = (
        [jax.ShapeDtypeStruct((rows, width), BF16)] * 2
        + [jax.ShapeDtypeStruct((layers,) + shape, F32) for shape in finals]
        + [jax.ShapeDtypeStruct((8 * layers, width), F32)]
        + [jax.ShapeDtypeStruct(*shape) for shape in spilled_shapes(rows, width, hidden)]
    )

    def low(*shape):
        return pltpu.VMEM(shape, BF16)

    def full(*shape):
        return pltpu.VMEM(shape, F32)

    return pl.pallas_call(
        lambda *refs: encoder_kernel(layers, *refs),
        out_shape=outs,
        in_specs=[any_spec, any_spec] + [vmem_spec] * 7 + [any_spec] * 6,
        out_specs=[any_spec] * 8 + [vmem_spec] + [any_spec] * 5,
        scratch_shapes=[pltpu.VMEM(*shape) for shape in spilled_shapes(rows, width, hidden)]
        + [low(8 * n, count, LANES) for n, count in tensors]
        + [low(landing_count(n), count, LANES) for n, count in tensors]
        + [low(4 * n, count, LANES) for n, count in plans]
        + [full(*shape) for shape in parts]
        + [low(width, 3 * width), low(width, width), low(width, hidden), low(hidden, width)]
        + [sem((6,)), sem((5,)), sem((5,)), sem((len(plans),))]
        + [
            low(layers, 4, rows, width),
            low(layers, 4, rows, LANES),
            low(layers, 2, rows, width),
            low(layers, 2, rows, width),
            low(layers, 2, 4, rows, hidden // 8),
            low(layers, 4, rows, hidden // 8),
            low(layers, rows, width),
            low(layers, rows, width),
            full(layers, rows, LANES),
        ]
        + [low(rows, width), low(rows, LANES), low(4, rows, LANES), low(rows, width), sem((5, 3))]
        + [sem((layers, 4))] * 6
        + [sem((4,))] * 2
        + [
            low(layers, 4, rows, width + LANES),
            low(layers, rows, width),
            low(layers, 2, 2, rows, width),
            low(layers, 2, rows, width),
            low(layers, rows, width // 2),
            low(rows, 3 * width),
            low(3, 2, rows, width // 2),
            low(layers, 3, rows, width // 2),
        ]
        + [sem((layers, 11, 2)), sem((len(tensors), 5)), sem((len(tensors), 5))]
        + [pltpu.SemaphoreType.REGULAR((len(plans),))]
        + [full(rows, width), full(8 * layers, width), full(5, 8 * layers, width), sem((5, 2))],
        compiler_params=pltpu.CompilerParams(
            collective_id=0, has_side_effects=True, vmem_limit_bytes=VMEM_BYTES
        ),
    )(patches, cotangent, keep, coords, *norms, freqs, *whole)


def beyond_eight(result):
    dp_size = lax.axis_size(DP)
    groups = dp_size // 8
    if groups == 1:
        return result
    result = lax.psum(result, DP, axis_index_groups=[[g * 8 + i for g in range(groups)] for i in range(8)])
    whole = lax.all_gather(
        result, DP, axis=1, tiled=True, axis_index_groups=[[g * 8 + i for i in range(8)] for g in range(groups)]
    )
    rows = whole.shape[1] // dp_size
    return lax.dynamic_slice_in_dim(whole, lax.axis_index(DP) * rows, rows, axis=1)


def final_kernel(count, *refs):
    sources, refs = refs[: 3 + count], refs[3 + count :]
    targets, refs = refs[: 7 + count], refs[7 + count :]
    arrived, refs = refs[: 3 + count], refs[3 + count :]
    grad_copy, turned, in_sems, out_sems = refs
    copies = [pltpu.make_async_copy(a, b, in_sems.at[i]) for i, (a, b) in enumerate(zip(sources, arrived))]
    for copy in copies:
        copy.start()
    leaving = []

    def leave(source, target):
        copy = pltpu.make_async_copy(source, target, out_sems.at[len(leaving)])
        copy.start()
        leaving.append(copy)

    copies[0].wait()
    leave(arrived[0], targets[0])
    copies[1].wait()
    grad_copy[...] = arrived[1][...].astype(F32)
    leave(grad_copy, targets[1])
    last = 2 + count
    copies[last].wait()
    layers = turned.shape[0]
    for layer_no in range(layers):
        turned[layer_no] = arrived[last][layer_no].T
    leave(turned, targets[last - 1])
    for i in range(3, last):
        copies[i].wait()
        leave(arrived[i], targets[i - 1])
    copies[2].wait()
    small, norms, turns = arrived[2], targets[last : last + 4], targets[last + 4]
    columns = norms[0].shape[1]
    at = lax.axis_index(BLK)
    half = turns.shape[3]
    for blk in range(small.shape[1] // columns):

        @pl.when(at == blk)
        def _(blk=blk):
            for layer_no in range(layers):
                mine = small[8 * layer_no : 8 * layer_no + 8, blk * columns : blk * columns + columns]
                for row, norm in enumerate(norms):
                    norm[layer_no : layer_no + 1] = mine[row : row + 1]
                for row in range(2):
                    for head in range(turns.shape[1]):
                        pair = mine[4 + row : 5 + row, 2 * half * head : 2 * half * head + 2 * half]
                        turns[layer_no, head, row : row + 1] = pair[:, half:] - pair[:, :half]

    for copy in leaving:
        copy.wait()


def final_call(output, grad_patches, small, large, half):
    any_spec, vmem_spec = pl.BlockSpec(memory_space=pl.ANY), pl.BlockSpec(memory_space=pltpu.VMEM)
    layers = small.shape[0] // 8
    columns = small.shape[1] // lax.axis_size(BLK)
    sources = (output, grad_patches, small, *large)
    turned = (layers,) + large[-1].shape[:0:-1]
    shapes = [(output.shape, output.dtype), (grad_patches.shape, F32)]
    shapes += [(a.shape, F32) for a in large[:-1]] + [(turned, F32)]
    norms = [((layers, columns), F32)] * 4 + [((layers, columns // (2 * half), 2, half), F32)]
    return pl.pallas_call(
        lambda *refs: final_kernel(len(large), *refs),
        out_shape=[jax.ShapeDtypeStruct(*shape) for shape in shapes + norms],
        in_specs=[any_spec] * len(sources),
        out_specs=[any_spec] * len(shapes) + [vmem_spec] * len(norms),
        scratch_shapes=[pltpu.VMEM(a.shape, a.dtype) for a in sources]
        + [pltpu.VMEM(grad_patches.shape, F32), pltpu.VMEM(turned, F32)]
        + [pltpu.SemaphoreType.DMA((len(sources),)), pltpu.SemaphoreType.DMA((len(shapes),))],
    )(*sources)


def shards(
    patches,
    keep,
    coords,
    query_w,
    key_w,
    value_w,
    proj_w,
    up_w,
    down_w,
    norm1_gain,
    norm1_bias,
    norm2_gain,
    norm2_bias,
    freqs,
    cotangent,
):
    whole = (query_w, key_w, value_w, proj_w, up_w, down_w)
    norms = (norm1_gain, norm1_bias, norm2_gain, norm2_bias)
    results = encoder_call(patches[0], cotangent[0], keep, coords, norms, jnp.swapaxes(freqs, 1, 2), whole)
    output, grad_patches, grad_down, grad_up, *others, small = results[:9]
    large = [beyond_eight(grad) for grad in (*others[1:], others[0], grad_up, grad_down)]
    groups = lax.axis_size(DP) // 8
    if groups > 1:
        small = lax.psum(small, DP, axis_index_groups=[[g * 8 + i for g in range(groups)] for i in range(8)])
    output, grad_patches, *rest = final_call(output, grad_patches, small, large, freqs.shape[3])
    rest[5], rest[-1] = jnp.swapaxes(rest[5], 1, 2), jnp.swapaxes(rest[-1], 1, 2)
    return (output[None], grad_patches[None], *rest)


def solution(mesh):
    block = P(DP, BLK, None)
    placed = (block, P(DP, BLK), P(None, DP, BLK)) + (P(),) * 11 + (block,)
    results = (block, block) + (P(None, DP, BLK),) * 6 + (P(None, BLK),) * 4 + (P(None, None, BLK, None),)
    return jax.shard_map(shards, mesh=mesh, in_specs=placed, out_specs=results, check_vma=False)
```

```python
import jax
import jax.numpy as jnp
from jax import lax
from jax.experimental import pallas as pl
from jax.experimental.pallas import tpu as pltpu
from jax.sharding import PartitionSpec as P

MESH = pl.DeviceIdType.MESH
DP, BLK = "dp", "blk"
C, X, Y, Z0, Z1 = range(5)
BF16, F32 = jnp.bfloat16, jnp.float32
MASKED_SCORE = -1e30
NORM_EPSILON = 1e-06
LANES = 128
SCALE_LANE = 64
VMEM_BYTES = 127 * 512 * 1024


def rows_by_columns(left, right):
    return lax.dot_general(left, right, (((1,), (0,)), ((), ())), preferred_element_type=F32)


def rows_by_rows(left, right):
    return lax.dot_general(left, right, (((1,), (1,)), ((), ())), preferred_element_type=F32)


def columns_by_columns(left, right):
    return lax.dot_general(left, right, (((0,), (0,)), ((), ())), preferred_element_type=F32)


class Place:
    def __init__(self):
        self.dp = lax.axis_index(DP)
        self.blk = lax.axis_index(BLK)
        self.c = lax.rem(self.dp, 2)
        self.x = lax.rem(self.dp // 2, 2)
        self.y = lax.rem(self.dp // 4, 2)
        self.z0 = lax.rem(self.blk, 2)
        self.z1 = lax.rem(self.blk // 2, 2)
        self.bits = (self.c, self.x, self.y, self.z0, self.z1)
        self.worker = (self.dp - self.c + self.z0, 2 * self.c + self.z1)
        self.owner = (self.dp - self.c + self.z1, 2 * self.z0 + self.c)
        self.stays = (self.worker[0] == self.dp) & (self.worker[1] == self.blk)

    def other(self, axis):
        if axis <= Y:
            return (self.dp + (1 << axis) * (1 - 2 * self.bits[axis]), self.blk)
        return (self.dp, self.blk + (1 << axis - Z0) * (1 - 2 * self.bits[axis]))

    def greet(self, axes):
        barrier = pltpu.get_barrier_semaphore()
        mine = 2 * self.blk + self.c
        for step in range(1, 8):
            them = lax.rem(mine + step, 8)
            pl.semaphore_signal(
                barrier, inc=1, device_id=(self.dp - self.c + lax.rem(them, 2), them // 2), device_id_type=MESH
            )
        for axis in axes:
            pl.semaphore_signal(barrier, inc=1, device_id=self.other(axis), device_id_type=MESH)
        pl.semaphore_wait(barrier, 7 + len(axes))


class Relocation:
    def __init__(self, place, source, target, sems, back=False):
        self.place, self.source, self.target, self.sems = place, source, target, sems
        self.device = place.owner if back else place.worker

    def remote(self):
        return pltpu.make_async_remote_copy(
            src_ref=self.source,
            dst_ref=self.target,
            send_sem=self.sems.at[0],
            recv_sem=self.sems.at[1],
            device_id=self.device,
            device_id_type=MESH,
        )

    def local(self):
        return pltpu.make_async_copy(self.source, self.target, self.sems.at[2])

    def start(self):
        pl.when(self.place.stays)(lambda: self.local().start())
        pl.when(jnp.logical_not(self.place.stays))(lambda: self.remote().start())

    def wait(self):
        pl.when(self.place.stays)(lambda: self.local().wait())
        pl.when(jnp.logical_not(self.place.stays))(lambda: self.remote().wait())


class Gather:
    def __init__(self, place, slots, sends, receives):
        self.place, self.slots, self.sends, self.receives = place, slots, sends, receives

    def copy(self, source, slot, axis):
        return pltpu.make_async_remote_copy(
            src_ref=self.slots.at[source],
            dst_ref=self.slots.at[slot],
            send_sem=self.sends.at[slot],
            recv_sem=self.receives.at[slot],
            device_id=self.place.other(axis),
            device_id_type=MESH,
        )

    def start(self):
        self.copy(0, 2, Z0).start()
        self.copy(0, 1, C).start()

    def near(self):
        self.copy(0, 1, C).wait_recv()

    def far(self):
        self.copy(0, 2, Z0).wait_recv()
        self.copy(2, 3, C).start()

    def last(self):
        self.copy(2, 3, C).wait_recv()

    def drain(self):
        self.copy(0, 1, C).wait_send()
        self.copy(0, 2, Z0).wait_send()
        self.copy(2, 3, C).wait_send()


class Swap:
    def __init__(self, place, axis, source, target, sems):
        self.place, self.axis, self.source, self.target, self.sems = place, axis, source, target, sems

    def copy(self):
        return pltpu.make_async_remote_copy(
            src_ref=self.source,
            dst_ref=self.target,
            send_sem=self.sems.at[0],
            recv_sem=self.sems.at[1],
            device_id=self.place.other(self.axis),
            device_id_type=MESH,
        )

    def start(self):
        self.copy().start()

    def arrive(self):
        self.copy().wait_recv()

    def drain(self):
        self.copy().wait_send()


def lane_index(rows):
    return lax.broadcasted_iota(jnp.int32, (rows, LANES), 1)


def partner_tile(tile, former):
    return jnp.where(former, pltpu.roll(tile, 96, 1), pltpu.roll(tile, 32, 1))


def rotate_tile(tile, cosine, signed_sine, former):
    return tile * cosine + partner_tile(tile, former) * signed_sine


def tile_of(index):
    return slice(LANES * index, LANES * index + LANES)


def normalise(values):
    centre = values - jnp.mean(values, axis=-1, keepdims=True)
    spread = jnp.mean(centre * centre, axis=-1, keepdims=True)
    scale = lax.rsqrt(spread + NORM_EPSILON)
    return centre * scale, scale


QUERY_W, KEY_W, VALUE_W, PROJ_W, UP_W, DOWN_W = range(6)


class Weights:
    def __init__(self, whole, qkv, proj, up, down, sems):
        width = qkv.shape[1] // 3
        self.whole, self.sems = whole, sems
        self.buffers = [qkv.at[:, pl.ds(part * width, width)] for part in range(3)] + [proj, up, down]

    def copy(self, name, layer_no):
        return pltpu.make_async_copy(self.whole[name].at[layer_no], self.buffers[name], self.sems.at[name])

    def load(self, layer_no, *names):
        for name in names:
            self.copy(name, layer_no).start()

    def ready(self, layer_no, *names):
        for name in names:
            self.copy(name, layer_no).wait()


def spread_lanes(columns, lane, last):
    columns = jnp.where(lane < 16, columns, 0.0)
    high = columns.astype(BF16).astype(F32)
    middle = (columns - high).astype(BF16).astype(F32)
    low = columns - high - middle
    spread = high + pltpu.roll(middle, 16, 1) + pltpu.roll(low, 32, 1)
    return jnp.where(lane == 127, last, spread)


class Reduction:
    def __init__(self, place, axes, n, share, first_landing, landing, sends, receives, credit, gives, takes):
        self.place, self.axes = place, axes + (Z1, Z1)
        self.share, self.first_landing, self.landing = share, first_landing, landing
        self.sends, self.receives = sends, receives
        self.credit, self.gives, self.takes = credit, gives, takes
        self.n, self.rows = n, share.shape[1]
        self.plan = []
        base, half, land = 0, 4 * n, 0
        for axis in axes:
            bit = place.bits[axis]
            self.plan.append((base + (1 - bit) * half, base + bit * half, half, land))
            base, land, half = base + bit * half, land + half if self.plan[1:] else 0, half // 2
        self.spare = self.plan[0][0]
        self.base, self.land = base, land
        self.plan.append((base + (n - 1) * (1 - place.z1), base + (n - 1) * place.z1, 1, land))

    def copy(self, stage):
        if stage < 4:
            send, _, count, land = self.plan[stage]
            landing = self.first_landing if stage == 0 else self.landing
            source, target = self.share.at[pl.ds(send, count)], landing.at[pl.ds(land, count)]
        else:
            half = pl.ds(0, self.rows // 2)
            source, target = self.share.at[self.spare, half], self.landing.at[self.land + 1, half]
        return pltpu.make_async_remote_copy(
            src_ref=source,
            dst_ref=target,
            send_sem=self.sends.at[stage],
            recv_sem=self.receives.at[stage],
            device_id=self.place.other(self.axes[stage]),
            device_id_type=MESH,
        )

    def start(self, stage=0):
        if stage == 0 and self.takes:
            pl.semaphore_wait(self.credit, 1)
        self.copy(stage).start()

    def step(self, stage):
        _, keep, count, land = self.plan[stage]
        self.copy(stage).wait_recv()

        landing = self.first_landing if stage == 0 else self.landing

        def body(i, carry):
            self.share[keep + i] = self.share[keep + i] + landing[land + i]
            return carry

        lax.fori_loop(0, count, body, 0)
        self.start(stage + 1)
        if stage == 0:
            self.copy(0).wait_send()
            if self.gives:
                pl.semaphore_signal(self.credit, inc=1, device_id=self.place.other(C), device_id_type=MESH)
        if stage == 2 and self.n == 3:
            half = self.rows // 2
            shared = self.share[self.base + 1].astype(F32)
            upper, lower = shared[:half], shared[half:]
            first = lane_index(half) < 64
            low_lanes = jnp.where(first, upper, pltpu.roll(lower, 64, 1))
            high_lanes = jnp.where(first, pltpu.roll(upper, 64, 1), lower)
            self.share[self.spare, :half] = jnp.where(self.place.z1 == 1, low_lanes, high_lanes).astype(BF16)
            self.start(4)

    def finish(self, write):
        self.copy(3).wait_recv()
        _, keep, _, land = self.plan[3]
        own = self.share[keep].astype(F32) + self.landing[land].astype(F32)
        if self.n == 2:
            write(own)
            return
        self.copy(4).wait_recv()
        half = self.rows // 2
        packed = self.landing[self.land + 1, :half].astype(F32)
        shared = self.share[self.base + 1].astype(F32)
        shared = jnp.where(self.place.z1 == 0, shared, pltpu.roll(shared, 64, 1))
        rest = shared + jnp.concatenate([packed, pltpu.roll(packed, 64, 1)], axis=0)
        write(own, rest[:, :64])

    def drain(self):
        for stage in range(1, 4 if self.n == 2 else 5):
            self.copy(stage).wait_send()


class Doubling:
    AXES = (C, X, Y, Z0, Z1)

    def __init__(self, place, sums, landing, sems):
        self.place, self.sums, self.landing, self.sems = place, sums, landing, sems

    def copy(self, stage):
        return pltpu.make_async_remote_copy(
            src_ref=self.sums,
            dst_ref=self.landing.at[stage],
            send_sem=self.sems.at[stage, 0],
            recv_sem=self.sems.at[stage, 1],
            device_id=self.place.other(self.AXES[stage]),
            device_id_type=MESH,
        )

    def start(self):
        self.copy(0).start()

    def step(self, stage):
        self.copy(stage).wait()
        self.sums[...] += self.landing[stage]
        if stage + 1 < len(self.AXES):
            self.copy(stage + 1).start()


TENSORS = DOWN_A, DOWN_B, UP_A, UP_B, PROJ, QUERY, KEY, VALUE = range(8)
HALVING = ((C, Y, Z0),) * 2 + ((C, X, Y),) * 3 + ((C, Y, X), (C, X, Y), (C, Y, X))


def tile_plan(width, hidden):
    size = width // 8
    return ((3, hidden // 16),) * 2 + ((2, size * (hidden // 8 // LANES)),) * 2 + ((3, size),) * 4


def landing_count(n):
    return 2 * n + n + n - 1


def by_halves(tiles, first):
    def turned(tile):
        return pltpu.roll(tile, 64, 1)

    return (
        (tiles[0], jnp.where(first, tiles[1], turned(tiles[4])), tiles[3]),
        (
            jnp.where(first, turned(tiles[1]), turned(tiles[2])),
            jnp.where(first, turned(tiles[2]), tiles[5]),
            jnp.where(first, turned(tiles[4]), turned(tiles[5])),
        ),
    )


KEYS, VALUES, QUERIES, ANGLES, SLOPES = SPILLED = range(5)


def spilled_shapes(rows, width, hidden):
    return (
        ((4, rows, width), BF16),
        ((4, rows, width), BF16),
        ((4, rows, width), BF16),
        ((2, rows, width), F32),
        ((rows, hidden), BF16),
    )


def encoder_kernel(layers, *refs):
    patches, cotangent, keep, coords, gain1, bias1, gain2, bias2, freqs = refs[:9]
    whole = refs[9:15]
    output, grad_patches = refs[15:17]
    results = refs[17:23]
    grad_small = refs[23]
    saved = refs[24:29]
    held = refs[29:34]
    refs = refs[34:]
    count = layers * len(TENSORS)
    shares, landings, first_landings = refs[:count], refs[count : 2 * count], refs[2 * count : 2 * count + len(TENSORS)]
    refs = refs[2 * count + len(TENSORS) :]
    stagings = refs[: len(TENSORS)]
    refs = refs[len(TENSORS) :]
    (qkv_w, proj_w, up_w, down_w, w_sems, spill_sems, load_sems, stage_sems) = refs[:8]
    (normed, logs_low, mixed, normed2, acts, far_acts, hat1, hat2, stats) = refs[8:17]
    (start, own_marks, marks, returned, relocation_sems) = refs[17:22]
    (h_sends, h_receives, do_sends, do_receives, q_sends, q_receives, m_sends, m_receives) = refs[22:30]
    (douts, errors, grad_hidden, far_hidden, far_middle, grad_qkv, half_qkv, far_qkv) = refs[30:38]
    (swap_sems, sends, receives, credits, carried, sums, sums_landing, sums_sems) = refs[38:]
    place = Place()
    rows, width = carried.shape
    hidden = up_w.shape[1]
    half = hidden // 8
    size = width // 8
    pairs = width // LANES
    top, low = layers - 1, layers - 2
    weights = Weights(whole, qkv_w, proj_w, up_w, down_w, w_sems)
    weights.load(0, KEY_W, VALUE_W, QUERY_W, PROJ_W, UP_W, DOWN_W)
    line = lax.broadcasted_iota(jnp.int32, (LANES, rows), 0)
    own = jnp.where(line == 0, jnp.where(keep[...] > 0, 0.0, MASKED_SCORE), 0.0)
    for number in range(2):
        own = jnp.where(line == 1 + number, coords[number].astype(F32), own)
    own_marks[...] = own.T.astype(BF16)
    place.greet((X, Y))

    lane = lane_index(rows)
    former = lax.rem(lane, 64) < 32
    first_head = lane < 64
    heads_lanes = (first_head, jnp.logical_not(first_head))
    two_lane = lane_index(2 * rows)
    upper = lax.broadcasted_iota(jnp.int32, (2 * rows, LANES), 0) < rows
    one_lane = jnp.where(two_lane == 0, 1.0, 0.0).astype(BF16)

    def both(tile):
        return jnp.where((two_lane < 64) == upper, jnp.concatenate([tile, tile], axis=0), jnp.zeros((), tile.dtype))

    def beside(values):
        return jnp.where(first_head, values[:rows], values[rows:])

    def columns_of(values, index):
        return jnp.concatenate([values[:, 2 * index : 2 * index + 1], values[:, 2 * index + 1 : 2 * index + 2]], axis=0)

    plans = tile_plan(width, hidden)
    away = 1 - place.z0

    def relocation(number, source, target, back=False):
        return Relocation(place, source, target, relocation_sems.at[number], back)

    def swap(layer_no, number, axis, source, target):
        return Swap(place, axis, source, target, swap_sems.at[layer_no, number])

    every = range(layers)

    def grad_middle(z0):
        return normed.at[top, 1, :, pl.ds(pl.multiple_of(z0 * (width // 2), LANES), width // 2)]

    mark_arrival = relocation(0, own_marks, marks.at[0])
    arrival = relocation(1, patches, start)
    other_arrival = relocation(2, cotangent, returned)
    out_return = relocation(3, start, output, True)
    grad_return = relocation(4, returned, grad_patches, True)
    mark_gather = Gather(place, marks, m_sends, m_receives)
    h_gathers = [Gather(place, normed.at[l], h_sends.at[l], h_receives.at[l]) for l in every]
    log_gathers = [Gather(place, logs_low.at[l], q_sends.at[l], q_receives.at[l]) for l in every]
    do_gathers = [Gather(place, douts.at[l], do_sends.at[l], do_receives.at[l]) for l in every]
    own_errors = [normed.at[0, 1 + 2 * l] for l in every]
    error_swaps = [swap(l, 0, X, own_errors[l], errors.at[l]) for l in every]
    hidden_swaps = [
        [
            swap(l, 1 + part, Z0, grad_hidden.at[l, away, :, :, columns], far_hidden.at[l, :, :, columns])
            for part, columns in enumerate((pl.ds(0, half), pl.ds(half, half)))
        ]
        for l in every
    ]
    middle_swaps = [swap(l, 3, Z0, grad_middle(away), far_middle.at[l]) for l in every]
    qkv_swaps = [[swap(l, 4 + part, Z0, half_qkv.at[part, away], far_qkv.at[l, part]) for part in range(3)] for l in every]
    mixed_swaps = [swap(l, 7, Z0, mixed.at[l, 0], mixed.at[l, 1]) for l in every]
    normed_swaps = [swap(l, 8, Z0, normed2.at[l, 0], normed2.at[l, 1]) for l in every]
    acts_swaps = [
        [
            swap(l, 9 + y, X, acts.at[l, 1 - place.x, pl.ds(2 * y, 2)], far_acts.at[l, pl.ds(2 * y, 2)])
            for y in range(2)
        ]
        for l in every
    ]
    doubling = Doubling(place, sums, sums_landing, sums_sems)
    reductions = {}
    for layer_no in every:
        for name in TENSORS:
            at = layer_no * len(TENSORS) + name
            reductions[layer_no, name] = Reduction(
                place,
                HALVING[name],
                plans[name][0],
                shares[at],
                first_landings[name],
                landings[at],
                sends.at[at],
                receives.at[at],
                credits.at[name],
                layer_no > 0,
                layer_no < top,
            )

    def spill(name):
        return pltpu.make_async_copy(held[name], saved[name], spill_sems.at[name])

    def loading(name):
        return pltpu.make_async_copy(saved[name], held[name], load_sems.at[name])

    def load(layer_no, *names):
        for name in names:
            loading(name).start()

    def ready(layer_no, *names):
        if layer_no < top:
            for name in names:
                loading(name).wait()


    def freq_tile(layer_no, which, index):
        return jnp.concatenate(
            [freqs[layer_no, 4 * index + member, which : which + 1] for member in range(4)], axis=1
        )

    def twice(tile):
        once, half_way, back = (pltpu.roll(tile, shift, 1) for shift in (32, 64, 96))
        quarter, last = lane < 32, lane >= 96
        return (
            jnp.where(quarter, tile, jnp.where(last, half_way, once)),
            jnp.where(quarter, half_way, jnp.where(last, tile, back)),
        )

    def angle_refs(slot):
        if slot == 0:
            return held[ANGLES].at[0], held[ANGLES].at[1]
        return grad_hidden.at[0, slot // 2, slot % 2], grad_hidden.at[1, slot // 2, slot % 2]

    def make_angles(layer_no, slot):
        rows_at = marks[slot][:, 1:2].astype(F32)
        columns_at = marks[slot][:, 2:3].astype(F32)
        cosine, sine = angle_refs(slot)
        sign = jnp.where(former, -1.0, 1.0)
        for index in range(pairs // 2):
            angle = rows_at * freq_tile(layer_no, 0, index) + columns_at * freq_tile(layer_no, 1, index)
            for member, (even, odd) in enumerate(zip(twice(jnp.cos(angle)), twice(jnp.sin(angle)))):
                cosine[:, tile_of(2 * index + member)] = even.astype(cosine.dtype)
                sine[:, tile_of(2 * index + member)] = (sign * odd).astype(sine.dtype)

    def project(layer_no, slot):
        cosine, sine = angle_refs(slot)
        block = normed[layer_no, slot]
        for name, part, scale in ((QUERIES, 0, 0.125), (KEYS, 1, 1.0)):
            products = rows_by_columns(block, qkv_w[:, part * width : part * width + width])
            for index in range(pairs):
                sl = tile_of(index)
                turned = rotate_tile(products[:, sl], cosine[:, sl].astype(F32), sine[:, sl].astype(F32), former)
                held[name][slot, :, sl] = (scale * turned).astype(BF16)
        held[VALUES][slot] = rows_by_columns(block, qkv_w[:, 2 * width :]).astype(BF16)

    def normalise_first(layer_no):
        hat, scale = normalise(carried[...])
        hat1[layer_no] = hat.astype(BF16)
        stats[layer_no] = jnp.where(lane == SCALE_LANE, scale, 0.0)
        normed[layer_no, 0] = (hat * gain1[layer_no : layer_no + 1] + bias1[layer_no : layer_no + 1]).astype(BF16)
        h_gathers[layer_no].start()

    def attend(layer_no):
        marks_of_keys = marks[...].reshape(4 * rows, LANES)
        sums_of_rows = jnp.zeros((rows, LANES), F32)
        for index in range(pairs):
            sl = tile_of(index)
            query_pair = held[QUERIES][0, :, sl]
            key_pair = held[KEYS][:, :, sl].reshape(4 * rows, LANES)
            value_pair = held[VALUES][:, :, sl].reshape(4 * rows, LANES)
            extended = jnp.concatenate([key_pair, marks_of_keys], axis=1)
            scores = rows_by_rows(jnp.concatenate([both(query_pair), one_lane], axis=1), extended)
            highest = jnp.max(scores, axis=1, keepdims=True)
            weight = jnp.exp(scores - highest)
            total = jnp.sum(weight, axis=1, keepdims=True)
            result = rows_by_columns(weight.astype(BF16), value_pair) / total
            mixed[layer_no, 0, :, sl] = beside(result).astype(BF16)
            log_sum = highest + jnp.log(total)
            for member in range(2):
                part = log_sum[member * rows : member * rows + rows]
                sums_of_rows = jnp.where(lane == 2 * index + member, part, sums_of_rows)
        stats[layer_no] = jnp.where(lane < 16, sums_of_rows, stats[layer_no])
        logs_low[layer_no, 0] = spread_lanes(-sums_of_rows, lane, 1.0).astype(BF16)

    def project_out(layer_no):
        weights.ready(layer_no, PROJ_W)
        middle = carried[...] + rows_by_columns(mixed[layer_no, 0], proj_w[...])
        carried[...] = middle
        if layer_no < top:
            weights.load(layer_no + 1, PROJ_W)
        hat, scale = normalise(middle)
        hat2[layer_no] = hat.astype(BF16)
        stats[layer_no] = jnp.where(lane == SCALE_LANE + 1, scale, stats[layer_no])
        normed2[layer_no, 0] = (hat * gain2[layer_no : layer_no + 1] + bias2[layer_no : layer_no + 1]).astype(BF16)

    def quarter_of(quarter):
        return slice(2 * half * quarter, 2 * half * quarter + 2 * half)

    def feed_forward(layer_no, quarter):
        if quarter == 0:
            weights.ready(layer_no, UP_W)
        columns = quarter_of(quarter)
        hidden_part = rows_by_columns(normed2[layer_no, 0], up_w[:, columns])
        share = 0.5 + 0.5 * lax.erf(hidden_part * 0.7071067811865476)
        active = (hidden_part * share).astype(BF16)
        slope = share + hidden_part * (0.3989422804014327 * jnp.exp(-0.5 * hidden_part * hidden_part))
        held[SLOPES][:, columns] = slope.astype(BF16)
        y, x = quarter // 2, quarter % 2
        acts[layer_no, x, 2 * y] = active[:, :half]
        acts[layer_no, x, 2 * y + 1] = active[:, half:]
        if quarter == 0:
            weights.ready(layer_no, DOWN_W)
        carried[...] += rows_by_columns(active, down_w[columns, :])


    def note(layer_no, row, values):
        sums[8 * layer_no + row : 8 * layer_no + row + 1] = jnp.sum(values, axis=0, keepdims=True)

    def norm_back(layer_no, number, grad, hat, scale):
        note(layer_no, 2 * number, grad * hat)
        note(layer_no, 2 * number + 1, grad)
        grad = grad * (gain1, gain2)[number][layer_no : layer_no + 1]
        mean = jnp.mean(grad, axis=-1, keepdims=True)
        slope = jnp.mean(grad * hat, axis=-1, keepdims=True)
        return scale * (grad - mean - hat * slope)

    def halves_of(values):
        return by_halves([values[:, tile_of(i)] for i in range(pairs)], first_head)

    def send_error(layer_no, values):
        for z0, tiles in enumerate(halves_of(values)):
            for i, tile in enumerate(tiles):
                own_errors[layer_no][:, tile_of(3 * z0 + i)] = tile.astype(BF16)
        error_swaps[layer_no].start()

    def hidden_back(layer_no):
        error = carried[...].astype(BF16)
        if layer_no < top:
            weights.ready(layer_no, DOWN_W)
        ready(layer_no, SLOPES)
        for quarter in range(4):
            grad = rows_by_rows(error, down_w[quarter_of(quarter), :])
            grad = grad * held[SLOPES][:, quarter_of(quarter)].astype(F32)
            grad_hidden[layer_no, quarter % 2, quarter // 2] = grad.astype(BF16)
        if layer_no > 0:
            weights.load(layer_no - 1, DOWN_W)
            load(layer_no - 1, SLOPES)

    def middle_back(layer_no):
        if layer_no < top:
            weights.ready(layer_no, UP_W)
        total = jnp.zeros((rows, width), F32)
        for quarter in range(4):
            total = total + rows_by_rows(grad_hidden[layer_no, quarter % 2, quarter // 2], up_w[:, quarter_of(quarter)])
        if layer_no > 0:
            weights.load(layer_no - 1, UP_W)
        carried[...] += norm_back(layer_no, 1, total, hat2[layer_no].astype(F32), stats[layer_no][:, SCALE_LANE + 1 : SCALE_LANE + 2])

    def project_back(layer_no):
        if layer_no < top:
            weights.ready(layer_no, PROJ_W)
        grad = rows_by_rows(carried[...].astype(BF16), proj_w[...])
        if layer_no > 0:
            weights.load(layer_no - 1, PROJ_W)
        deltas = jnp.zeros((rows, LANES), F32)
        for index in range(pairs):
            sl = tile_of(index)
            low_grad = grad[:, sl].astype(BF16)
            douts[layer_no, 0, :, sl] = low_grad
            product = low_grad.astype(F32) * mixed[layer_no, 0, :, sl].astype(F32)
            for member, mine in enumerate(heads_lanes):
                delta = jnp.sum(jnp.where(mine, product, 0.0), axis=1, keepdims=True)
                deltas = jnp.where(lane == 2 * index + member, delta, deltas)
        douts[layer_no, 0, :, width:] = spread_lanes(-deltas, lane, 0.0).astype(BF16)
        do_gathers[layer_no].start()
        kept_deltas.append(deltas)

    kept_deltas = []

    def middle_send(layer_no):
        for z0, tiles in enumerate(halves_of(carried[...])):
            for i, tile in enumerate(tiles):
                grad_middle(z0)[:, tile_of(i)] = tile.astype(BF16)
        middle_swaps[layer_no].start()

    def turned_back(layer_no, part, index, grad, forward):
        sl = tile_of(index)
        back = grad * held[ANGLES][0, :, sl] - partner_tile(grad, former) * held[ANGLES][1, :, sl]
        grad_qkv[:, part * width + LANES * index : part * width + LANES * index + LANES] = back.astype(BF16)
        return back, grad * partner_tile(forward.astype(F32), former)

    def note_turn(layer_no, index, turn, first):
        for row in range(2):
            at = 8 * layer_no + 4 + row
            total = jnp.sum(turn * marks[0][:, 1 + row : 2 + row].astype(F32), axis=0, keepdims=True)
            if not first:
                total = total + sums[at : at + 1, tile_of(index)]
            sums[at : at + 1, tile_of(index)] = total

    def split_half(part, tiles):
        for z0, group in enumerate(by_halves(tiles, first_head)):
            for i, tile in enumerate(group):
                half_qkv[part, z0, :, tile_of(i)] = tile.astype(BF16)

    def own_queries(layer_no):
        ready(layer_no, KEYS, VALUES, ANGLES, QUERIES)
        deltas = kept_deltas[-1]
        key_marks = marks[...].reshape(4 * rows, LANES)
        backs = []
        for index in range(pairs):
            sl = tile_of(index)
            query_pair = held[QUERIES][0, :, sl]
            key_pair = held[KEYS][:, :, sl].reshape(4 * rows, LANES)
            value_pair = held[VALUES][:, :, sl].reshape(4 * rows, LANES)
            grad_pair = douts[layer_no, 0, :, sl]
            extended = jnp.concatenate([key_pair, key_marks], axis=1)
            scores = rows_by_rows(jnp.concatenate([both(query_pair), one_lane], axis=1), extended)
            weight = jnp.exp(scores - columns_of(stats[layer_no], index))
            grad = rows_by_rows(both(grad_pair), value_pair)
            grad = (weight * (grad - columns_of(deltas, index))).astype(BF16)
            grad = 0.125 * beside(rows_by_columns(grad, key_pair))
            back, turn = turned_back(layer_no, 0, index, grad, 8.0 * query_pair.astype(F32))
            note_turn(layer_no, index, turn, True)
            backs.append(back)
        split_half(0, backs)

    def own_keys(layer_no):
        do_gathers[layer_no].near()
        do_gathers[layer_no].last()
        if layer_no == top:
            log_gathers[layer_no].near()
            log_gathers[layer_no].last()
        own_marks = jnp.broadcast_to(jnp.concatenate([marks[0][:, 0:1]] * 2, axis=0), (2 * rows, LANES))
        key_backs, value_backs = [], []
        for index in range(pairs):
            sl = tile_of(index)
            key_pair, value_pair = held[KEYS][0, :, sl], held[VALUES][0, :, sl]
            query_pair = held[QUERIES][:, :, sl].reshape(4 * rows, LANES)
            grad_pair = douts[layer_no, :, :, sl].reshape(4 * rows, LANES)
            queries = jnp.concatenate([query_pair, logs_low[layer_no].reshape(4 * rows, LANES)], axis=1)
            grads = jnp.concatenate([grad_pair, douts[layer_no, :, :, width:].reshape(4 * rows, LANES)], axis=1)
            head = jnp.where(upper, 2 * index, 2 * index + 1)
            chosen = jnp.where((two_lane < 48) & (lax.rem(two_lane, 16) == head), 1.0, 0.0).astype(BF16)
            marked = jnp.where(two_lane == 127, own_marks, chosen)
            weight = jnp.exp(rows_by_rows(jnp.concatenate([both(key_pair), marked], axis=1), queries))
            grad = rows_by_rows(jnp.concatenate([both(value_pair), chosen], axis=1), grads)
            value_grad = beside(rows_by_columns(weight.astype(BF16), grad_pair))
            grad = beside(rows_by_columns((weight * grad).astype(BF16), query_pair))
            back, turn = turned_back(layer_no, 1, index, grad, key_pair)
            note_turn(layer_no, index, turn, False)
            key_backs.append(back)
            grad = value_grad
            grad_qkv[:, 2 * width + LANES * index : 2 * width + LANES * index + LANES] = grad.astype(BF16)
            value_backs.append(grad)
        split_half(1, key_backs)
        split_half(2, value_backs)
        if layer_no > 0:
            load(layer_no - 1, KEYS, VALUES, ANGLES, QUERIES)

    def input_back(layer_no):
        if layer_no < top:
            weights.ready(layer_no, QUERY_W, KEY_W, VALUE_W)
        total = rows_by_rows(grad_qkv[...], qkv_w[...])
        if layer_no > 0:
            weights.load(layer_no - 1, QUERY_W, KEY_W, VALUE_W)
        carried[...] += norm_back(layer_no, 0, total, hat1[layer_no].astype(F32), stats[layer_no][:, SCALE_LANE : SCALE_LANE + 1])
        if layer_no > 0:
            send_error(layer_no - 1, carried[...])

    def put(layer_no, name, values, column, blocks, skipped=0):
        share = reductions[layer_no, name].share
        for first_row, count, tile in blocks:
            for i in range(values.shape[1] // LANES):
                piece = values[first_row - skipped : first_row - skipped + count, tile_of(i)].astype(BF16)
                at_tile, at_row = column(tile, i)
                share[at_tile, at_row : at_row + count] = piece

    def blocks_of(name):
        n, axes = plans[name][0], HALVING[name]
        blocks = []
        for number in range(8):
            bits = (number % 2, (number // 2) % 2, number // 4)
            tile = ((bits[axes[0]] * 2 + bits[axes[1]]) * 2 + bits[axes[2]]) * n
            blocks.append((number * size, size, tile))
        return blocks

    def down_product(layer_no):
        error_swaps[layer_no].arrive()
        if layer_no == top:
            for part in acts_swaps[layer_no]:
                part.arrive()
        for y in range(2):
            for c in range(2):
                for z0 in range(2):
                    columns = slice(z0 * width // 2, (z0 + 1) * width // 2)
                    product = columns_by_columns(
                        acts[layer_no, place.x, 2 * y + c], own_errors[layer_no][:, columns]
                    ) + columns_by_columns(far_acts[layer_no, 2 * y + c], errors[layer_no, :, columns])
                    tile = ((2 * c + y) * 2 + z0) * 3
                    for part in range(2):
                        block = (half // 2 * part, half // 2, tile)
                        put(layer_no, DOWN_A + part, product, lambda tile, i: (tile + i, 0), [block])
        reductions[layer_no, DOWN_A].start()
        reductions[layer_no, DOWN_B].start()

    def up_product(layer_no, part):
        hidden_swaps[layer_no][part].arrive()
        if layer_no == top and part == 0:
            normed_swaps[layer_no].arrive()
        columns = pl.ds(half * part, half)
        for z1 in range(2):
            for side in range(2):
                inputs = slice(side * 4 * size, side * 4 * size + 4 * size)
                product = columns_by_columns(
                    normed2[layer_no, 0, :, inputs], grad_hidden[layer_no, place.z0, z1, :, columns]
                ) + columns_by_columns(normed2[layer_no, 1, :, inputs], far_hidden[layer_no, z1, :, columns])
                put(
                    layer_no,
                    UP_A + part,
                    product,
                    lambda tile, i: (tile + z1, size * i),
                    blocks_of(UP_A + part)[4 * side : 4 * side + 4],
                    4 * size * side,
                )
        reductions[layer_no, UP_A + part].start()
        hidden_swaps[layer_no][part].drain()

    def narrow_product(layer_no, name, left, right, far):
        blocks = blocks_of(name)
        for side in range(2):
            columns = slice(side * 4 * size, side * 4 * size + 4 * size)
            product = columns_by_columns(left[0][:, columns], right) + columns_by_columns(left[1][:, columns], far)
            put(layer_no, name, product, lambda tile, i: (tile + i, 0), blocks[4 * side : 4 * side + 4], 4 * size * side)
        reductions[layer_no, name].start()

    def proj_product(layer_no):
        middle_swaps[layer_no].arrive()
        if layer_no == top:
            mixed_swaps[layer_no].arrive()
        left = (mixed.at[layer_no, 0], mixed.at[layer_no, 1])
        narrow_product(layer_no, PROJ, left, grad_middle(place.z0)[...], far_middle[layer_no])
        middle_swaps[layer_no].drain()

    def part_product(layer_no, part):
        qkv_swaps[layer_no][part].arrive()
        left = (normed.at[layer_no, 0], normed.at[layer_no, 2])
        narrow_product(layer_no, QUERY + part, left, half_qkv[part, place.z0], far_qkv[layer_no, part])
        qkv_swaps[layer_no][part].drain()

    def hand_out(layer_no, name):
        if name < UP_A:
            target = results[0].at[layer_no, pl.ds(half // 2 * (name - DOWN_A), half // 2)]
        elif name < PROJ:
            target = results[1].at[layer_no, :, pl.ds(half * (name - UP_A), half)]
        else:
            target = results[name - 2].at[layer_no]
        return pltpu.make_async_copy(stagings[name], target, stage_sems.at[name])

    def finish(layer_no, name):
        target = stagings[name]
        if layer_no < top:
            hand_out(layer_no + 1, name).wait()

        def write(own, rest=None):
            if rest is None:
                for part in range(own.shape[0] // size):
                    target[:, tile_of(part)] = own[size * part : size * part + size]
            else:
                target[:, :LANES] = own
                target[:, LANES : LANES + 64] = rest

        reductions[layer_no, name].finish(write)
        hand_out(layer_no, name).start()

    def step(layer_no, name, stage):
        reductions[layer_no, name].step(stage)

    def return_grad():
        out_return.wait()
        returned[...] = carried[...].astype(BF16)
        grad_return.start()

    def low_arrivals():
        log_gathers[low].last()
        for one in [mixed_swaps[low], normed_swaps[low]] + acts_swaps[low]:
            one.arrive()

    mark_arrival.start()
    arrival.start()
    sums[...] = jnp.zeros(sums.shape, F32)
    mark_arrival.wait()
    mark_gather.start()
    make_angles(0, 0)
    arrival.wait()
    carried[...] = start[...].astype(F32)
    normalise_first(0)
    weights.ready(0, KEY_W, VALUE_W, QUERY_W)
    project(0, 0)
    mark_gather.near()
    mark_gather.far()
    make_angles(0, 1)
    h_gathers[0].near()
    project(0, 1)
    make_angles(0, 2)
    mark_gather.last()
    make_angles(0, 3)
    h_gathers[0].far()
    other_arrival.start()
    project(0, 2)
    h_gathers[0].last()
    project(0, 3)
    weights.load(1, KEY_W, VALUE_W, QUERY_W)
    for name in (KEYS, VALUES, QUERIES, ANGLES):
        spill(name).start()
    attend(0)
    mixed_swaps[0].start()
    project_out(0)
    for quarter in range(4):
        feed_forward(0, quarter)
    weights.load(1, UP_W, DOWN_W)
    spill(SLOPES).start()
    for part in acts_swaps[0]:
        part.start()
    normalise_first(1)
    normed_swaps[0].start()
    log_gathers[0].start()
    for name in (KEYS, VALUES, QUERIES, ANGLES):
        spill(name).wait()
    make_angles(1, 0)
    weights.ready(1, KEY_W, VALUE_W, QUERY_W)
    project(1, 0)
    make_angles(1, 1)
    h_gathers[1].near()
    project(1, 1)
    make_angles(1, 2)
    make_angles(1, 3)
    other_arrival.wait()
    send_error(1, returned[...].astype(F32))
    h_gathers[1].far()
    project(1, 2)
    h_gathers[1].last()
    project(1, 3)
    log_gathers[0].near()
    log_gathers[0].far()
    attend(1)
    log_gathers[1].start()
    mixed_swaps[1].start()
    project_out(1)
    normed_swaps[1].start()
    spill(SLOPES).wait()
    feed_forward(1, 0)
    feed_forward(1, 1)
    acts_swaps[1][0].start()
    feed_forward(1, 2)
    feed_forward(1, 3)
    acts_swaps[1][1].start()
    start[...] = carried[...].astype(BF16)
    carried[...] = returned[...].astype(F32)
    low_arrivals()
    hidden_back(top)
    middle_back(top)
    project_back(top)
    own_queries(top)
    hidden_swaps[top][0].start()
    middle_send(top)
    log_gathers[top].far()
    qkv_swaps[top][0].start()
    out_return.start()
    hidden_swaps[top][1].start()
    down_product(top)
    do_gathers[top].far()
    step(top, DOWN_A, 0)
    step(top, DOWN_B, 0)
    own_keys(top)
    up_product(top, 0)
    qkv_swaps[top][1].start()
    qkv_swaps[top][2].start()
    input_back(top)
    hidden_back(low)
    middle_back(low)
    project_back(low)
    step(top, DOWN_A, 1)
    hidden_swaps[low][1].start()
    part_product(top, 0)
    step(top, UP_A, 0)
    hidden_swaps[low][0].start()
    own_queries(low)
    step(top, DOWN_B, 1)
    qkv_swaps[low][0].start()
    step(top, QUERY, 0)
    down_product(low)
    up_product(top, 1)
    proj_product(top)
    part_product(top, 1)
    middle_send(low)
    step(low, DOWN_A, 0)
    step(low, DOWN_B, 0)
    part_product(top, 2)
    step(top, QUERY, 1)
    step(top, UP_A, 1)
    step(top, UP_B, 0)
    step(top, PROJ, 0)
    step(top, KEY, 0)
    step(top, VALUE, 0)
    do_gathers[low].far()
    step(top, QUERY, 2)
    own_keys(low)
    finish(top, QUERY)
    step(low, DOWN_A, 1)
    qkv_swaps[low][1].start()
    qkv_swaps[low][2].start()
    step(top, DOWN_A, 2)
    step(top, UP_B, 1)
    input_back(low)
    doubling.start()
    up_product(low, 1)
    return_grad()
    doubling.step(0)
    step(top, PROJ, 1)
    step(low, DOWN_B, 1)
    step(low, UP_B, 0)
    step(top, UP_A, 2)
    step(top, KEY, 1)
    up_product(low, 0)
    finish(top, DOWN_A)
    doubling.step(1)
    step(low, UP_A, 0)
    step(top, VALUE, 1)
    step(top, DOWN_B, 2)
    part_product(low, 0)
    step(top, UP_B, 2)
    finish(top, UP_A)
    step(low, UP_B, 1)
    proj_product(low)
    step(low, QUERY, 0)
    step(top, PROJ, 2)
    step(top, KEY, 2)
    step(low, PROJ, 0)
    doubling.step(2)
    finish(top, DOWN_B)
    step(low, DOWN_A, 2)
    finish(top, UP_B)
    step(low, UP_B, 2)
    part_product(low, 1)
    step(low, UP_A, 1)
    finish(top, PROJ)
    step(top, VALUE, 2)
    step(low, KEY, 0)
    step(low, QUERY, 1)
    finish(top, KEY)
    part_product(low, 2)
    step(low, PROJ, 1)
    step(low, VALUE, 0)
    finish(low, DOWN_A)
    step(low, UP_A, 2)
    step(low, KEY, 1)
    finish(low, UP_B)
    step(low, PROJ, 2)
    step(low, QUERY, 2)
    finish(top, VALUE)
    step(low, VALUE, 1)
    step(low, DOWN_B, 2)
    step(low, KEY, 2)
    finish(low, UP_A)
    finish(low, PROJ)
    step(low, VALUE, 2)
    finish(low, QUERY)
    doubling.step(3)
    finish(low, DOWN_B)
    finish(low, KEY)
    finish(low, VALUE)
    doubling.step(4)
    grad_small[...] = sums[...]
    grad_return.wait()
    for name in TENSORS:
        hand_out(low, name).wait()
    for red in reductions.values():
        red.drain()
    for gather in [mark_gather] + h_gathers + log_gathers + do_gathers:
        gather.drain()
    for one in error_swaps + mixed_swaps + normed_swaps + acts_swaps[low] + acts_swaps[top]:
        one.drain()


def encoder_call(patches, cotangent, keep, coords, norms, freqs, whole):
    layers = freqs.shape[0]
    rows, width = patches.shape
    hidden = whole[4].shape[2]
    size, quarter = width // 8, width // 4
    plans = tile_plan(width, hidden)
    tensors = plans * layers
    sem = pltpu.SemaphoreType.DMA
    any_spec, vmem_spec = pl.BlockSpec(memory_space=pl.ANY), pl.BlockSpec(memory_space=pltpu.VMEM)
    finals = [(hidden // 8, quarter), (size, hidden // 4)] + [(size, quarter)] * 4
    parts = [(hidden // 16, quarter)] * 2 + [(size, hidden // 8)] * 2 + [(size, quarter)] * 4
    outs = (
        [jax.ShapeDtypeStruct((rows, width), BF16)] * 2
        + [jax.ShapeDtypeStruct((layers,) + shape, F32) for shape in finals]
        + [jax.ShapeDtypeStruct((8 * layers, width), F32)]
        + [jax.ShapeDtypeStruct(*shape) for shape in spilled_shapes(rows, width, hidden)]
    )

    def low(*shape):
        return pltpu.VMEM(shape, BF16)

    def full(*shape):
        return pltpu.VMEM(shape, F32)

    return pl.pallas_call(
        lambda *refs: encoder_kernel(layers, *refs),
        out_shape=outs,
        in_specs=[any_spec, any_spec] + [vmem_spec] * 7 + [any_spec] * 6,
        out_specs=[any_spec] * 8 + [vmem_spec] + [any_spec] * 5,
        scratch_shapes=[pltpu.VMEM(*shape) for shape in spilled_shapes(rows, width, hidden)]
        + [low(8 * n, count, LANES) for n, count in tensors]
        + [low(landing_count(n), count, LANES) for n, count in tensors]
        + [low(4 * n, count, LANES) for n, count in plans]
        + [full(*shape) for shape in parts]
        + [low(width, 3 * width), low(width, width), low(width, hidden), low(hidden, width)]
        + [sem((6,)), sem((5,)), sem((5,)), sem((len(plans),))]
        + [
            low(layers, 4, rows, width),
            low(layers, 4, rows, LANES),
            low(layers, 2, rows, width),
            low(layers, 2, rows, width),
            low(layers, 2, 4, rows, hidden // 8),
            low(layers, 4, rows, hidden // 8),
            low(layers, rows, width),
            low(layers, rows, width),
            full(layers, rows, LANES),
        ]
        + [low(rows, width), low(rows, LANES), low(4, rows, LANES), low(rows, width), sem((5, 3))]
        + [sem((layers, 4))] * 6
        + [sem((4,))] * 2
        + [
            low(layers, 4, rows, width + LANES),
            low(layers, rows, width),
            low(layers, 2, 2, rows, width),
            low(layers, 2, rows, width),
            low(layers, rows, width // 2),
            low(rows, 3 * width),
            low(3, 2, rows, width // 2),
            low(layers, 3, rows, width // 2),
        ]
        + [sem((layers, 11, 2)), sem((len(tensors), 5)), sem((len(tensors), 5))]
        + [pltpu.SemaphoreType.REGULAR((len(plans),))]
        + [full(rows, width), full(8 * layers, width), full(5, 8 * layers, width), sem((5, 2))],
        compiler_params=pltpu.CompilerParams(
            collective_id=0, has_side_effects=True, vmem_limit_bytes=VMEM_BYTES
        ),
    )(patches, cotangent, keep, coords, *norms, freqs, *whole)


def beyond_eight(result):
    dp_size = lax.axis_size(DP)
    groups = dp_size // 8
    if groups == 1:
        return result
    result = lax.psum(result, DP, axis_index_groups=[[g * 8 + i for g in range(groups)] for i in range(8)])
    whole = lax.all_gather(
        result, DP, axis=1, tiled=True, axis_index_groups=[[g * 8 + i for i in range(8)] for g in range(groups)]
    )
    rows = whole.shape[1] // dp_size
    return lax.dynamic_slice_in_dim(whole, lax.axis_index(DP) * rows, rows, axis=1)


def final_kernel(count, *refs):
    output, grad_patches, small = refs[:3]
    large = refs[3 : 3 + count]
    refs = refs[3 + count :]
    out_copy, grad_copy = refs[:2]
    large_copies = refs[2 : 2 + count]
    norms, turns = refs[2 + count : 6 + count], refs[6 + count]
    out_copy[...] = output[...]
    grad_copy[...] = grad_patches[...].astype(F32)
    for source, target in zip(large[:-1], large_copies[:-1]):
        target[...] = source[...]
    layers, columns = norms[0].shape
    for layer_no in range(layers):
        large_copies[-1][layer_no] = large[-1][layer_no].T
    at = lax.axis_index(BLK)
    half = turns.shape[3]
    for blk in range(small.shape[1] // columns):

        @pl.when(at == blk)
        def _(blk=blk):
            for layer_no in range(layers):
                mine = small[8 * layer_no : 8 * layer_no + 8, blk * columns : blk * columns + columns]
                for row, norm in enumerate(norms):
                    norm[layer_no : layer_no + 1] = mine[row : row + 1]
                for row in range(2):
                    for head in range(turns.shape[1]):
                        pair = mine[4 + row : 5 + row, 2 * half * head : 2 * half * head + 2 * half]
                        turns[layer_no, head, row : row + 1] = pair[:, half:] - pair[:, :half]


def final_call(output, grad_patches, small, large, half):
    vmem_spec = pl.BlockSpec(memory_space=pltpu.VMEM)
    layers = small.shape[0] // 8
    columns = small.shape[1] // lax.axis_size(BLK)
    return pl.pallas_call(
        lambda *refs: final_kernel(len(large), *refs),
        out_shape=[
            jax.ShapeDtypeStruct(output.shape, output.dtype),
            jax.ShapeDtypeStruct(grad_patches.shape, F32),
        ]
        + [jax.ShapeDtypeStruct(a.shape, F32) for a in large[:-1]]
        + [jax.ShapeDtypeStruct((layers,) + large[-1].shape[:0:-1], F32)]
        + [jax.ShapeDtypeStruct((layers, columns), F32)] * 4
        + [jax.ShapeDtypeStruct((layers, columns // (2 * half), 2, half), F32)],
        in_specs=[vmem_spec] * (3 + len(large)),
        out_specs=[vmem_spec] * (7 + len(large)),
    )(output, grad_patches, small, *large)


def shards(
    patches,
    keep,
    coords,
    query_w,
    key_w,
    value_w,
    proj_w,
    up_w,
    down_w,
    norm1_gain,
    norm1_bias,
    norm2_gain,
    norm2_bias,
    freqs,
    cotangent,
):
    whole = (query_w, key_w, value_w, proj_w, up_w, down_w)
    norms = (norm1_gain, norm1_bias, norm2_gain, norm2_bias)
    results = encoder_call(patches[0], cotangent[0], keep, coords, norms, jnp.swapaxes(freqs, 1, 2), whole)
    output, grad_patches, grad_down, grad_up, *others, small = results[:9]
    large = [beyond_eight(grad) for grad in (*others[1:], others[0], grad_up, grad_down)]
    groups = lax.axis_size(DP) // 8
    if groups > 1:
        small = lax.psum(small, DP, axis_index_groups=[[g * 8 + i for g in range(groups)] for i in range(8)])
    output, grad_patches, *rest = final_call(output, grad_patches, small, large, freqs.shape[3])
    rest[5], rest[-1] = jnp.swapaxes(rest[5], 1, 2), jnp.swapaxes(rest[-1], 1, 2)
    return (output[None], grad_patches[None], *rest)


def solution(mesh):
    block = P(DP, BLK, None)
    placed = (block, P(DP, BLK), P(None, DP, BLK)) + (P(),) * 11 + (block,)
    results = (block, block) + (P(None, DP, BLK),) * 6 + (P(None, BLK),) * 4 + (P(None, None, BLK, None),)
    return jax.shard_map(shards, mesh=mesh, in_specs=placed, out_specs=results, check_vma=False)
```

```python
import jax
import jax.numpy as jnp
from jax import lax
from jax.experimental import pallas as pl
from jax.experimental.pallas import tpu as pltpu
from jax.sharding import PartitionSpec as P

MESH = pl.DeviceIdType.MESH
DP, BLK = "dp", "blk"
C, X, Y, Z0, Z1 = range(5)
BF16, F32 = jnp.bfloat16, jnp.float32
MASKED_SCORE = -1e30
NORM_EPSILON = 1e-06
LANES = 128
SCALE_LANE = 64
VMEM_BYTES = 127 * 512 * 1024


def rows_by_columns(left, right):
    return lax.dot_general(left, right, (((1,), (0,)), ((), ())), preferred_element_type=F32)


def rows_by_rows(left, right):
    return lax.dot_general(left, right, (((1,), (1,)), ((), ())), preferred_element_type=F32)


def columns_by_columns(left, right):
    return lax.dot_general(left, right, (((0,), (0,)), ((), ())), preferred_element_type=F32)


class Place:
    def __init__(self):
        self.dp = lax.axis_index(DP)
        self.blk = lax.axis_index(BLK)
        self.c = lax.rem(self.dp, 2)
        self.x = lax.rem(self.dp // 2, 2)
        self.y = lax.rem(self.dp // 4, 2)
        self.z0 = lax.rem(self.blk, 2)
        self.z1 = lax.rem(self.blk // 2, 2)
        self.bits = (self.c, self.x, self.y, self.z0, self.z1)
        self.worker = (self.dp - self.c + self.z0, 2 * self.c + self.z1)
        self.owner = (self.dp - self.c + self.z1, 2 * self.z0 + self.c)
        self.stays = (self.worker[0] == self.dp) & (self.worker[1] == self.blk)

    def other(self, axis):
        if axis <= Y:
            return (self.dp + (1 << axis) * (1 - 2 * self.bits[axis]), self.blk)
        return (self.dp, self.blk + (1 << axis - Z0) * (1 - 2 * self.bits[axis]))

    def greet(self, axes):
        barrier = pltpu.get_barrier_semaphore()
        mine = 2 * self.blk + self.c
        for step in range(1, 8):
            them = lax.rem(mine + step, 8)
            pl.semaphore_signal(
                barrier, inc=1, device_id=(self.dp - self.c + lax.rem(them, 2), them // 2), device_id_type=MESH
            )
        for axis in axes:
            pl.semaphore_signal(barrier, inc=1, device_id=self.other(axis), device_id_type=MESH)
        pl.semaphore_wait(barrier, 7 + len(axes))


class Relocation:
    def __init__(self, place, source, target, sems, back=False):
        self.place, self.source, self.target, self.sems = place, source, target, sems
        self.device = place.owner if back else place.worker

    def remote(self):
        return pltpu.make_async_remote_copy(
            src_ref=self.source,
            dst_ref=self.target,
            send_sem=self.sems.at[0],
            recv_sem=self.sems.at[1],
            device_id=self.device,
            device_id_type=MESH,
        )

    def local(self):
        return pltpu.make_async_copy(self.source, self.target, self.sems.at[2])

    def start(self):
        pl.when(self.place.stays)(lambda: self.local().start())
        pl.when(jnp.logical_not(self.place.stays))(lambda: self.remote().start())

    def wait(self):
        pl.when(self.place.stays)(lambda: self.local().wait())
        pl.when(jnp.logical_not(self.place.stays))(lambda: self.remote().wait())


class Gather:
    def __init__(self, place, slots, sends, receives):
        self.place, self.slots, self.sends, self.receives = place, slots, sends, receives

    def copy(self, source, slot, axis):
        return pltpu.make_async_remote_copy(
            src_ref=self.slots.at[source],
            dst_ref=self.slots.at[slot],
            send_sem=self.sends.at[slot],
            recv_sem=self.receives.at[slot],
            device_id=self.place.other(axis),
            device_id_type=MESH,
        )

    def start(self):
        self.copy(0, 2, Z0).start()
        self.copy(0, 1, C).start()

    def near(self):
        self.copy(0, 1, C).wait_recv()

    def far(self):
        self.copy(0, 2, Z0).wait_recv()
        self.copy(2, 3, C).start()

    def last(self):
        self.copy(2, 3, C).wait_recv()

    def drain(self):
        self.copy(0, 1, C).wait_send()
        self.copy(0, 2, Z0).wait_send()
        self.copy(2, 3, C).wait_send()


class Swap:
    def __init__(self, place, axis, source, target, sems):
        self.place, self.axis, self.source, self.target, self.sems = place, axis, source, target, sems

    def copy(self):
        return pltpu.make_async_remote_copy(
            src_ref=self.source,
            dst_ref=self.target,
            send_sem=self.sems.at[0],
            recv_sem=self.sems.at[1],
            device_id=self.place.other(self.axis),
            device_id_type=MESH,
        )

    def start(self):
        self.copy().start()

    def arrive(self):
        self.copy().wait_recv()

    def drain(self):
        self.copy().wait_send()


def lane_index(rows):
    return lax.broadcasted_iota(jnp.int32, (rows, LANES), 1)


def partner_tile(tile, former):
    return jnp.where(former, pltpu.roll(tile, 96, 1), pltpu.roll(tile, 32, 1))


def rotate_tile(tile, cosine, signed_sine, former):
    return tile * cosine + partner_tile(tile, former) * signed_sine


def tile_of(index):
    return slice(LANES * index, LANES * index + LANES)


def normalise(values):
    centre = values - jnp.mean(values, axis=-1, keepdims=True)
    spread = jnp.mean(centre * centre, axis=-1, keepdims=True)
    scale = lax.rsqrt(spread + NORM_EPSILON)
    return centre * scale, scale


QUERY_W, KEY_W, VALUE_W, PROJ_W, UP_W, DOWN_W = range(6)


class Weights:
    def __init__(self, whole, qkv, proj, up, down, sems):
        width = qkv.shape[1] // 3
        self.whole, self.sems = whole, sems
        self.buffers = [qkv.at[:, pl.ds(part * width, width)] for part in range(3)] + [proj, up, down]

    def copy(self, name, layer_no):
        return pltpu.make_async_copy(self.whole[name].at[layer_no], self.buffers[name], self.sems.at[name])

    def load(self, layer_no, *names):
        for name in names:
            self.copy(name, layer_no).start()

    def ready(self, layer_no, *names):
        for name in names:
            self.copy(name, layer_no).wait()


def spread_lanes(columns, lane, last):
    columns = jnp.where(lane < 16, columns, 0.0)
    high = columns.astype(BF16).astype(F32)
    middle = (columns - high).astype(BF16).astype(F32)
    low = columns - high - middle
    spread = high + pltpu.roll(middle, 16, 1) + pltpu.roll(low, 32, 1)
    return jnp.where(lane == 127, last, spread)


class Reduction:
    def __init__(self, place, axes, n, share, first_landing, landing, sends, receives, credit, gives, takes):
        self.place, self.axes = place, axes + (Z1, Z1)
        self.share, self.first_landing, self.landing = share, first_landing, landing
        self.sends, self.receives = sends, receives
        self.credit, self.gives, self.takes = credit, gives, takes
        self.n, self.rows = n, share.shape[1]
        self.plan = []
        base, half, land = 0, 4 * n, 0
        for axis in axes:
            bit = place.bits[axis]
            self.plan.append((base + (1 - bit) * half, base + bit * half, half, land))
            base, land, half = base + bit * half, land + half if self.plan[1:] else 0, half // 2
        self.spare = self.plan[0][0]
        self.base, self.land = base, land
        self.plan.append((base + (n - 1) * (1 - place.z1), base + (n - 1) * place.z1, 1, land))

    def copy(self, stage):
        if stage < 4:
            send, _, count, land = self.plan[stage]
            landing = self.first_landing if stage == 0 else self.landing
            source, target = self.share.at[pl.ds(send, count)], landing.at[pl.ds(land, count)]
        else:
            half = pl.ds(0, self.rows // 2)
            source, target = self.share.at[self.spare, half], self.landing.at[self.land + 1, half]
        return pltpu.make_async_remote_copy(
            src_ref=source,
            dst_ref=target,
            send_sem=self.sends.at[stage],
            recv_sem=self.receives.at[stage],
            device_id=self.place.other(self.axes[stage]),
            device_id_type=MESH,
        )

    def start(self, stage=0):
        if stage == 0 and self.takes:
            pl.semaphore_wait(self.credit, 1)
        self.copy(stage).start()

    def step(self, stage):
        _, keep, count, land = self.plan[stage]
        self.copy(stage).wait_recv()

        landing = self.first_landing if stage == 0 else self.landing

        def body(i, carry):
            self.share[keep + i] = self.share[keep + i] + landing[land + i]
            return carry

        lax.fori_loop(0, count, body, 0)
        self.start(stage + 1)
        if stage == 0:
            self.copy(0).wait_send()
            if self.gives:
                pl.semaphore_signal(self.credit, inc=1, device_id=self.place.other(C), device_id_type=MESH)
        if stage == 2 and self.n == 3:
            half = self.rows // 2
            shared = self.share[self.base + 1].astype(F32)
            upper, lower = shared[:half], shared[half:]
            first = lane_index(half) < 64
            low_lanes = jnp.where(first, upper, pltpu.roll(lower, 64, 1))
            high_lanes = jnp.where(first, pltpu.roll(upper, 64, 1), lower)
            self.share[self.spare, :half] = jnp.where(self.place.z1 == 1, low_lanes, high_lanes).astype(BF16)
            self.start(4)

    def finish(self, write):
        self.copy(3).wait_recv()
        _, keep, _, land = self.plan[3]
        own = self.share[keep].astype(F32) + self.landing[land].astype(F32)
        if self.n == 2:
            write(own)
            return
        self.copy(4).wait_recv()
        half = self.rows // 2
        packed = self.landing[self.land + 1, :half].astype(F32)
        shared = self.share[self.base + 1].astype(F32)
        shared = jnp.where(self.place.z1 == 0, shared, pltpu.roll(shared, 64, 1))
        rest = shared + jnp.concatenate([packed, pltpu.roll(packed, 64, 1)], axis=0)
        write(own, rest[:, :64])

    def drain(self):
        for stage in range(1, 4 if self.n == 2 else 5):
            self.copy(stage).wait_send()


class Doubling:
    AXES = (C, X, Y, Z0, Z1)

    def __init__(self, place, sums, landing, sems):
        self.place, self.sums, self.landing, self.sems = place, sums, landing, sems

    def copy(self, stage):
        return pltpu.make_async_remote_copy(
            src_ref=self.sums,
            dst_ref=self.landing.at[stage],
            send_sem=self.sems.at[stage, 0],
            recv_sem=self.sems.at[stage, 1],
            device_id=self.place.other(self.AXES[stage]),
            device_id_type=MESH,
        )

    def start(self):
        self.copy(0).start()

    def step(self, stage):
        self.copy(stage).wait()
        self.sums[...] += self.landing[stage]
        if stage + 1 < len(self.AXES):
            self.copy(stage + 1).start()


TENSORS = DOWN_A, DOWN_B, UP_A, UP_B, PROJ, QUERY, KEY, VALUE = range(8)
HALVING = ((C, Y, Z0),) * 2 + ((C, X, Y),) * 3 + ((C, Y, X), (C, X, Y), (C, Y, X))


def tile_plan(width, hidden):
    size = width // 8
    return ((3, hidden // 16),) * 2 + ((2, size * (hidden // 8 // LANES)),) * 2 + ((3, size),) * 4


def landing_count(n):
    return 2 * n + n + n - 1


def by_halves(tiles, first):
    def turned(tile):
        return pltpu.roll(tile, 64, 1)

    return (
        (tiles[0], jnp.where(first, tiles[1], turned(tiles[4])), tiles[3]),
        (
            jnp.where(first, turned(tiles[1]), turned(tiles[2])),
            jnp.where(first, turned(tiles[2]), tiles[5]),
            jnp.where(first, turned(tiles[4]), turned(tiles[5])),
        ),
    )


KEYS, VALUES, QUERIES, ANGLES, SLOPES = SPILLED = range(5)


def spilled_shapes(rows, width, hidden):
    return (
        ((4, rows, width), BF16),
        ((4, rows, width), BF16),
        ((4, rows, width), BF16),
        ((2, rows, width), F32),
        ((rows, hidden), BF16),
    )


def encoder_kernel(layers, *refs):
    patches, cotangent, keep, coords, gain1, bias1, gain2, bias2, freqs = refs[:9]
    whole = refs[9:15]
    output, grad_patches = refs[15:17]
    results = refs[17:23]
    grad_small = refs[23]
    saved = refs[24:29]
    held = refs[29:34]
    refs = refs[34:]
    count = layers * len(TENSORS)
    shares, landings, first_landings = refs[:count], refs[count : 2 * count], refs[2 * count : 2 * count + len(TENSORS)]
    refs = refs[2 * count + len(TENSORS) :]
    stagings = refs[: len(TENSORS)]
    refs = refs[len(TENSORS) :]
    (qkv_w, proj_w, up_w, down_w, w_sems, spill_sems, load_sems, stage_sems) = refs[:8]
    (normed, logs_low, mixed, normed2, acts, far_acts, hat1, hat2, stats) = refs[8:17]
    (start, own_marks, marks, returned, relocation_sems) = refs[17:22]
    (h_sends, h_receives, do_sends, do_receives, q_sends, q_receives, m_sends, m_receives) = refs[22:30]
    (douts, errors, grad_hidden, far_hidden, far_middle, grad_qkv, half_qkv, far_qkv) = refs[30:38]
    (swap_sems, sends, receives, credits, carried, sums, sums_landing, sums_sems) = refs[38:]
    place = Place()
    rows, width = carried.shape
    hidden = up_w.shape[1]
    half = hidden // 8
    size = width // 8
    pairs = width // LANES
    top, low = layers - 1, layers - 2
    weights = Weights(whole, qkv_w, proj_w, up_w, down_w, w_sems)
    weights.load(0, KEY_W, VALUE_W, QUERY_W, PROJ_W, UP_W, DOWN_W)
    line = lax.broadcasted_iota(jnp.int32, (LANES, rows), 0)
    own = jnp.where(line == 0, jnp.where(keep[...] > 0, 0.0, MASKED_SCORE), 0.0)
    for number in range(2):
        own = jnp.where(line == 1 + number, coords[number].astype(F32), own)
    own_marks[...] = own.T.astype(BF16)
    place.greet((X, Y))

    lane = lane_index(rows)
    former = lax.rem(lane, 64) < 32
    first_head = lane < 64
    heads_lanes = (first_head, jnp.logical_not(first_head))
    two_lane = lane_index(2 * rows)
    upper = lax.broadcasted_iota(jnp.int32, (2 * rows, LANES), 0) < rows
    one_lane = jnp.where(two_lane == 0, 1.0, 0.0).astype(BF16)

    def both(tile):
        return jnp.where((two_lane < 64) == upper, jnp.concatenate([tile, tile], axis=0), jnp.zeros((), tile.dtype))

    def beside(values):
        return jnp.where(first_head, values[:rows], values[rows:])

    def columns_of(values, index):
        return jnp.concatenate([values[:, 2 * index : 2 * index + 1], values[:, 2 * index + 1 : 2 * index + 2]], axis=0)

    plans = tile_plan(width, hidden)
    away = 1 - place.z0

    def relocation(number, source, target, back=False):
        return Relocation(place, source, target, relocation_sems.at[number], back)

    def swap(layer_no, number, axis, source, target):
        return Swap(place, axis, source, target, swap_sems.at[layer_no, number])

    every = range(layers)

    def grad_middle(z0):
        return normed.at[top, 1, :, pl.ds(pl.multiple_of(z0 * (width // 2), LANES), width // 2)]

    mark_arrival = relocation(0, own_marks, marks.at[0])
    arrival = relocation(1, patches, start)
    other_arrival = relocation(2, cotangent, returned)
    out_return = relocation(3, start, output, True)
    grad_return = relocation(4, returned, grad_patches, True)
    mark_gather = Gather(place, marks, m_sends, m_receives)
    h_gathers = [Gather(place, normed.at[l], h_sends.at[l], h_receives.at[l]) for l in every]
    log_gathers = [Gather(place, logs_low.at[l], q_sends.at[l], q_receives.at[l]) for l in every]
    do_gathers = [Gather(place, douts.at[l], do_sends.at[l], do_receives.at[l]) for l in every]
    own_errors = [normed.at[0, 1 + 2 * l] for l in every]
    error_swaps = [swap(l, 0, X, own_errors[l], errors.at[l]) for l in every]
    hidden_swaps = [
        [
            swap(l, 1 + part, Z0, grad_hidden.at[l, away, :, :, columns], far_hidden.at[l, :, :, columns])
            for part, columns in enumerate((pl.ds(0, half), pl.ds(half, half)))
        ]
        for l in every
    ]
    middle_swaps = [swap(l, 3, Z0, grad_middle(away), far_middle.at[l]) for l in every]
    qkv_swaps = [[swap(l, 4 + part, Z0, half_qkv.at[part, away], far_qkv.at[l, part]) for part in range(3)] for l in every]
    mixed_swaps = [swap(l, 7, Z0, mixed.at[l, 0], mixed.at[l, 1]) for l in every]
    normed_swaps = [swap(l, 8, Z0, normed2.at[l, 0], normed2.at[l, 1]) for l in every]
    acts_swaps = [
        [
            swap(l, 9 + y, X, acts.at[l, 1 - place.x, pl.ds(2 * y, 2)], far_acts.at[l, pl.ds(2 * y, 2)])
            for y in range(2)
        ]
        for l in every
    ]
    doubling = Doubling(place, sums, sums_landing, sums_sems)
    reductions = {}
    for layer_no in every:
        for name in TENSORS:
            at = layer_no * len(TENSORS) + name
            reductions[layer_no, name] = Reduction(
                place,
                HALVING[name],
                plans[name][0],
                shares[at],
                first_landings[name],
                landings[at],
                sends.at[at],
                receives.at[at],
                credits.at[name],
                layer_no > 0,
                layer_no < top,
            )

    def spill(name):
        return pltpu.make_async_copy(held[name], saved[name], spill_sems.at[name])

    def loading(name):
        return pltpu.make_async_copy(saved[name], held[name], load_sems.at[name])

    def load(layer_no, *names):
        for name in names:
            loading(name).start()

    def ready(layer_no, *names):
        if layer_no < top:
            for name in names:
                loading(name).wait()


    def freq_tile(layer_no, which, index):
        return jnp.concatenate(
            [freqs[layer_no, 4 * index + member, which : which + 1] for member in range(4)], axis=1
        )

    def twice(tile):
        once, half_way, back = (pltpu.roll(tile, shift, 1) for shift in (32, 64, 96))
        quarter, last = lane < 32, lane >= 96
        return (
            jnp.where(quarter, tile, jnp.where(last, half_way, once)),
            jnp.where(quarter, half_way, jnp.where(last, tile, back)),
        )

    def angle_refs(slot):
        if slot == 0:
            return held[ANGLES].at[0], held[ANGLES].at[1]
        return grad_hidden.at[0, slot // 2, slot % 2], grad_hidden.at[1, slot // 2, slot % 2]

    def make_angles(layer_no, slot):
        rows_at = marks[slot][:, 1:2].astype(F32)
        columns_at = marks[slot][:, 2:3].astype(F32)
        cosine, sine = angle_refs(slot)
        sign = jnp.where(former, -1.0, 1.0)
        for index in range(pairs // 2):
            angle = rows_at * freq_tile(layer_no, 0, index) + columns_at * freq_tile(layer_no, 1, index)
            for member, (even, odd) in enumerate(zip(twice(jnp.cos(angle)), twice(jnp.sin(angle)))):
                cosine[:, tile_of(2 * index + member)] = even.astype(cosine.dtype)
                sine[:, tile_of(2 * index + member)] = (sign * odd).astype(sine.dtype)

    def project(layer_no, slot):
        cosine, sine = angle_refs(slot)
        block = normed[layer_no, slot]
        for name, part, scale in ((QUERIES, 0, 0.125), (KEYS, 1, 1.0)):
            products = rows_by_columns(block, qkv_w[:, part * width : part * width + width])
            for index in range(pairs):
                sl = tile_of(index)
                turned = rotate_tile(products[:, sl], cosine[:, sl].astype(F32), sine[:, sl].astype(F32), former)
                held[name][slot, :, sl] = (scale * turned).astype(BF16)
        held[VALUES][slot] = rows_by_columns(block, qkv_w[:, 2 * width :]).astype(BF16)

    def normalise_first(layer_no):
        hat, scale = normalise(carried[...])
        hat1[layer_no] = hat.astype(BF16)
        stats[layer_no] = jnp.where(lane == SCALE_LANE, scale, 0.0)
        normed[layer_no, 0] = (hat * gain1[layer_no : layer_no + 1] + bias1[layer_no : layer_no + 1]).astype(BF16)
        h_gathers[layer_no].start()

    def attend(layer_no):
        marks_of_keys = marks[...].reshape(4 * rows, LANES)
        sums_of_rows = jnp.zeros((rows, LANES), F32)
        for index in range(pairs):
            sl = tile_of(index)
            query_pair = held[QUERIES][0, :, sl]
            key_pair = held[KEYS][:, :, sl].reshape(4 * rows, LANES)
            value_pair = held[VALUES][:, :, sl].reshape(4 * rows, LANES)
            extended = jnp.concatenate([key_pair, marks_of_keys], axis=1)
            scores = rows_by_rows(jnp.concatenate([both(query_pair), one_lane], axis=1), extended)
            highest = jnp.max(scores, axis=1, keepdims=True)
            weight = jnp.exp(scores - highest)
            total = jnp.sum(weight, axis=1, keepdims=True)
            result = rows_by_columns(weight.astype(BF16), value_pair) / total
            mixed[layer_no, 0, :, sl] = beside(result).astype(BF16)
            log_sum = highest + jnp.log(total)
            for member in range(2):
                part = log_sum[member * rows : member * rows + rows]
                sums_of_rows = jnp.where(lane == 2 * index + member, part, sums_of_rows)
        stats[layer_no] = jnp.where(lane < 16, sums_of_rows, stats[layer_no])
        logs_low[layer_no, 0] = spread_lanes(-sums_of_rows, lane, 1.0).astype(BF16)

    def project_out(layer_no):
        weights.ready(layer_no, PROJ_W)
        middle = carried[...] + rows_by_columns(mixed[layer_no, 0], proj_w[...])
        carried[...] = middle
        if layer_no < top:
            weights.load(layer_no + 1, PROJ_W)
        hat, scale = normalise(middle)
        hat2[layer_no] = hat.astype(BF16)
        stats[layer_no] = jnp.where(lane == SCALE_LANE + 1, scale, stats[layer_no])
        normed2[layer_no, 0] = (hat * gain2[layer_no : layer_no + 1] + bias2[layer_no : layer_no + 1]).astype(BF16)

    def quarter_of(quarter):
        return slice(2 * half * quarter, 2 * half * quarter + 2 * half)

    def feed_forward(layer_no, quarter):
        if quarter == 0:
            weights.ready(layer_no, UP_W)
        columns = quarter_of(quarter)
        hidden_part = rows_by_columns(normed2[layer_no, 0], up_w[:, columns])
        share = 0.5 + 0.5 * lax.erf(hidden_part * 0.7071067811865476)
        active = (hidden_part * share).astype(BF16)
        slope = share + hidden_part * (0.3989422804014327 * jnp.exp(-0.5 * hidden_part * hidden_part))
        held[SLOPES][:, columns] = slope.astype(BF16)
        y, x = quarter // 2, quarter % 2
        acts[layer_no, x, 2 * y] = active[:, :half]
        acts[layer_no, x, 2 * y + 1] = active[:, half:]
        if quarter == 0:
            weights.ready(layer_no, DOWN_W)
        carried[...] += rows_by_columns(active, down_w[columns, :])


    def note(layer_no, row, values):
        sums[8 * layer_no + row : 8 * layer_no + row + 1] = jnp.sum(values, axis=0, keepdims=True)

    def norm_back(layer_no, number, grad, hat, scale):
        note(layer_no, 2 * number, grad * hat)
        note(layer_no, 2 * number + 1, grad)
        grad = grad * (gain1, gain2)[number][layer_no : layer_no + 1]
        mean = jnp.mean(grad, axis=-1, keepdims=True)
        slope = jnp.mean(grad * hat, axis=-1, keepdims=True)
        return scale * (grad - mean - hat * slope)

    def halves_of(values):
        return by_halves([values[:, tile_of(i)] for i in range(pairs)], first_head)

    def send_error(layer_no, values):
        for z0, tiles in enumerate(halves_of(values)):
            for i, tile in enumerate(tiles):
                own_errors[layer_no][:, tile_of(3 * z0 + i)] = tile.astype(BF16)
        error_swaps[layer_no].start()

    def hidden_back(layer_no):
        error = carried[...].astype(BF16)
        if layer_no < top:
            weights.ready(layer_no, DOWN_W)
        ready(layer_no, SLOPES)
        for quarter in range(4):
            grad = rows_by_rows(error, down_w[quarter_of(quarter), :])
            grad = grad * held[SLOPES][:, quarter_of(quarter)].astype(F32)
            grad_hidden[layer_no, quarter % 2, quarter // 2] = grad.astype(BF16)
        if layer_no > 0:
            weights.load(layer_no - 1, DOWN_W)
            load(layer_no - 1, SLOPES)

    def middle_back(layer_no):
        if layer_no < top:
            weights.ready(layer_no, UP_W)
        total = jnp.zeros((rows, width), F32)
        for quarter in range(4):
            total = total + rows_by_rows(grad_hidden[layer_no, quarter % 2, quarter // 2], up_w[:, quarter_of(quarter)])
        if layer_no > 0:
            weights.load(layer_no - 1, UP_W)
        carried[...] += norm_back(layer_no, 1, total, hat2[layer_no].astype(F32), stats[layer_no][:, SCALE_LANE + 1 : SCALE_LANE + 2])

    def project_back(layer_no):
        if layer_no < top:
            weights.ready(layer_no, PROJ_W)
        grad = rows_by_rows(carried[...].astype(BF16), proj_w[...])
        if layer_no > 0:
            weights.load(layer_no - 1, PROJ_W)
        deltas = jnp.zeros((rows, LANES), F32)
        for index in range(pairs):
            sl = tile_of(index)
            low_grad = grad[:, sl].astype(BF16)
            douts[layer_no, 0, :, sl] = low_grad
            product = low_grad.astype(F32) * mixed[layer_no, 0, :, sl].astype(F32)
            for member, mine in enumerate(heads_lanes):
                delta = jnp.sum(jnp.where(mine, product, 0.0), axis=1, keepdims=True)
                deltas = jnp.where(lane == 2 * index + member, delta, deltas)
        douts[layer_no, 0, :, width:] = spread_lanes(-deltas, lane, 0.0).astype(BF16)
        do_gathers[layer_no].start()
        kept_deltas.append(deltas)

    kept_deltas = []

    def middle_send(layer_no):
        for z0, tiles in enumerate(halves_of(carried[...])):
            for i, tile in enumerate(tiles):
                grad_middle(z0)[:, tile_of(i)] = tile.astype(BF16)
        middle_swaps[layer_no].start()

    def turned_back(layer_no, part, index, grad, forward):
        sl = tile_of(index)
        back = grad * held[ANGLES][0, :, sl] - partner_tile(grad, former) * held[ANGLES][1, :, sl]
        grad_qkv[:, part * width + LANES * index : part * width + LANES * index + LANES] = back.astype(BF16)
        return back, grad * partner_tile(forward.astype(F32), former)

    def note_turn(layer_no, index, turn, first):
        for row in range(2):
            at = 8 * layer_no + 4 + row
            total = jnp.sum(turn * marks[0][:, 1 + row : 2 + row].astype(F32), axis=0, keepdims=True)
            if not first:
                total = total + sums[at : at + 1, tile_of(index)]
            sums[at : at + 1, tile_of(index)] = total

    def split_half(part, tiles):
        for z0, group in enumerate(by_halves(tiles, first_head)):
            for i, tile in enumerate(group):
                half_qkv[part, z0, :, tile_of(i)] = tile.astype(BF16)

    def own_queries(layer_no):
        ready(layer_no, KEYS, VALUES, ANGLES, QUERIES)
        deltas = kept_deltas[-1]
        key_marks = marks[...].reshape(4 * rows, LANES)
        backs = []
        for index in range(pairs):
            sl = tile_of(index)
            query_pair = held[QUERIES][0, :, sl]
            key_pair = held[KEYS][:, :, sl].reshape(4 * rows, LANES)
            value_pair = held[VALUES][:, :, sl].reshape(4 * rows, LANES)
            grad_pair = douts[layer_no, 0, :, sl]
            extended = jnp.concatenate([key_pair, key_marks], axis=1)
            scores = rows_by_rows(jnp.concatenate([both(query_pair), one_lane], axis=1), extended)
            weight = jnp.exp(scores - columns_of(stats[layer_no], index))
            grad = rows_by_rows(both(grad_pair), value_pair)
            grad = (weight * (grad - columns_of(deltas, index))).astype(BF16)
            grad = 0.125 * beside(rows_by_columns(grad, key_pair))
            back, turn = turned_back(layer_no, 0, index, grad, 8.0 * query_pair.astype(F32))
            note_turn(layer_no, index, turn, True)
            backs.append(back)
        split_half(0, backs)

    def own_keys(layer_no):
        do_gathers[layer_no].near()
        do_gathers[layer_no].last()
        if layer_no == top:
            log_gathers[layer_no].near()
            log_gathers[layer_no].last()
        own_marks = jnp.broadcast_to(jnp.concatenate([marks[0][:, 0:1]] * 2, axis=0), (2 * rows, LANES))
        key_backs, value_backs = [], []
        for index in range(pairs):
            sl = tile_of(index)
            key_pair, value_pair = held[KEYS][0, :, sl], held[VALUES][0, :, sl]
            query_pair = held[QUERIES][:, :, sl].reshape(4 * rows, LANES)
            grad_pair = douts[layer_no, :, :, sl].reshape(4 * rows, LANES)
            queries = jnp.concatenate([query_pair, logs_low[layer_no].reshape(4 * rows, LANES)], axis=1)
            grads = jnp.concatenate([grad_pair, douts[layer_no, :, :, width:].reshape(4 * rows, LANES)], axis=1)
            head = jnp.where(upper, 2 * index, 2 * index + 1)
            chosen = jnp.where((two_lane < 48) & (lax.rem(two_lane, 16) == head), 1.0, 0.0).astype(BF16)
            marked = jnp.where(two_lane == 127, own_marks, chosen)
            weight = jnp.exp(rows_by_rows(jnp.concatenate([both(key_pair), marked], axis=1), queries))
            grad = rows_by_rows(jnp.concatenate([both(value_pair), chosen], axis=1), grads)
            value_grad = beside(rows_by_columns(weight.astype(BF16), grad_pair))
            grad = beside(rows_by_columns((weight * grad).astype(BF16), query_pair))
            back, turn = turned_back(layer_no, 1, index, grad, key_pair)
            note_turn(layer_no, index, turn, False)
            key_backs.append(back)
            grad = value_grad
            grad_qkv[:, 2 * width + LANES * index : 2 * width + LANES * index + LANES] = grad.astype(BF16)
            value_backs.append(grad)
        split_half(1, key_backs)
        split_half(2, value_backs)
        if layer_no > 0:
            load(layer_no - 1, KEYS, VALUES, ANGLES, QUERIES)

    def input_back(layer_no):
        if layer_no < top:
            weights.ready(layer_no, QUERY_W, KEY_W, VALUE_W)
        total = rows_by_rows(grad_qkv[...], qkv_w[...])
        if layer_no > 0:
            weights.load(layer_no - 1, QUERY_W, KEY_W, VALUE_W)
        carried[...] += norm_back(layer_no, 0, total, hat1[layer_no].astype(F32), stats[layer_no][:, SCALE_LANE : SCALE_LANE + 1])
        if layer_no > 0:
            send_error(layer_no - 1, carried[...])

    def put(layer_no, name, values, column, blocks, skipped=0):
        share = reductions[layer_no, name].share
        for first_row, count, tile in blocks:
            for i in range(values.shape[1] // LANES):
                piece = values[first_row - skipped : first_row - skipped + count, tile_of(i)].astype(BF16)
                at_tile, at_row = column(tile, i)
                share[at_tile, at_row : at_row + count] = piece

    def blocks_of(name):
        n, axes = plans[name][0], HALVING[name]
        blocks = []
        for number in range(8):
            bits = (number % 2, (number // 2) % 2, number // 4)
            tile = ((bits[axes[0]] * 2 + bits[axes[1]]) * 2 + bits[axes[2]]) * n
            blocks.append((number * size, size, tile))
        return blocks

    def down_product(layer_no):
        error_swaps[layer_no].arrive()
        if layer_no == top:
            for part in acts_swaps[layer_no]:
                part.arrive()
        for y in range(2):
            for c in range(2):
                for z0 in range(2):
                    columns = slice(z0 * width // 2, (z0 + 1) * width // 2)
                    product = columns_by_columns(
                        acts[layer_no, place.x, 2 * y + c], own_errors[layer_no][:, columns]
                    ) + columns_by_columns(far_acts[layer_no, 2 * y + c], errors[layer_no, :, columns])
                    tile = ((2 * c + y) * 2 + z0) * 3
                    for part in range(2):
                        block = (half // 2 * part, half // 2, tile)
                        put(layer_no, DOWN_A + part, product, lambda tile, i: (tile + i, 0), [block])
        reductions[layer_no, DOWN_A].start()
        reductions[layer_no, DOWN_B].start()

    def up_product(layer_no, part):
        hidden_swaps[layer_no][part].arrive()
        if layer_no == top and part == 0:
            normed_swaps[layer_no].arrive()
        columns = pl.ds(half * part, half)
        for z1 in range(2):
            for side in range(2):
                inputs = slice(side * 4 * size, side * 4 * size + 4 * size)
                product = columns_by_columns(
                    normed2[layer_no, 0, :, inputs], grad_hidden[layer_no, place.z0, z1, :, columns]
                ) + columns_by_columns(normed2[layer_no, 1, :, inputs], far_hidden[layer_no, z1, :, columns])
                put(
                    layer_no,
                    UP_A + part,
                    product,
                    lambda tile, i: (tile + z1, size * i),
                    blocks_of(UP_A + part)[4 * side : 4 * side + 4],
                    4 * size * side,
                )
        reductions[layer_no, UP_A + part].start()
        hidden_swaps[layer_no][part].drain()

    def narrow_product(layer_no, name, left, right, far):
        blocks = blocks_of(name)
        for side in range(2):
            columns = slice(side * 4 * size, side * 4 * size + 4 * size)
            product = columns_by_columns(left[0][:, columns], right) + columns_by_columns(left[1][:, columns], far)
            put(layer_no, name, product, lambda tile, i: (tile + i, 0), blocks[4 * side : 4 * side + 4], 4 * size * side)
        reductions[layer_no, name].start()

    def proj_product(layer_no):
        middle_swaps[layer_no].arrive()
        if layer_no == top:
            mixed_swaps[layer_no].arrive()
        left = (mixed.at[layer_no, 0], mixed.at[layer_no, 1])
        narrow_product(layer_no, PROJ, left, grad_middle(place.z0)[...], far_middle[layer_no])
        middle_swaps[layer_no].drain()

    def part_product(layer_no, part):
        qkv_swaps[layer_no][part].arrive()
        left = (normed.at[layer_no, 0], normed.at[layer_no, 2])
        narrow_product(layer_no, QUERY + part, left, half_qkv[part, place.z0], far_qkv[layer_no, part])
        qkv_swaps[layer_no][part].drain()

    def hand_out(layer_no, name):
        if name < UP_A:
            target = results[0].at[layer_no, pl.ds(half // 2 * (name - DOWN_A), half // 2)]
        elif name < PROJ:
            target = results[1].at[layer_no, :, pl.ds(half * (name - UP_A), half)]
        else:
            target = results[name - 2].at[layer_no]
        return pltpu.make_async_copy(stagings[name], target, stage_sems.at[name])

    def finish(layer_no, name):
        target = stagings[name]
        if layer_no < top:
            hand_out(layer_no + 1, name).wait()

        def write(own, rest=None):
            if rest is None:
                for part in range(own.shape[0] // size):
                    target[:, tile_of(part)] = own[size * part : size * part + size]
            else:
                target[:, :LANES] = own
                target[:, LANES : LANES + 64] = rest

        reductions[layer_no, name].finish(write)
        hand_out(layer_no, name).start()

    def step(layer_no, name, stage):
        reductions[layer_no, name].step(stage)

    def return_grad():
        out_return.wait()
        returned[...] = carried[...].astype(BF16)
        grad_return.start()

    def low_arrivals():
        log_gathers[low].last()
        for one in [mixed_swaps[low], normed_swaps[low]] + acts_swaps[low]:
            one.arrive()

    mark_arrival.start()
    arrival.start()
    sums[...] = jnp.zeros(sums.shape, F32)
    mark_arrival.wait()
    mark_gather.start()
    make_angles(0, 0)
    arrival.wait()
    carried[...] = start[...].astype(F32)
    normalise_first(0)
    weights.ready(0, KEY_W, VALUE_W, QUERY_W)
    project(0, 0)
    mark_gather.near()
    mark_gather.far()
    make_angles(0, 1)
    h_gathers[0].near()
    project(0, 1)
    make_angles(0, 2)
    mark_gather.last()
    make_angles(0, 3)
    h_gathers[0].far()
    other_arrival.start()
    project(0, 2)
    h_gathers[0].last()
    project(0, 3)
    weights.load(1, KEY_W, VALUE_W, QUERY_W)
    for name in (KEYS, VALUES, QUERIES, ANGLES):
        spill(name).start()
    attend(0)
    mixed_swaps[0].start()
    project_out(0)
    for quarter in range(4):
        feed_forward(0, quarter)
    weights.load(1, UP_W, DOWN_W)
    spill(SLOPES).start()
    for part in acts_swaps[0]:
        part.start()
    normalise_first(1)
    normed_swaps[0].start()
    log_gathers[0].start()
    for name in (KEYS, VALUES, QUERIES, ANGLES):
        spill(name).wait()
    make_angles(1, 0)
    weights.ready(1, KEY_W, VALUE_W, QUERY_W)
    project(1, 0)
    make_angles(1, 1)
    h_gathers[1].near()
    project(1, 1)
    make_angles(1, 2)
    make_angles(1, 3)
    other_arrival.wait()
    send_error(1, returned[...].astype(F32))
    h_gathers[1].far()
    project(1, 2)
    h_gathers[1].last()
    project(1, 3)
    attend(1)
    log_gathers[1].start()
    mixed_swaps[1].start()
    project_out(1)
    normed_swaps[1].start()
    spill(SLOPES).wait()
    feed_forward(1, 0)
    feed_forward(1, 1)
    acts_swaps[1][0].start()
    log_gathers[0].near()
    log_gathers[0].far()
    feed_forward(1, 2)
    feed_forward(1, 3)
    acts_swaps[1][1].start()
    start[...] = carried[...].astype(BF16)
    carried[...] = returned[...].astype(F32)
    hidden_back(top)
    middle_back(top)
    project_back(top)
    own_queries(top)
    hidden_swaps[top][0].start()
    middle_send(top)
    log_gathers[top].far()
    qkv_swaps[top][0].start()
    out_return.start()
    hidden_swaps[top][1].start()
    down_product(top)
    do_gathers[top].far()
    step(top, DOWN_A, 0)
    step(top, DOWN_B, 0)
    own_keys(top)
    up_product(top, 0)
    qkv_swaps[top][1].start()
    qkv_swaps[top][2].start()
    input_back(top)
    low_arrivals()
    hidden_back(low)
    middle_back(low)
    project_back(low)
    step(top, DOWN_A, 1)
    hidden_swaps[low][1].start()
    part_product(top, 0)
    step(top, UP_A, 0)
    hidden_swaps[low][0].start()
    own_queries(low)
    step(top, DOWN_B, 1)
    qkv_swaps[low][0].start()
    step(top, QUERY, 0)
    down_product(low)
    up_product(top, 1)
    proj_product(top)
    part_product(top, 1)
    middle_send(low)
    step(low, DOWN_A, 0)
    step(low, DOWN_B, 0)
    part_product(top, 2)
    step(top, QUERY, 1)
    step(top, UP_A, 1)
    step(top, UP_B, 0)
    step(top, PROJ, 0)
    step(top, KEY, 0)
    step(top, VALUE, 0)
    do_gathers[low].far()
    step(top, QUERY, 2)
    own_keys(low)
    finish(top, QUERY)
    step(low, DOWN_A, 1)
    qkv_swaps[low][1].start()
    qkv_swaps[low][2].start()
    step(top, DOWN_A, 2)
    step(top, UP_B, 1)
    input_back(low)
    doubling.start()
    up_product(low, 1)
    return_grad()
    doubling.step(0)
    step(top, PROJ, 1)
    step(low, DOWN_B, 1)
    step(low, UP_B, 0)
    step(top, UP_A, 2)
    step(top, KEY, 1)
    up_product(low, 0)
    finish(top, DOWN_A)
    doubling.step(1)
    step(low, UP_A, 0)
    step(top, VALUE, 1)
    step(top, DOWN_B, 2)
    part_product(low, 0)
    step(top, UP_B, 2)
    finish(top, UP_A)
    step(low, UP_B, 1)
    proj_product(low)
    step(low, QUERY, 0)
    step(top, PROJ, 2)
    step(top, KEY, 2)
    step(low, PROJ, 0)
    doubling.step(2)
    finish(top, DOWN_B)
    step(low, DOWN_A, 2)
    finish(top, UP_B)
    step(low, UP_B, 2)
    part_product(low, 1)
    step(low, UP_A, 1)
    finish(top, PROJ)
    step(top, VALUE, 2)
    step(low, KEY, 0)
    step(low, QUERY, 1)
    finish(top, KEY)
    part_product(low, 2)
    step(low, PROJ, 1)
    step(low, VALUE, 0)
    finish(low, DOWN_A)
    step(low, UP_A, 2)
    step(low, KEY, 1)
    finish(low, UP_B)
    step(low, PROJ, 2)
    step(low, QUERY, 2)
    finish(top, VALUE)
    step(low, VALUE, 1)
    step(low, DOWN_B, 2)
    step(low, KEY, 2)
    finish(low, UP_A)
    finish(low, PROJ)
    step(low, VALUE, 2)
    finish(low, QUERY)
    doubling.step(3)
    finish(low, DOWN_B)
    finish(low, KEY)
    finish(low, VALUE)
    doubling.step(4)
    grad_small[...] = sums[...]
    grad_return.wait()
    for name in TENSORS:
        hand_out(low, name).wait()
    for red in reductions.values():
        red.drain()
    for gather in [mark_gather] + h_gathers + log_gathers + do_gathers:
        gather.drain()
    for one in error_swaps + mixed_swaps + normed_swaps + acts_swaps[low] + acts_swaps[top]:
        one.drain()


def encoder_call(patches, cotangent, keep, coords, norms, freqs, whole):
    layers = freqs.shape[0]
    rows, width = patches.shape
    hidden = whole[4].shape[2]
    size, quarter = width // 8, width // 4
    plans = tile_plan(width, hidden)
    tensors = plans * layers
    sem = pltpu.SemaphoreType.DMA
    any_spec, vmem_spec = pl.BlockSpec(memory_space=pl.ANY), pl.BlockSpec(memory_space=pltpu.VMEM)
    finals = [(hidden // 8, quarter), (size, hidden // 4)] + [(size, quarter)] * 4
    parts = [(hidden // 16, quarter)] * 2 + [(size, hidden // 8)] * 2 + [(size, quarter)] * 4
    outs = (
        [jax.ShapeDtypeStruct((rows, width), BF16)] * 2
        + [jax.ShapeDtypeStruct((layers,) + shape, F32) for shape in finals]
        + [jax.ShapeDtypeStruct((8 * layers, width), F32)]
        + [jax.ShapeDtypeStruct(*shape) for shape in spilled_shapes(rows, width, hidden)]
    )

    def low(*shape):
        return pltpu.VMEM(shape, BF16)

    def full(*shape):
        return pltpu.VMEM(shape, F32)

    return pl.pallas_call(
        lambda *refs: encoder_kernel(layers, *refs),
        out_shape=outs,
        in_specs=[any_spec, any_spec] + [vmem_spec] * 7 + [any_spec] * 6,
        out_specs=[any_spec] * 8 + [vmem_spec] + [any_spec] * 5,
        scratch_shapes=[pltpu.VMEM(*shape) for shape in spilled_shapes(rows, width, hidden)]
        + [low(8 * n, count, LANES) for n, count in tensors]
        + [low(landing_count(n), count, LANES) for n, count in tensors]
        + [low(4 * n, count, LANES) for n, count in plans]
        + [full(*shape) for shape in parts]
        + [low(width, 3 * width), low(width, width), low(width, hidden), low(hidden, width)]
        + [sem((6,)), sem((5,)), sem((5,)), sem((len(plans),))]
        + [
            low(layers, 4, rows, width),
            low(layers, 4, rows, LANES),
            low(layers, 2, rows, width),
            low(layers, 2, rows, width),
            low(layers, 2, 4, rows, hidden // 8),
            low(layers, 4, rows, hidden // 8),
            low(layers, rows, width),
            low(layers, rows, width),
            full(layers, rows, LANES),
        ]
        + [low(rows, width), low(rows, LANES), low(4, rows, LANES), low(rows, width), sem((5, 3))]
        + [sem((layers, 4))] * 6
        + [sem((4,))] * 2
        + [
            low(layers, 4, rows, width + LANES),
            low(layers, rows, width),
            low(layers, 2, 2, rows, width),
            low(layers, 2, rows, width),
            low(layers, rows, width // 2),
            low(rows, 3 * width),
            low(3, 2, rows, width // 2),
            low(layers, 3, rows, width // 2),
        ]
        + [sem((layers, 11, 2)), sem((len(tensors), 5)), sem((len(tensors), 5))]
        + [pltpu.SemaphoreType.REGULAR((len(plans),))]
        + [full(rows, width), full(8 * layers, width), full(5, 8 * layers, width), sem((5, 2))],
        compiler_params=pltpu.CompilerParams(
            collective_id=0, has_side_effects=True, vmem_limit_bytes=VMEM_BYTES
        ),
    )(patches, cotangent, keep, coords, *norms, freqs, *whole)


def beyond_eight(result):
    dp_size = lax.axis_size(DP)
    groups = dp_size // 8
    if groups == 1:
        return result
    result = lax.psum(result, DP, axis_index_groups=[[g * 8 + i for g in range(groups)] for i in range(8)])
    whole = lax.all_gather(
        result, DP, axis=1, tiled=True, axis_index_groups=[[g * 8 + i for i in range(8)] for g in range(groups)]
    )
    rows = whole.shape[1] // dp_size
    return lax.dynamic_slice_in_dim(whole, lax.axis_index(DP) * rows, rows, axis=1)


def final_kernel(count, *refs):
    output, grad_patches, small = refs[:3]
    large = refs[3 : 3 + count]
    refs = refs[3 + count :]
    out_copy, grad_copy = refs[:2]
    large_copies = refs[2 : 2 + count]
    norms, turns = refs[2 + count : 6 + count], refs[6 + count]
    out_copy[...] = output[...]
    grad_copy[...] = grad_patches[...].astype(F32)
    for source, target in zip(large[:-1], large_copies[:-1]):
        target[...] = source[...]
    layers, columns = norms[0].shape
    for layer_no in range(layers):
        large_copies[-1][layer_no] = large[-1][layer_no].T
    at = lax.axis_index(BLK)
    half = turns.shape[3]
    for blk in range(small.shape[1] // columns):

        @pl.when(at == blk)
        def _(blk=blk):
            for layer_no in range(layers):
                mine = small[8 * layer_no : 8 * layer_no + 8, blk * columns : blk * columns + columns]
                for row, norm in enumerate(norms):
                    norm[layer_no : layer_no + 1] = mine[row : row + 1]
                for row in range(2):
                    for head in range(turns.shape[1]):
                        pair = mine[4 + row : 5 + row, 2 * half * head : 2 * half * head + 2 * half]
                        turns[layer_no, head, row : row + 1] = pair[:, half:] - pair[:, :half]


def final_call(output, grad_patches, small, large, half):
    vmem_spec = pl.BlockSpec(memory_space=pltpu.VMEM)
    layers = small.shape[0] // 8
    columns = small.shape[1] // lax.axis_size(BLK)
    return pl.pallas_call(
        lambda *refs: final_kernel(len(large), *refs),
        out_shape=[
            jax.ShapeDtypeStruct(output.shape, output.dtype),
            jax.ShapeDtypeStruct(grad_patches.shape, F32),
        ]
        + [jax.ShapeDtypeStruct(a.shape, F32) for a in large[:-1]]
        + [jax.ShapeDtypeStruct((layers,) + large[-1].shape[:0:-1], F32)]
        + [jax.ShapeDtypeStruct((layers, columns), F32)] * 4
        + [jax.ShapeDtypeStruct((layers, columns // (2 * half), 2, half), F32)],
        in_specs=[vmem_spec] * (3 + len(large)),
        out_specs=[vmem_spec] * (7 + len(large)),
    )(output, grad_patches, small, *large)


def shards(
    patches,
    keep,
    coords,
    query_w,
    key_w,
    value_w,
    proj_w,
    up_w,
    down_w,
    norm1_gain,
    norm1_bias,
    norm2_gain,
    norm2_bias,
    freqs,
    cotangent,
):
    whole = (query_w, key_w, value_w, proj_w, up_w, down_w)
    norms = (norm1_gain, norm1_bias, norm2_gain, norm2_bias)
    results = encoder_call(patches[0], cotangent[0], keep, coords, norms, jnp.swapaxes(freqs, 1, 2), whole)
    output, grad_patches, grad_down, grad_up, *others, small = results[:9]
    large = [beyond_eight(grad) for grad in (*others[1:], others[0], grad_up, grad_down)]
    groups = lax.axis_size(DP) // 8
    if groups > 1:
        small = lax.psum(small, DP, axis_index_groups=[[g * 8 + i for g in range(groups)] for i in range(8)])
    output, grad_patches, *rest = final_call(output, grad_patches, small, large, freqs.shape[3])
    rest[5], rest[-1] = jnp.swapaxes(rest[5], 1, 2), jnp.swapaxes(rest[-1], 1, 2)
    return (output[None], grad_patches[None], *rest)


def solution(mesh):
    block = P(DP, BLK, None)
    placed = (block, P(DP, BLK), P(None, DP, BLK)) + (P(),) * 11 + (block,)
    results = (block, block) + (P(None, DP, BLK),) * 6 + (P(None, BLK),) * 4 + (P(None, None, BLK, None),)
    return jax.shard_map(shards, mesh=mesh, in_specs=placed, out_specs=results, check_vma=False)
```
